128 devices in a mesh: view: 4 (over z), tile: 32 (over x, y, core).
Axes of the slice: x: 4, y: 4, z: 4, core: 2. Of those that a mesh axis runs over, the one named last changes fastest.
Arguments:
- centres: float32 [3, 131072], P(None, ('view', 'tile')), may hold values from -6 to 6
- shape_raw: float32 [6, 131072], P(None, ('view', 'tile')), may hold values from -1 to 0.2
- opacity_logit: float32 [131072], P(('view', 'tile')), may hold values from -6 to -1
- colours: float32 [3, 131072], P(None, ('view', 'tile')), may hold values from -6 to 6
- camera: float32 [8, 2, 4], replicated, may hold values from -15 to 15
- target: float32 [8, 512, 3, 256], P('view', 'tile'), may hold values from -3 to 3
- intersection_ids: int32 [8, 512, 256], P('view', 'tile'), may hold values from 0 to 131071, as said below
- depth_order: int32 [8, 512, 256], P('view', 'tile'), may hold values from 0 to 255, each once within a row
- live_count: int32 [8, 512], P('view', 'tile'), may hold values from 1 to 256, as said below
Outputs:
- rendered: float32 [8, 512, 3, 256], P('view', 'tile')
- grad_centres: float32 [3, 131072], P(None, ('view', 'tile'))
- grad_shape: float32 [6, 131072], P(None, ('view', 'tile'))
- grad_opacity: float32 [131072], P(('view', 'tile'))
- grad_colours: float32 [3, 131072], P(None, ('view', 'tile'))
- next_owner: int32 [8, 512], P('view', 'tile')
The draws below stay inside these ranges and needn't reach their ends.
Inputs may be any that keep to these rules, and one draw needn't show every extreme that they name: `intersection_ids`: gaussian g is held by device g div 1024, devices counted along view+tile. Among the 2 x 16 x 256 slots held by one device at most 128 name Gaussians of any one device, and in every draw some device is named exactly 128 times by the slots of every device. `depth_order`: each tile's entries are a permutation of the slot numbers. Slot s of tile (v, t) is live when s < live_count[v, t]; every view has a tile with all 256 slots live.
All inputs are finite; a program needn't handle non-finite values.
Results may differ from the reference program's by a relative error of at most 0.0003.
Values sent between devices are 32-bit elements; how exact they have to be, the bound alone decides.
A program may use at most 128 MiB of HBM per device.

```python
import math
import jax
import jax.numpy as jnp
from jax import lax

SIDE = 16
PIX = 256
K = 256
VG = 2
TILE_DEV = 16
G_DEV = 1024
VIEWS = 8
TILES = 512
G = 131072
CAP = 128
N_VIEW = 4
N_TILE = 32


def draw_intersection_ids(key, part):
    devices = N_VIEW * N_TILE
    slots_here = VG * TILE_DEV * K
    tiles_local = VG * TILE_DEV
    front_count = devices // 4
    front_slots = front_count * CAP
    back_slots = slots_here - front_slots
    key_hot, key_pool, key_local = jax.random.split(jax.random.fold_in(key, 17), 3)
    hottest = jax.random.randint(key_hot, (), 0, devices).astype(jnp.int32)

    def requester_owners(pair_key):
        first_key, second_key, third_key = jax.random.split(pair_key, 3)
        shuffled = jax.random.permutation(first_key, devices - 1).astype(jnp.int32)
        others = ((hottest + 1 + shuffled) % devices).astype(jnp.int32)
        front_owners = jnp.concatenate([hottest[None], others[:front_count - 1]])
        front_owners = jax.random.permutation(second_key, front_owners)
        front_run = front_owners[jnp.arange(front_slots, dtype=jnp.int32) // CAP]
        rest = others[front_count - 1:]
        pool_length = rest.shape[0] * CAP
        pool = rest[jnp.arange(pool_length, dtype=jnp.int32) // CAP]
        back_run = jax.random.permutation(third_key, pool)[:back_slots]
        ordered_run = jnp.concatenate([front_run, back_run])
        return jnp.transpose(ordered_run.reshape(K, tiles_local)).reshape(slots_here)
    owners = jax.vmap(requester_owners)(jax.random.split(key_pool, devices))
    local = jax.random.randint(key_local, (devices, slots_here), 0, G_DEV).astype(jnp.int32)
    named = (owners * G_DEV + local).astype(jnp.int32)
    named = named.reshape(N_VIEW, N_TILE, VG, TILE_DEV, K).transpose(0, 2, 1, 3, 4)
    return named.reshape(VG * N_VIEW, TILE_DEV * N_TILE, K)


def draw_live_count(key, part):
    key_base, key_hot = jax.random.split(jax.random.fold_in(key, 29))
    base = jax.random.randint(key_base, (VIEWS, TILES), 0, K).astype(jnp.int32)
    place = jnp.arange(TILES, dtype=jnp.int32)[None, :]
    grown = 1 + base * (TILES + 2 * place) // (3 * TILES)
    hottest = jax.random.randint(key_hot, (VIEWS, 1), 0, TILES).astype(jnp.int32)
    return jnp.where(place == hottest, K, grown).astype(jnp.int32)


def steps_of(rng, shape, pieces, low, high):
    def one(dim, blocks):
        draws = jax.random.uniform(jax.random.fold_in(jax.random.fold_in(rng, 6), dim), (blocks,), jnp.float32, low / len(pieces), high / len(pieces))
        return jnp.repeat(jnp.exp(draws), shape[dim] // blocks).reshape((-1,) + (1,) * (len(shape) - dim - 1))

    level = one(*pieces[0])
    for cut in pieces[1:]:
        level = level * one(*cut)
    return level


def centred(rng, dims, spread, bound, cuts=(), kind=jnp.bfloat16):
    array = spread * jax.random.normal(rng, dims, jnp.float32)
    if cuts:
        array = array * steps_of(rng, dims, cuts, -0.22, 0.18)
    return jnp.clip(array, -bound, bound).astype(kind)


def setup_inputs(seed: int = 0) -> dict:
    streams_of = jax.random.split(jax.random.key(seed), 10)
    return {
        "centres": centred(streams_of[0], (3, G), 1.0, 6.0, ((1, 128),), jnp.float32),
        "shape_raw": jnp.clip(-1.0 + 1.2 * jax.random.uniform(streams_of[1], (6, G), jnp.float32) ** steps_of(streams_of[1], (6, G), ((1, 128),), -0.2, 0.2), -1.0, 0.2),
        "opacity_logit": jnp.clip(-6.0 + 5.0 * jax.random.uniform(streams_of[2], (G,), jnp.float32) ** steps_of(streams_of[2], (G,), ((0, 128),), -0.2, 0.2), -6.0, -1.0),
        "colours": centred(streams_of[3], (3, G), 1.0, 6.0, ((1, 128),), jnp.float32),
        "camera": centred(streams_of[4], (VIEWS, 2, 4), 3.0, 15.0, (), jnp.float32),
        "target": centred(streams_of[5], (VIEWS, TILES, 3, PIX), 0.5, 3.0, ((0, 4), (1, 32)), jnp.float32),
        "intersection_ids": draw_intersection_ids(jax.random.fold_in(streams_of[9], 71), 0),
        "depth_order": jax.vmap(lambda own: jax.random.permutation(own, K))(jax.random.split(streams_of[7], VIEWS * TILES)).reshape((VIEWS, TILES, K)).astype(jnp.int32),
        "live_count": draw_live_count(jax.random.fold_in(streams_of[9], 71), 0),
    }


exact_mode = lax.Precision.HIGHEST

def lower_factor(shape_raw):
    empty_cells = jnp.zeros_like(shape_raw[0])
    first_row = jnp.stack([jnp.exp(shape_raw[0]), empty_cells, empty_cells])
    second_row = jnp.stack([shape_raw[1], jnp.exp(shape_raw[2]), empty_cells])
    third_row = jnp.stack([shape_raw[3], shape_raw[4], jnp.exp(shape_raw[5])])
    return jnp.stack([first_row, second_row, third_row])

def project(centres, shape_raw, opacity_logit, colours, camera):
    view_count = camera.shape[0]
    gaussians = centres.shape[1]
    linear = camera[:, :, 0:3]
    screen = jnp.einsum('vij,jg->vig', linear, centres, precision=exact_mode) + camera[:, :, 3][:, :, None]
    factor = jnp.einsum('vik,kjg->vijg', linear, lower_factor(shape_raw), precision=exact_mode)
    var_x = lax.optimization_barrier(jnp.sum(factor[:, 0] * factor[:, 0], axis=1)) + 0.3
    cov_xy = lax.optimization_barrier(jnp.sum(factor[:, 0] * factor[:, 1], axis=1))
    var_y = lax.optimization_barrier(jnp.sum(factor[:, 1] * factor[:, 1], axis=1)) + 0.3
    determinant = var_x * var_y - cov_xy * cov_xy
    opacity = 0.95 / (1.0 + jnp.exp(-opacity_logit))
    fields = [screen[:, 0], screen[:, 1], var_y / determinant, -cov_xy / determinant, var_x / determinant, jnp.broadcast_to(opacity, (view_count, gaussians))]
    for channel in range(3):
        fields.append(jnp.broadcast_to(colours[channel], (view_count, gaussians)))
    return jnp.stack(fields)

def pixel_offsets():
    pixel_index = jnp.arange(SIDE * SIDE, dtype=jnp.int32)
    across = (pixel_index % SIDE).astype(jnp.float32) - (SIDE - 1) / 2.0
    downward = (pixel_index // SIDE).astype(jnp.float32) - (SIDE - 1) / 2.0
    return (across, downward)

def render_tile(slot_rec, order, live_count):
    ordered = jnp.take(slot_rec, order, axis=1)
    active_slots = (order < live_count).astype(jnp.float32)
    across, downward = pixel_offsets()
    delta_x = across[:, None] - ordered[0][None, :]
    delta_y = downward[:, None] - ordered[1][None, :]
    radius = ordered[2] * delta_x * delta_x + 2.0 * ordered[3] * delta_x * delta_y + ordered[4] * delta_y * delta_y
    coverage = active_slots * ordered[5] * jnp.exp(-0.5 * radius)
    keep_log = jnp.log1p(-coverage)
    slot_count = order.shape[0]
    earlier = (lax.broadcasted_iota(jnp.int32, (slot_count, slot_count), 0) < lax.broadcasted_iota(jnp.int32, (slot_count, slot_count), 1)).astype(jnp.float32)
    through = jnp.exp(jnp.dot(keep_log, earlier, precision=exact_mode))
    weights = through * coverage
    return jnp.einsum('ck,pk->cp', ordered[6:9], weights, precision=exact_mode)

def render_block(slot_rec, order, live_count):
    return jax.vmap(render_tile)(slot_rec, order, live_count)

def render_all(slot_rec, order, live_count):
    lead_count, tile_count, slot_count = order.shape
    total_tiles = lead_count * tile_count
    block_size = math.gcd(total_tiles, 8)
    records = jnp.moveaxis(slot_rec, 0, 2).reshape(total_tiles // block_size, block_size, 9, slot_count)
    orders = order.reshape(total_tiles // block_size, block_size, slot_count)
    counts = live_count.reshape(total_tiles // block_size, block_size)
    blocked = jax.checkpoint(render_block)

    def one_block(packed):
        return blocked(packed[0], packed[1], packed[2])
    images = lax.map(one_block, (records, orders, counts))
    return images.reshape(lead_count, tile_count, 3, SIDE * SIDE)

def reference(centres, shape_raw, opacity_logit, colours, camera, target, intersection_ids, depth_order, live_count):

    def forward(centres, shape_raw, opacity_logit, colours):
        records = project(centres, shape_raw, opacity_logit, colours, camera)
        view_index = lax.broadcasted_iota(jnp.int32, intersection_ids.shape, 0)
        slot_rec = records[:, view_index, intersection_ids]
        return render_all(slot_rec, depth_order, live_count)
    rendered, pullback = jax.vjp(forward, centres, shape_raw, opacity_logit, colours)
    gradients = pullback(rendered - target)
    starts = (jnp.cumsum(live_count, axis=1) - live_count).astype(jnp.int32)
    totals = lax.optimization_barrier(jnp.sum(live_count, axis=1, keepdims=True)).astype(jnp.int32)
    next_owner = (starts * N_TILE // totals).astype(jnp.int32)
    return (rendered, gradients[0], gradients[1], gradients[2], gradients[3], next_owner)
```

```python
from functools import partial

import jax
import jax.numpy as jnp
from jax import lax
from jax.experimental import pallas as pl
from jax.experimental.pallas import tpu as pltpu
from jax.sharding import PartitionSpec as P

SIDE = 16
PIX = SIDE * SIDE
LANES = 128
LANE_BITS = 7
ROWS = 8
FIELDS = 9
MOVING = 5
F32 = jnp.float32
BF16 = jnp.bfloat16
I32 = jnp.int32


def lanes(table, index):
    return jnp.take_along_axis(table, index, axis=1, mode="promise_in_bounds")


def iota(shape, axis):
    return lax.broadcasted_iota(I32, shape, axis)


def spread(row, count):
    return jnp.broadcast_to(row, (count, row.shape[1]))


def halves(array):
    high = array.astype(BF16)
    return high, (array - high.astype(F32)).astype(BF16)


def dot_nn(a, b):
    return lax.dot_general(a, b, (((1,), (0,)), ((), ())), preferred_element_type=F32)


def dot_nt(a, b):
    return lax.dot_general(a, b, (((1,), (1,)), ((), ())), preferred_element_type=F32)


def dot_tn(a, b):
    return lax.dot_general(a, b, (((0,), (0,)), ((), ())), preferred_element_type=F32)


def route_kernel(own_count, ids_ref, order_ref, live_ref, send_ref, inverse_ref, owner_ref, rank_ref, value_ref, acc_ref):
    tiles, slots = ids_ref.shape
    own_bits = own_count.bit_length() - 1
    devices = acc_ref.shape[0] // 4
    blocks = slots // LANES
    local_view = (iota((tiles, LANES), 0) >= tiles // 2).astype(I32)
    for block in range(blocks):
        here = slice(block * LANES, (block + 1) * LANES)
        order = order_ref[:, here]
        low, high = order & (LANES - 1), order >> LANE_BITS
        picked = jnp.zeros((tiles, LANES), I32)
        for source in range(blocks):
            found = lanes(ids_ref[:, source * LANES : (source + 1) * LANES], low)
            picked = jnp.where(high == source, found, picked)
        owner = jnp.where(order < live_ref[...], picked >> own_bits, -1)
        value = (picked & (own_count - 1)) + local_view * own_count
        for t in range(tiles):
            owner_ref[t, :, here] = owner[t : t + 1, :]
            value_ref[t, :, here] = value[t : t + 1, :]
    upto = (iota((slots, slots), 0) <= iota((slots, slots), 1)).astype(BF16)
    acc_ref[...] = jnp.zeros_like(acc_ref)
    peers = iota((devices, slots), 0)
    ranks = iota((LANES, slots), 0)
    place = iota((1, slots), 1)

    def tile(t, before):
        owner = owner_ref[t]
        value = value_ref[t]
        named = peers == owner
        count = dot_nn(named.astype(BF16), upto)
        rank = jnp.sum(jnp.where(named, count + before, 0.0), axis=0, keepdims=True) - 1.0
        rank = rank.astype(I32)
        rank_ref[t] = rank
        at_rank = (ranks == rank).astype(BF16)
        parts = [
            (value & 255).astype(F32),
            (value >> 8).astype(F32),
            place.astype(F32),
            jnp.full((1, slots), t + 1).astype(F32),
        ]
        left = jnp.concatenate([jnp.where(named, part, 0.0).astype(BF16) for part in parts], axis=0)
        acc_ref[...] += dot_nt(left, at_rank)
        return before + count[:, slots - 1 :]

    lax.fori_loop(0, tiles, tile, jnp.zeros((devices, 1), F32))
    part = [acc_ref[n * devices : (n + 1) * devices, :].astype(I32) for n in range(4)]
    send_ref[...] = part[0] + 256 * part[1]
    inverse_ref[...] = part[2] + 256 * (part[3] - 1)


def field_of(ref, row):
    return jnp.concatenate([ref[row : row + 1, h * LANES : (h + 1) * LANES] for h in range(ROWS)], axis=0)


def moving_fields(centres, shape_raw, view):
    rows = [view[0:4], view[4:8]]
    e0, e2, e5 = jnp.exp(shape_raw[0]), jnp.exp(shape_raw[2]), jnp.exp(shape_raw[5])
    screen, factor = [], []
    for m in rows:
        screen.append(m[0] * centres[0] + m[1] * centres[1] + m[2] * centres[2] + m[3])
        factor.append(
            (
                m[0] * e0 + m[1] * shape_raw[1] + m[2] * shape_raw[3],
                m[1] * e2 + m[2] * shape_raw[4],
                m[2] * e5,
            )
        )
    fx, fy = factor
    var_x = fx[0] * fx[0] + fx[1] * fx[1] + fx[2] * fx[2] + 0.3
    cov_xy = fx[0] * fy[0] + fx[1] * fy[1] + fx[2] * fy[2]
    var_y = fy[0] * fy[0] + fy[1] * fy[1] + fy[2] * fy[2] + 0.3
    inverse = 1.0 / (var_x * var_y - cov_xy * cov_xy)
    return screen[0], screen[1], var_y * inverse, -cov_xy * inverse, var_x * inverse


def opacity_of(logit):
    return 0.95 / (1.0 + jnp.exp(-logit))


def camera_view(camera_ref, view):
    return [camera_ref[view * 8 + n] for n in range(8)]


def answer_kernel(views, here, centres_ref, shape_ref, logit_ref, colours_ref, camera_ref, got_ref, out_ref, moving_ref, fixed_ref):
    centres = [field_of(centres_ref, n) for n in range(3)]
    shape_raw = [field_of(shape_ref, n) for n in range(6)]
    for view in range(views):
        found = moving_fields(centres, shape_raw, camera_view(camera_ref, view))
        for k in range(MOVING):
            moving_ref[view // here, k, (view % here) * ROWS : (view % here + 1) * ROWS, :] = found[k]
    fixed_ref[0] = opacity_of(logit_ref[...])
    for n in range(3):
        fixed_ref[1 + n] = field_of(colours_ref, n)
    devices = got_ref.shape[0]
    per_group = devices // (views // here) // ROWS

    def block(n, carry):
        row = pl.multiple_of(n * ROWS, ROWS)
        group = n // per_group
        ids = got_ref[pl.ds(row, ROWS), 0:LANES]
        low, high = ids & (LANES - 1), ids >> LANE_BITS
        high_fixed = high & (ROWS - 1)
        for k in range(FIELDS):
            moves = k < MOVING
            total = jnp.zeros((ROWS, LANES), F32)
            for h in range(ROWS * here if moves else ROWS):
                line = moving_ref[group, k, h : h + 1, :] if moves else fixed_ref[k - MOVING, h : h + 1, :]
                total = jnp.where((high if moves else high_fixed) == h, lanes(spread(line, ROWS), low), total)
            out_ref[pl.ds(row, ROWS), k * LANES : (k + 1) * LANES] = total
        return carry

    lax.fori_loop(0, devices // ROWS, block, 0)


def back_kernel(
    views, here, centres_ref, shape_ref, logit_ref, colours_ref, camera_ref, got_ref, given_ref,
    d_centres_ref, d_shape_ref, d_logit_ref, d_colours_ref, moving_ref, fixed_ref,
):
    devices = got_ref.shape[0]
    groups = views // here
    moving_ref[...] = jnp.zeros_like(moving_ref)
    fixed_ref[...] = jnp.zeros_like(fixed_ref)
    wide = ROWS * here
    per_step = 2

    def block(n, carry):
        row = pl.multiple_of(n * ROWS, ROWS)
        group = n // (devices // groups // ROWS)
        ids = got_ref[pl.ds(row, ROWS), 0:LANES]
        values = [given_ref[pl.ds(row, ROWS), k * LANES : (k + 1) * LANES] for k in range(FIELDS)]
        total = None
        for first in range(0, ROWS, per_step):
            lefts, onehots = [], []
            for src in range(first, first + per_step):
                low, high = ids[src : src + 1] & (LANES - 1), ids[src : src + 1] >> LANE_BITS
                at_wide = iota((wide, LANES), 0) == high
                at_row = iota((ROWS, LANES), 0) == (high & (ROWS - 1))
                rows = [
                    jnp.where(at_wide if k < MOVING else at_row, values[k][src : src + 1], 0.0)
                    for k in range(FIELDS)
                ]
                lefts.append(jnp.concatenate(rows, axis=0))
                onehots.append((iota((LANES, LANES), 0) == low).astype(BF16))
            left_high, left_low = halves(jnp.concatenate(lefts, axis=1))
            right = jnp.concatenate(onehots, axis=1)
            found = dot_nt(left_high, right) + dot_nt(left_low, right)
            total = found if total is None else total + found
        moving_ref[group] += total[: MOVING * wide]
        fixed_ref[...] += total[MOVING * wide :]
        return carry

    lax.fori_loop(0, devices // ROWS, block, 0)

    centres = [field_of(centres_ref, n) for n in range(3)]
    shape_raw = [field_of(shape_ref, n) for n in range(6)]
    d_centres = [jnp.zeros((ROWS, LANES), F32)] * 3
    d_shape = [jnp.zeros((ROWS, LANES), F32)] * 6
    for view in range(views):
        camera = camera_view(camera_ref, view)
        _, pull = jax.vjp(lambda c, s: moving_fields(c, s, camera), centres, shape_raw)
        base = (view % here) * ROWS
        given = tuple(
            moving_ref[view // here, k * wide + base : k * wide + base + ROWS, :] for k in range(MOVING)
        )
        more_centres, more_shape = pull(given)
        d_centres = [a + b for a, b in zip(d_centres, more_centres)]
        d_shape = [a + b for a, b in zip(d_shape, more_shape)]

    def put(ref, row, value):
        for h in range(ROWS):
            ref[row : row + 1, h * LANES : (h + 1) * LANES] = value[h : h + 1, :]

    for n in range(3):
        put(d_centres_ref, n, d_centres[n])
        put(d_colours_ref, n, fixed_ref[(1 + n) * ROWS : (2 + n) * ROWS, :])
    for n in range(6):
        put(d_shape_ref, n, d_shape[n])
    _, pull = jax.vjp(opacity_of, logit_ref[...])
    d_logit_ref[...] = pull(fixed_ref[0:ROWS, :])[0]


def render_kernel(
    recv_ref, owner_ref, rank_ref, inverse_ref, target_ref, image_ref, back_ref,
    cov_ref, high_ref, low_ref, dots_ref, grad_ref,
):
    tiles, _, slots = owner_ref.shape
    devices = recv_ref.shape[0]
    blocks = slots // LANES
    half = (SIDE - 1) / 2.0
    log2e = 1.4426950408889634
    before = (iota((slots, slots), 0) < iota((slots, slots), 1)).astype(BF16)
    after = (iota((slots, slots), 0) > iota((slots, slots), 1)).astype(BF16)
    across = iota((SIDE, slots), 0).astype(F32) - half
    sublane = iota((ROWS, LANES), 0)

    def fetch(t, block):
        here = slice(block * LANES, (block + 1) * LANES)
        owner = spread(owner_ref[t, :, here], ROWS) - sublane
        rank = spread(jnp.maximum(rank_ref[t, :, here], 0), ROWS)
        total = [jnp.zeros((ROWS, LANES), F32)] * FIELDS
        for group in range(devices // ROWS):
            mine = owner == group * ROWS
            for k in range(FIELDS):
                table = recv_ref[group * ROWS : (group + 1) * ROWS, k * LANES : (k + 1) * LANES]
                total[k] = jnp.where(mine, lanes(table, rank), total[k])
        return [jnp.sum(one, axis=0, keepdims=True) for one in total]

    def tile(t, carry):
        found = [fetch(t, block) for block in range(blocks)]
        u, w, a, b, c, opacity, red, green, blue = (
            jnp.concatenate([found[block][k] for block in range(blocks)], axis=1) for k in range(FIELDS)
        )
        dx = across - u
        scale = -0.5 * log2e
        first = (scale * a) * dx * dx
        second = (2.0 * scale * b) * dx
        third = scale * c
        for y in range(SIDE):
            rows = slice(y * SIDE, (y + 1) * SIDE)
            dy = (y - half) - w
            cover = opacity * jnp.exp2((second + third * dy) * dy + first)
            cov_ref[rows, :] = cover
            high, low = halves(jnp.log(1.0 - cover))
            high_ref[rows, :] = high
            low_ref[rows, :] = low
        through = jnp.exp(dot_nn(high_ref[...], before) + dot_nn(low_ref[...], before))
        weights = through * cov_ref[...]
        w_high, w_low = halves(weights)
        colour = jnp.concatenate([red, green, blue], axis=0)
        c_high = colour.astype(BF16).astype(F32)
        c_low = colour - c_high
        pair = jnp.concatenate([c_high, c_low], axis=0).astype(BF16)
        drawn = dot_nt(pair, w_high) + dot_nt(pair, w_low)
        image = drawn[0:3] + drawn[3:6]
        image_ref[t] = image
        error = image - target_ref[t]
        e_high = error.astype(BF16).astype(F32)
        e_low = error - e_high
        d_colour = jnp.concatenate([e_high, e_low], axis=0).astype(BF16)
        d_colour = dot_nn(d_colour, w_high) + dot_nn(d_colour, w_low)
        d_colour = d_colour[0:3] + d_colour[3:6]
        left = jnp.concatenate([e_high, e_high, e_low, e_low], axis=0).astype(BF16)
        right = jnp.concatenate([c_high, c_low, c_high, c_low], axis=0).astype(BF16)
        shade = dot_tn(left, right)
        s_high, s_low = halves(weights * shade)
        behind = dot_nn(s_high, after) + dot_nn(s_low, after)
        dots_ref[...] = through * shade * cov_ref[...] - behind * (cov_ref[...] / (1.0 - cov_ref[...]))
        sum0 = jnp.zeros((SIDE, slots), F32)
        sum1, sum2 = sum0, sum0
        for y in range(SIDE):
            given = dots_ref[y * SIDE : (y + 1) * SIDE, :]
            dy = (y - half) - w
            once = given * dy
            sum0, sum1, sum2 = sum0 + given, sum1 + once, sum2 + once * dy

        def down(x):
            return jnp.sum(x, axis=0, keepdims=True)

        once = sum0 * dx
        s0, sx, sxx = down(sum0), down(once), down(once * dx)
        sy, sxy, syy = down(sum1), down(sum1 * dx), down(sum2)
        grads = [
            a * sx + b * sy,
            b * sx + c * sy,
            -0.5 * sxx,
            -sxy,
            -0.5 * syy,
            jnp.where(opacity > 0.0, s0 / opacity, 0.0),
            d_colour[0:1],
            d_colour[1:2],
            d_colour[2:3],
        ]
        for k in range(FIELDS):
            for block in range(blocks):
                grad_ref[k, t * blocks + block] = grads[k][:, block * LANES : (block + 1) * LANES]
        return carry

    lax.fori_loop(0, tiles, tile, 0)

    def give(group, carry):
        row = pl.multiple_of(group * ROWS, ROWS)
        index = inverse_ref[pl.ds(row, ROWS), :]
        low = index & (LANES - 1)
        high = index >> LANE_BITS

        def step(h, totals):
            totals = list(totals)
            for half_step in range(blocks):
                place = h * blocks + half_step
                mine = high == place
                for k in range(FIELDS):
                    totals[k] = jnp.where(mine, lanes(spread(grad_ref[k, place], ROWS), low), totals[k])
            return tuple(totals)

        totals = lax.fori_loop(0, tiles, step, (jnp.zeros((ROWS, LANES), F32),) * FIELDS)
        for k in range(FIELDS):
            back_ref[pl.ds(row, ROWS), k * LANES : (k + 1) * LANES] = totals[k]
        return carry

    lax.fori_loop(0, devices // ROWS, give, 0)


VMEM = pl.BlockSpec(memory_space=pltpu.VMEM)
SMEM = pl.BlockSpec(memory_space=pltpu.SMEM)


def params():
    return pltpu.CompilerParams(vmem_limit_bytes=40 * 2**20)


def shape(dims, kind=F32):
    return jax.ShapeDtypeStruct(dims, kind)


def route(ids, order, live, devices, own_count):
    tiles, slots = ids.shape
    table = shape((devices, LANES), I32)
    return pl.pallas_call(
        partial(route_kernel, own_count),
        out_shape=(table, table, shape((tiles, 1, slots), I32), shape((tiles, 1, slots), I32)),
        in_specs=[VMEM] * 3,
        out_specs=(VMEM,) * 4,
        scratch_shapes=[pltpu.VMEM((tiles, 1, slots), I32), pltpu.VMEM((4 * devices, LANES), F32)],
        compiler_params=params(),
        name="route",
    )(ids, order, live)


def answer(centres, shape_raw, logit, colours, camera, got, views, here):
    return pl.pallas_call(
        partial(answer_kernel, views, here),
        out_shape=shape((got.shape[0], FIELDS * LANES)),
        in_specs=[VMEM] * 4 + [SMEM, VMEM],
        out_specs=VMEM,
        scratch_shapes=[
            pltpu.VMEM((views // here, MOVING, here * ROWS, LANES), F32),
            pltpu.VMEM((FIELDS - MOVING, ROWS, LANES), F32),
        ],
        compiler_params=params(),
        name="answer",
    )(centres, shape_raw, logit, colours, camera, got)


def render(recv, owner, rank, inverse, target):
    tiles, _, slots = owner.shape
    return pl.pallas_call(
        render_kernel,
        out_shape=(shape(target.shape), shape(recv.shape)),
        in_specs=[VMEM] * 5,
        out_specs=(VMEM, VMEM),
        scratch_shapes=[
            pltpu.VMEM((PIX, slots), F32),
            pltpu.VMEM((PIX, slots), BF16),
            pltpu.VMEM((PIX, slots), BF16),
            pltpu.VMEM((PIX, slots), F32),
            pltpu.VMEM((FIELDS, tiles * slots // LANES, 1, LANES), F32),
        ],
        compiler_params=params(),
        name="render",
    )(recv, owner, rank, inverse, target)


def back(centres, shape_raw, logit, colours, camera, got, given, views, here):
    return pl.pallas_call(
        partial(back_kernel, views, here),
        out_shape=(shape(centres.shape), shape(shape_raw.shape), shape(logit.shape), shape(colours.shape)),
        in_specs=[VMEM] * 4 + [SMEM, VMEM, VMEM],
        out_specs=(VMEM,) * 4,
        scratch_shapes=[
            pltpu.VMEM((views // here, MOVING * here * ROWS, LANES), F32),
            pltpu.VMEM(((FIELDS - MOVING) * ROWS, LANES), F32),
        ],
        compiler_params=params(),
        name="back",
    )(centres, shape_raw, logit, colours, camera, got, given)


def shards(centres, shape_raw, opacity_logit, colours, camera, target, intersection_ids, depth_order, live_count):
    view_group, tile_group = lax.axis_size("view"), lax.axis_size("tile")
    devices = view_group * tile_group
    own_count = centres.shape[1]
    here, tiles_here, slots = intersection_ids.shape
    views = camera.shape[0]
    tiles = here * tiles_here
    axes = ("view", "tile")
    exchange = partial(lax.all_to_all, axis_name=axes, split_axis=0, concat_axis=0, tiled=True)

    send, inverse, owner, rank = route(
        intersection_ids.reshape(tiles, slots),
        depth_order.reshape(tiles, slots),
        live_count.reshape(tiles, 1),
        devices,
        own_count,
    )
    totals = jnp.sum(live_count, axis=1)
    told = jnp.zeros((devices, LANES), I32).at[:, 0:here].set(totals[None, :])
    got = exchange(jnp.concatenate([send, told], axis=1))
    logit = opacity_logit.reshape(ROWS, LANES)
    flat_camera = camera.reshape(-1)
    answers = answer(centres, shape_raw, logit, colours, flat_camera, got, views, here)
    recv = exchange(answers)
    image, returned = render(recv, owner, rank, inverse, target.reshape(tiles, 3, PIX))
    given = exchange(returned)
    d_centres, d_shape, d_logit, d_colours = back(
        centres, shape_raw, logit, colours, flat_camera, got, given, views, here
    )

    me_view, me_tile = lax.axis_index("view"), lax.axis_index("tile")
    source = jnp.arange(devices, dtype=I32)[:, None]
    in_group = source // tile_group == me_view
    counts = got[:, LANES : LANES + here]
    whole = jnp.sum(jnp.where(in_group, counts, 0), axis=0)
    before = jnp.sum(jnp.where(in_group & (source % tile_group < me_tile), counts, 0), axis=0)
    earlier = jnp.arange(tiles_here)[:, None] < jnp.arange(tiles_here)[None, :]
    within = jnp.sum(jnp.where(earlier[None], live_count[:, :, None], 0), axis=1)
    next_owner = (before[:, None] + within) * tile_group // whole[:, None]
    return (
        image.reshape(target.shape),
        d_centres,
        d_shape,
        d_logit.reshape(opacity_logit.shape),
        d_colours,
        next_owner.astype(I32),
    )


def solution(mesh):
    in_specs = (
        P(None, ("view", "tile")),
        P(None, ("view", "tile")),
        P(("view", "tile")),
        P(None, ("view", "tile")),
        P(),
        P("view", "tile", None, None),
        P("view", "tile", None),
        P("view", "tile", None),
        P("view", "tile"),
    )
    out_specs = (
        P("view", "tile", None, None),
        P(None, ("view", "tile")),
        P(None, ("view", "tile")),
        P(("view", "tile")),
        P(None, ("view", "tile")),
        P("view", "tile"),
    )
    return jax.shard_map(shards, mesh=mesh, in_specs=in_specs, out_specs=out_specs, check_vma=False)
```

```python
from functools import partial

import jax
import jax.numpy as jnp
from jax import lax
from jax.experimental import pallas as pl
from jax.experimental.pallas import tpu as pltpu
from jax.sharding import PartitionSpec as P

SIDE = 16
PIX = SIDE * SIDE
LANES = 128
LANE_BITS = 7
ROWS = 8
FIELDS = 9
MOVING = 5
TOGETHER = 4
F32 = jnp.float32
BF16 = jnp.bfloat16
I32 = jnp.int32


def lanes(table, index):
    return jnp.take_along_axis(table, index, axis=1, mode="promise_in_bounds")


def iota(shape, axis):
    return lax.broadcasted_iota(I32, shape, axis)


def spread(row, count):
    return jnp.broadcast_to(row, (count, row.shape[1]))


def halves(array):
    high = array.astype(BF16)
    return high, (array - high.astype(F32)).astype(BF16)


def dot_nn(a, b):
    return lax.dot_general(a, b, (((1,), (0,)), ((), ())), preferred_element_type=F32)


def dot_nt(a, b):
    return lax.dot_general(a, b, (((1,), (1,)), ((), ())), preferred_element_type=F32)


def dot_tn(a, b):
    return lax.dot_general(a, b, (((0,), (0,)), ((), ())), preferred_element_type=F32)


def route_kernel(own_count, ids_ref, order_ref, live_ref, send_ref, owner_ref, rank_ref, value_ref, acc_ref):
    tiles, slots = ids_ref.shape
    own_bits = own_count.bit_length() - 1
    devices = acc_ref.shape[0] // 2
    blocks = slots // LANES
    local_view = (iota((tiles, LANES), 0) >= tiles // 2).astype(I32)
    for block in range(blocks):
        here = slice(block * LANES, (block + 1) * LANES)
        order = order_ref[:, here]
        low, high = order & (LANES - 1), order >> LANE_BITS
        picked = jnp.zeros((tiles, LANES), I32)
        for source in range(blocks):
            found = lanes(ids_ref[:, source * LANES : (source + 1) * LANES], low)
            picked = jnp.where(high == source, found, picked)
        owner = jnp.where(order < live_ref[...], picked >> own_bits, -1)
        value = (picked & (own_count - 1)) + local_view * own_count
        for t in range(tiles):
            owner_ref[t, :, here] = owner[t : t + 1, :]
            value_ref[t, :, here] = value[t : t + 1, :]
    upto = (iota((slots, slots), 0) <= iota((slots, slots), 1)).astype(BF16)
    acc_ref[...] = jnp.zeros_like(acc_ref)
    peers = iota((devices, slots), 0)
    ranks = iota((LANES, slots), 0)

    def tile(t, before):
        owner = owner_ref[t]
        value = value_ref[t]
        named = peers == owner
        count = dot_nn(named.astype(BF16), upto)
        rank = jnp.sum(jnp.where(named, count + before, 0.0), axis=0, keepdims=True) - 1.0
        rank = rank.astype(I32)
        rank_ref[t] = rank
        at_rank = (ranks == rank).astype(BF16)
        parts = [(value & 255).astype(F32), (value >> 8).astype(F32)]
        left = jnp.concatenate([jnp.where(named, part, 0.0).astype(BF16) for part in parts], axis=0)
        acc_ref[...] += dot_nt(left, at_rank)
        return before + count[:, slots - 1 :]

    lax.fori_loop(0, tiles, tile, jnp.zeros((devices, 1), F32), unroll=8)
    low, high = acc_ref[0:devices, :].astype(I32), acc_ref[devices:, :].astype(I32)
    send_ref[...] = low + 256 * high


def field_of(ref, row):
    return jnp.concatenate([ref[row : row + 1, h * LANES : (h + 1) * LANES] for h in range(ROWS)], axis=0)


def moving_fields(centres, shape_raw, view):
    rows = [view[0:4], view[4:8]]
    e0, e2, e5 = jnp.exp(shape_raw[0]), jnp.exp(shape_raw[2]), jnp.exp(shape_raw[5])
    screen, factor = [], []
    for m in rows:
        screen.append(m[0] * centres[0] + m[1] * centres[1] + m[2] * centres[2] + m[3])
        factor.append(
            (
                m[0] * e0 + m[1] * shape_raw[1] + m[2] * shape_raw[3],
                m[1] * e2 + m[2] * shape_raw[4],
                m[2] * e5,
            )
        )
    fx, fy = factor
    var_x = fx[0] * fx[0] + fx[1] * fx[1] + fx[2] * fx[2] + 0.3
    cov_xy = fx[0] * fy[0] + fx[1] * fy[1] + fx[2] * fy[2]
    var_y = fy[0] * fy[0] + fy[1] * fy[1] + fy[2] * fy[2] + 0.3
    inverse = 1.0 / (var_x * var_y - cov_xy * cov_xy)
    return screen[0], screen[1], var_y * inverse, -cov_xy * inverse, var_x * inverse


def opacity_of(logit):
    return 0.95 / (1.0 + jnp.exp(-logit))


def camera_view(camera_ref, view):
    return [camera_ref[view * 8 + n] for n in range(8)]


def answer_kernel(views, here, centres_ref, shape_ref, logit_ref, colours_ref, camera_ref, got_ref, out_ref, moving_ref, fixed_ref):
    centres = [field_of(centres_ref, n) for n in range(3)]
    shape_raw = [field_of(shape_ref, n) for n in range(6)]
    for view in range(views):
        found = moving_fields(centres, shape_raw, camera_view(camera_ref, view))
        for k in range(MOVING):
            moving_ref[view // here, k, (view % here) * ROWS : (view % here + 1) * ROWS, :] = found[k]
    fixed_ref[0] = opacity_of(logit_ref[...])
    for n in range(3):
        fixed_ref[1 + n] = field_of(colours_ref, n)
    devices = got_ref.shape[0]
    per_group = devices // (views // here) // ROWS

    def block(n, carry):
        row = pl.multiple_of(n * ROWS, ROWS)
        group = n // per_group
        ids = got_ref[pl.ds(row, ROWS), 0:LANES]
        low, high = ids & (LANES - 1), ids >> LANE_BITS
        high_fixed = high & (ROWS - 1)
        for k in range(FIELDS):
            moves = k < MOVING
            total = jnp.zeros((ROWS, LANES), F32)
            for h in range(ROWS * here if moves else ROWS):
                line = moving_ref[group, k, h : h + 1, :] if moves else fixed_ref[k - MOVING, h : h + 1, :]
                total = jnp.where((high if moves else high_fixed) == h, lanes(spread(line, ROWS), low), total)
            out_ref[pl.ds(row, ROWS), k * LANES : (k + 1) * LANES] = total
        return carry

    lax.fori_loop(0, devices // ROWS, block, 0)


def back_kernel(
    views, here, centres_ref, shape_ref, logit_ref, colours_ref, camera_ref, got_ref, given_ref,
    d_centres_ref, d_shape_ref, d_logit_ref, d_colours_ref, moving_ref, fixed_ref,
):
    devices = got_ref.shape[0]
    groups = views // here
    moving_ref[...] = jnp.zeros_like(moving_ref)
    fixed_ref[...] = jnp.zeros_like(fixed_ref)
    wide = ROWS * here
    per_step = 2

    def block(n, carry):
        row = pl.multiple_of(n * ROWS, ROWS)
        group = n // (devices // groups // ROWS)
        ids = got_ref[pl.ds(row, ROWS), 0:LANES]
        values = [given_ref[pl.ds(row, ROWS), k * LANES : (k + 1) * LANES] for k in range(FIELDS)]
        total = None
        for first in range(0, ROWS, per_step):
            lefts, onehots = [], []
            for src in range(first, first + per_step):
                low, high = ids[src : src + 1] & (LANES - 1), ids[src : src + 1] >> LANE_BITS
                at_wide = iota((wide, LANES), 0) == high
                at_row = iota((ROWS, LANES), 0) == (high & (ROWS - 1))
                rows = [
                    jnp.where(at_wide if k < MOVING else at_row, values[k][src : src + 1], 0.0)
                    for k in range(FIELDS)
                ]
                lefts.append(jnp.concatenate(rows, axis=0))
                onehots.append((iota((LANES, LANES), 0) == low).astype(BF16))
            left_high, left_low = halves(jnp.concatenate(lefts, axis=1))
            right = jnp.concatenate(onehots, axis=1)
            found = dot_nt(left_high, right) + dot_nt(left_low, right)
            total = found if total is None else total + found
        moving_ref[group] += total[: MOVING * wide]
        fixed_ref[...] += total[MOVING * wide :]
        return carry

    lax.fori_loop(0, devices // ROWS, block, 0)

    centres = [field_of(centres_ref, n) for n in range(3)]
    shape_raw = [field_of(shape_ref, n) for n in range(6)]
    d_centres = [jnp.zeros((ROWS, LANES), F32)] * 3
    d_shape = [jnp.zeros((ROWS, LANES), F32)] * 6
    for view in range(views):
        camera = camera_view(camera_ref, view)
        _, pull = jax.vjp(lambda c, s: moving_fields(c, s, camera), centres, shape_raw)
        base = (view % here) * ROWS
        given = tuple(
            moving_ref[view // here, k * wide + base : k * wide + base + ROWS, :] for k in range(MOVING)
        )
        more_centres, more_shape = pull(given)
        d_centres = [a + b for a, b in zip(d_centres, more_centres)]
        d_shape = [a + b for a, b in zip(d_shape, more_shape)]

    def put(ref, row, value):
        for h in range(ROWS):
            ref[row : row + 1, h * LANES : (h + 1) * LANES] = value[h : h + 1, :]

    for n in range(3):
        put(d_centres_ref, n, d_centres[n])
        put(d_colours_ref, n, fixed_ref[(1 + n) * ROWS : (2 + n) * ROWS, :])
    for n in range(6):
        put(d_shape_ref, n, d_shape[n])
    _, pull = jax.vjp(opacity_of, logit_ref[...])
    d_logit_ref[...] = pull(fixed_ref[0:ROWS, :])[0]


def render_kernel(
    recv_ref, owner_ref, rank_ref, target_ref, image_ref, back_ref,
    cov_ref, odds_ref, high_ref, low_ref, dots_ref, acc_ref,
):
    tiles, _, slots = owner_ref.shape
    devices = recv_ref.shape[0]
    blocks = slots // LANES
    half = (SIDE - 1) / 2.0
    log2e = 1.4426950408889634
    before = (iota((slots, slots), 0) < iota((slots, slots), 1)).astype(BF16)
    after = (iota((slots, slots), 0) > iota((slots, slots), 1)).astype(BF16)
    across = iota((SIDE, slots), 0).astype(F32) - half
    sublane = iota((ROWS, LANES), 0)
    split = devices // 2
    peers, places = iota((split, slots), 0), iota((2 * LANES, slots), 0)

    def fetch(t, block):
        here = slice(block * LANES, (block + 1) * LANES)
        owner = spread(owner_ref[t, :, here], ROWS) - sublane
        rank = spread(jnp.maximum(rank_ref[t, :, here], 0), ROWS)
        total = [jnp.zeros((ROWS, LANES), F32)] * FIELDS
        for group in range(devices // ROWS):
            mine = owner == group * ROWS
            for k in range(FIELDS):
                table = recv_ref[group * ROWS : (group + 1) * ROWS, k * LANES : (k + 1) * LANES]
                total[k] = jnp.where(mine, lanes(table, rank), total[k])
        return [jnp.sum(one, axis=0, keepdims=True) for one in total]

    def tile(t, lane):
        cov, odds, high_part, low_part, dots = (
            ref.at[lane] for ref in (cov_ref, odds_ref, high_ref, low_ref, dots_ref)
        )
        found = [fetch(t, block) for block in range(blocks)]
        u, w, a, b, c, opacity, red, green, blue = (
            jnp.concatenate([found[block][k] for block in range(blocks)], axis=1) for k in range(FIELDS)
        )
        yield
        dx = across - u
        scale = -0.5 * log2e
        first = (scale * a) * dx * dx
        second = (2.0 * scale * b) * dx
        third = scale * c
        for y in range(SIDE):
            rows = slice(y * SIDE, (y + 1) * SIDE)
            dy = (y - half) - w
            cover = opacity * jnp.exp2((second + third * dy) * dy + first)
            cov[rows, :] = cover
            keep = jnp.log(1.0 - cover)
            odds[rows, :] = cover * jnp.exp(-keep)
            high, low = halves(keep)
            high_part[rows, :] = high
            low_part[rows, :] = low
        yield
        through = jnp.exp(dot_nn(high_part[...], before) + dot_nn(low_part[...], before))
        weights = through * cov[...]
        w_high, w_low = halves(weights)
        yield
        colour = jnp.concatenate([red, green, blue], axis=0)
        c_high = colour.astype(BF16).astype(F32)
        c_low = colour - c_high
        pair = jnp.concatenate([c_high, c_low], axis=0).astype(BF16)
        drawn = dot_nt(pair, w_high) + dot_nt(pair, w_low)
        image = drawn[0:3] + drawn[3:6]
        image_ref[t] = image
        error = image - target_ref[t]
        e_high = error.astype(BF16).astype(F32)
        e_low = error - e_high
        d_colour = jnp.concatenate([e_high, e_low], axis=0).astype(BF16)
        d_colour = dot_nn(d_colour, w_high) + dot_nn(d_colour, w_low)
        d_colour = d_colour[0:3] + d_colour[3:6]
        yield
        column = jnp.concatenate([error, jnp.zeros((ROWS - 3, PIX), F32)], axis=0).T
        shade = column[:, 0:1] * red + column[:, 1:2] * green + column[:, 2:3] * blue
        shaded = weights * shade
        s_high, s_low = halves(shaded)
        yield
        behind = dot_nn(s_high, after) + dot_nn(s_low, after)
        dots[...] = shaded - behind * odds[...]
        yield
        sum0 = jnp.zeros((SIDE, slots), F32)
        sum1, sum2 = sum0, sum0
        for y in range(SIDE):
            given = dots[y * SIDE : (y + 1) * SIDE, :]
            dy = (y - half) - w
            once = given * dy
            sum0, sum1, sum2 = sum0 + given, sum1 + once, sum2 + once * dy

        def down(x):
            return jnp.sum(x, axis=0, keepdims=True)

        once = sum0 * dx
        s0, sx, sxx = down(sum0), down(once), down(once * dx)
        sy, sxy, syy = down(sum1), down(sum1 * dx), down(sum2)
        grads = [
            a * sx + b * sy,
            b * sx + c * sy,
            -0.5 * sxx,
            -sxy,
            -0.5 * syy,
            jnp.where(opacity > 0.0, s0 / opacity, 0.0),
            d_colour[0:1],
            d_colour[1:2],
            d_colour[2:3],
        ]
        owner, rank = owner_ref[t], rank_ref[t]
        yield
        named = ((owner & (split - 1)) == peers).astype(BF16)
        place = (owner >> (split.bit_length() - 1)) * LANES + rank == places
        parts = [halves(grad) for grad in grads]
        left = [jnp.concatenate([named * part[n] for part in parts], axis=0) for n in range(2)]
        right = place.astype(BF16)
        acc_ref[...] += dot_nt(jnp.concatenate(left, axis=1), jnp.concatenate([right, right], axis=1))

    def together(n, carry):
        running = [tile(n * TOGETHER + lane, lane) for lane in range(TOGETHER)]
        while running:
            running = [one for one in running if next(one, one) is None]
        return carry

    acc_ref[...] = jnp.zeros_like(acc_ref)
    lax.fori_loop(0, tiles // TOGETHER, together, 0)
    for k in range(FIELDS):
        for n in range(2):
            back_ref[n * split : (n + 1) * split, k * LANES : (k + 1) * LANES] = acc_ref[
                k * split : (k + 1) * split, n * LANES : (n + 1) * LANES
            ]


VMEM = pl.BlockSpec(memory_space=pltpu.VMEM)
SMEM = pl.BlockSpec(memory_space=pltpu.SMEM)


def params():
    return pltpu.CompilerParams(vmem_limit_bytes=40 * 2**20)


def shape(dims, kind=F32):
    return jax.ShapeDtypeStruct(dims, kind)


def route(ids, order, live, devices, own_count):
    tiles, slots = ids.shape
    return pl.pallas_call(
        partial(route_kernel, own_count),
        out_shape=(shape((devices, LANES), I32), shape((tiles, 1, slots), I32), shape((tiles, 1, slots), I32)),
        in_specs=[VMEM] * 3,
        out_specs=(VMEM,) * 3,
        scratch_shapes=[pltpu.VMEM((tiles, 1, slots), I32), pltpu.VMEM((2 * devices, LANES), F32)],
        compiler_params=params(),
        name="route",
    )(ids, order, live)


def answer(centres, shape_raw, logit, colours, camera, got, views, here):
    return pl.pallas_call(
        partial(answer_kernel, views, here),
        out_shape=shape((got.shape[0], FIELDS * LANES)),
        in_specs=[VMEM] * 4 + [SMEM, VMEM],
        out_specs=VMEM,
        scratch_shapes=[
            pltpu.VMEM((views // here, MOVING, here * ROWS, LANES), F32),
            pltpu.VMEM((FIELDS - MOVING, ROWS, LANES), F32),
        ],
        compiler_params=params(),
        name="answer",
    )(centres, shape_raw, logit, colours, camera, got)


def render(recv, owner, rank, target):
    tiles, _, slots = owner.shape
    return pl.pallas_call(
        render_kernel,
        out_shape=(shape(target.shape), shape(recv.shape)),
        in_specs=[VMEM] * 4,
        out_specs=(VMEM, VMEM),
        scratch_shapes=[
            pltpu.VMEM((TOGETHER, PIX, slots), F32),
            pltpu.VMEM((TOGETHER, PIX, slots), F32),
            pltpu.VMEM((TOGETHER, PIX, slots), BF16),
            pltpu.VMEM((TOGETHER, PIX, slots), BF16),
            pltpu.VMEM((TOGETHER, PIX, slots), F32),
            pltpu.VMEM((FIELDS * recv.shape[0] // 2, 2 * LANES), F32),
        ],
        compiler_params=params(),
        name="render",
    )(recv, owner, rank, target)


def back(centres, shape_raw, logit, colours, camera, got, given, views, here):
    return pl.pallas_call(
        partial(back_kernel, views, here),
        out_shape=(shape(centres.shape), shape(shape_raw.shape), shape(logit.shape), shape(colours.shape)),
        in_specs=[VMEM] * 4 + [SMEM, VMEM, VMEM],
        out_specs=(VMEM,) * 4,
        scratch_shapes=[
            pltpu.VMEM((views // here, MOVING * here * ROWS, LANES), F32),
            pltpu.VMEM(((FIELDS - MOVING) * ROWS, LANES), F32),
        ],
        compiler_params=params(),
        name="back",
    )(centres, shape_raw, logit, colours, camera, got, given)


def shards(centres, shape_raw, opacity_logit, colours, camera, target, intersection_ids, depth_order, live_count):
    view_group, tile_group = lax.axis_size("view"), lax.axis_size("tile")
    devices = view_group * tile_group
    own_count = centres.shape[1]
    here, tiles_here, slots = intersection_ids.shape
    views = camera.shape[0]
    tiles = here * tiles_here
    axes = ("view", "tile")
    exchange = partial(lax.all_to_all, axis_name=axes, split_axis=0, concat_axis=0, tiled=True)

    send, owner, rank = route(
        intersection_ids.reshape(tiles, slots),
        depth_order.reshape(tiles, slots),
        live_count.reshape(tiles, 1),
        devices,
        own_count,
    )
    totals = jnp.sum(live_count, axis=1)
    told = jnp.zeros((devices, LANES), I32).at[:, 0:here].set(totals[None, :])
    got = exchange(jnp.concatenate([send, told], axis=1))
    logit = opacity_logit.reshape(ROWS, LANES)
    flat_camera = camera.reshape(-1)
    answers = answer(centres, shape_raw, logit, colours, flat_camera, got, views, here)
    recv = exchange(answers)
    image, returned = render(recv, owner, rank, target.reshape(tiles, 3, PIX))
    given = exchange(returned)
    d_centres, d_shape, d_logit, d_colours = back(
        centres, shape_raw, logit, colours, flat_camera, got, given, views, here
    )

    me_view, me_tile = lax.axis_index("view"), lax.axis_index("tile")
    source = jnp.arange(devices, dtype=I32)[:, None]
    in_group = source // tile_group == me_view
    counts = got[:, LANES : LANES + here]
    whole = jnp.sum(jnp.where(in_group, counts, 0), axis=0)
    before = jnp.sum(jnp.where(in_group & (source % tile_group < me_tile), counts, 0), axis=0)
    earlier = jnp.arange(tiles_here)[:, None] < jnp.arange(tiles_here)[None, :]
    within = jnp.sum(jnp.where(earlier[None], live_count[:, :, None], 0), axis=1)
    next_owner = (before[:, None] + within) * tile_group // whole[:, None]
    return (
        image.reshape(target.shape),
        d_centres,
        d_shape,
        d_logit.reshape(opacity_logit.shape),
        d_colours,
        next_owner.astype(I32),
    )


def solution(mesh):
    in_specs = (
        P(None, ("view", "tile")),
        P(None, ("view", "tile")),
        P(("view", "tile")),
        P(None, ("view", "tile")),
        P(),
        P("view", "tile", None, None),
        P("view", "tile", None),
        P("view", "tile", None),
        P("view", "tile"),
    )
    out_specs = (
        P("view", "tile", None, None),
        P(None, ("view", "tile")),
        P(None, ("view", "tile")),
        P(("view", "tile")),
        P(None, ("view", "tile")),
        P("view", "tile"),
    )
    return jax.shard_map(shards, mesh=mesh, in_specs=in_specs, out_specs=out_specs, check_vma=False)
```

```python
from functools import partial

import jax
import jax.numpy as jnp
from jax import lax
from jax.experimental import pallas as pl
from jax.experimental.pallas import tpu as pltpu
from jax.sharding import PartitionSpec as P

SIDE = 16
PIX = SIDE * SIDE
LANES = 128
LANE_BITS = 7
ROWS = 8
FIELDS = 9
MOVING = 5
TOGETHER = 4
F32 = jnp.float32
BF16 = jnp.bfloat16
I32 = jnp.int32


def lanes(table, index):
    return jnp.take_along_axis(table, index, axis=1, mode="promise_in_bounds")


def iota(shape, axis):
    return lax.broadcasted_iota(I32, shape, axis)


def spread(row, count):
    return jnp.broadcast_to(row, (count, row.shape[1]))


def halves(array):
    high = array.astype(BF16)
    return high, (array - high.astype(F32)).astype(BF16)


def dot_nn(a, b):
    return lax.dot_general(a, b, (((1,), (0,)), ((), ())), preferred_element_type=F32)


def dot_nt(a, b):
    return lax.dot_general(a, b, (((1,), (1,)), ((), ())), preferred_element_type=F32)


def dot_tn(a, b):
    return lax.dot_general(a, b, (((0,), (0,)), ((), ())), preferred_element_type=F32)


MESH = pl.DeviceIdType.MESH


class Ring:
    def __init__(self, view_group, tile_group):
        self.bits = tile_group.bit_length() - 1
        self.tiles = tile_group
        self.count = view_group * tile_group
        self.me = lax.axis_index("view") * tile_group + lax.axis_index("tile")

    def place(self, device):
        return (device >> self.bits, device & (self.tiles - 1))

    def after(self, step):
        return (self.me + step) & (self.count - 1)

    def greet(self, step):
        pl.semaphore_signal(
            pltpu.get_barrier_semaphore(), inc=1, device_id=self.place(self.after(step)), device_id_type=MESH
        )

    def copy(self, source, target, send_sem, recv_sem, device):
        return pltpu.make_async_remote_copy(
            src_ref=source,
            dst_ref=target,
            send_sem=send_sem.at[device],
            recv_sem=recv_sem.at[self.me],
            device_id=self.place(device),
            device_id_type=MESH,
        )


def each(first, last, unroll, body):
    def step(n, carry):
        body(n)
        return carry

    lax.fori_loop(first, last, step, 0, unroll=unroll)


def ask_kernel(
    sizes, views, ids_ref, order_ref, live_ref, centres_ref, shape_ref, logit_ref, colours_ref, camera_ref,
    recv_ref, got_ref, owner_ref, rank_ref,
    value_ref, acc_ref, send_ref, answer_ref, moving_ref, fixed_ref,
    request_send, request_recv, answer_send, answer_recv, local_sem,
):
    ring = Ring(*sizes)
    me, devices = ring.me, ring.count
    tiles, slots = ids_ref.shape
    here, tiles_here = live_ref.shape
    own_count = centres_ref.shape[1]
    own_bits = own_count.bit_length() - 1
    blocks = slots // LANES
    per_tile = devices // tiles
    turned = live_ref[...].astype(F32).T
    live = jnp.concatenate([turned[:, n : n + 1] for n in range(here)], axis=0).astype(I32)
    local_view = (iota((tiles, LANES), 0) >= tiles_here).astype(I32)
    for block in range(blocks):
        cut = slice(block * LANES, (block + 1) * LANES)
        order = order_ref[:, cut]
        low, high = order & (LANES - 1), order >> LANE_BITS
        picked = jnp.zeros((tiles, LANES), I32)
        for source in range(blocks):
            found = lanes(ids_ref[:, source * LANES : (source + 1) * LANES], low)
            picked = jnp.where(high == source, found, picked)
        owner = jnp.where(order < live, picked >> own_bits, -1)
        value = (picked & (own_count - 1)) + local_view * own_count
        for t in range(tiles):
            owner_ref[t, :, cut] = owner[t : t + 1, :]
            value_ref[t, :, cut] = value[t : t + 1, :]
    upto = (iota((slots, slots), 0) <= iota((slots, slots), 1)).astype(BF16)
    acc_ref[...] = jnp.zeros_like(acc_ref)
    peers = iota((devices, slots), 0)
    ranks = iota((LANES, slots), 0)

    def tile(t, before):
        for n in range(per_tile - 1):
            ring.greet(t * per_tile + n + 1)

        @pl.when(t < tiles - 1)
        def _():
            ring.greet(t * per_tile + per_tile)

        owner, value = owner_ref[t], value_ref[t]
        named = peers == owner
        count = dot_nn(named.astype(BF16), upto)
        rank = jnp.sum(jnp.where(named, count + before, 0.0), axis=0, keepdims=True) - 1.0
        rank = rank.astype(I32)
        rank_ref[t] = rank
        at_rank = (ranks == rank).astype(BF16)
        parts = [(value & 255).astype(F32), (value >> 8).astype(F32)]
        left = jnp.concatenate([jnp.where(named, part, 0.0).astype(BF16) for part in parts], axis=0)
        acc_ref[...] += dot_nt(left, at_rank)
        return before + count[:, slots - 1 :]

    lax.fori_loop(0, tiles, tile, jnp.zeros((devices, 1), F32), unroll=8)
    low, high = acc_ref[0:devices, :].astype(I32), acc_ref[devices:, :].astype(I32)
    lane = iota((1, LANES), 1)
    told = jnp.zeros((1, LANES), I32)
    for n in range(here):
        total = jnp.sum(live[n * tiles_here : (n + 1) * tiles_here].astype(F32), axis=0, keepdims=True)
        told = jnp.where(lane == n, total.astype(I32), told)
    send_ref[:, 0, 0:LANES] = low + 256 * high
    send_ref[:, 0, LANES:] = spread(told, devices)

    pl.semaphore_wait(pltpu.get_barrier_semaphore(), devices - 1)
    own_request = pltpu.make_async_copy(send_ref.at[me], got_ref.at[me], local_sem.at[0])
    own_request.start()

    def request(device):
        return ring.copy(send_ref.at[device], got_ref.at[me], request_send, request_recv, device)

    each(1, devices, 16, lambda step: request(ring.after(step)).start())

    centres = [field_of(centres_ref, n) for n in range(3)]
    shape_raw = [field_of(shape_ref, n) for n in range(6)]
    for view in range(views):
        found = moving_fields(centres, shape_raw, camera_view(camera_ref, view))
        for k in range(MOVING):
            moving_ref[view // here, k, (view % here) * ROWS : (view % here + 1) * ROWS, :] = found[k]
    fixed_ref[0] = opacity_of(logit_ref[...])
    for n in range(3):
        fixed_ref[1 + n] = field_of(colours_ref, n)
    own_request.wait()
    steps = devices // ROWS
    per_group = steps // (views // here)

    def arrived(semaphores, target, device):
        pltpu.make_async_copy(target, target, semaphores.at[device]).wait()

    def answer(device):
        return ring.copy(answer_ref.at[:, device], recv_ref.at[:, me], answer_send, answer_recv, device)

    def block(n):
        turn = ((me >> 3) - n) & (steps - 1)
        row = pl.multiple_of(turn * ROWS, ROWS)
        group = turn // per_group
        for s in range(ROWS):

            @pl.when(row + s != me)
            def _(s=s):
                arrived(request_recv, got_ref.at[row + s], row + s)

        ids = got_ref[pl.ds(row, ROWS), 0, 0:LANES]
        low, high = ids & (LANES - 1), ids >> LANE_BITS
        high_fixed = high & (ROWS - 1)
        for k in range(FIELDS):
            moves = k < MOVING
            total = jnp.zeros((ROWS, LANES), F32)
            for h in range(ROWS * here if moves else ROWS):
                line = moving_ref[group, k, h : h + 1, :] if moves else fixed_ref[k - MOVING, h : h + 1, :]
                total = jnp.where((high if moves else high_fixed) == h, lanes(spread(line, ROWS), low), total)
            answer_ref[k, pl.ds(row, ROWS), 0, :] = total
        for s in range(ROWS):
            device = row + ((me + s) & (ROWS - 1))

            @pl.when(device != me)
            def _(device=device):
                answer(device).start()

    each(0, steps, 1, block)
    own_answer = pltpu.make_async_copy(answer_ref.at[:, me], recv_ref.at[:, me], local_sem.at[1])
    own_answer.start()

    def finish(step):
        device = ring.after(step)
        request(device).wait_send()
        answer(device).wait_send()
        arrived(answer_recv, recv_ref.at[:, device], device)

    each(1, devices, 16, finish)
    own_answer.wait()


def field_of(ref, row):
    return jnp.concatenate([ref[row : row + 1, h * LANES : (h + 1) * LANES] for h in range(ROWS)], axis=0)


def moving_fields(centres, shape_raw, view):
    rows = [view[0:4], view[4:8]]
    e0, e2, e5 = jnp.exp(shape_raw[0]), jnp.exp(shape_raw[2]), jnp.exp(shape_raw[5])
    screen, factor = [], []
    for m in rows:
        screen.append(m[0] * centres[0] + m[1] * centres[1] + m[2] * centres[2] + m[3])
        factor.append(
            (
                m[0] * e0 + m[1] * shape_raw[1] + m[2] * shape_raw[3],
                m[1] * e2 + m[2] * shape_raw[4],
                m[2] * e5,
            )
        )
    fx, fy = factor
    var_x = fx[0] * fx[0] + fx[1] * fx[1] + fx[2] * fx[2] + 0.3
    cov_xy = fx[0] * fy[0] + fx[1] * fy[1] + fx[2] * fy[2]
    var_y = fy[0] * fy[0] + fy[1] * fy[1] + fy[2] * fy[2] + 0.3
    inverse = 1.0 / (var_x * var_y - cov_xy * cov_xy)
    return screen[0], screen[1], var_y * inverse, -cov_xy * inverse, var_x * inverse


def opacity_of(logit):
    return 0.95 / (1.0 + jnp.exp(-logit))


def camera_view(camera_ref, view):
    return [camera_ref[view, n // 4, n % 4] for n in range(8)]


def give_kernel(
    sizes, views, here, centres_ref, shape_ref, logit_ref, colours_ref, camera_ref, got_ref, table_ref,
    d_centres_ref, d_shape_ref, d_logit_ref, d_colours_ref,
    given_ref, moving_ref, fixed_ref, send_sem, recv_sem, local_sem,
):
    ring = Ring(*sizes)
    me, devices = ring.me, ring.count
    each(1, devices, 16, ring.greet)
    groups = views // here
    moving_ref[...] = jnp.zeros_like(moving_ref)
    fixed_ref[...] = jnp.zeros_like(fixed_ref)
    wide = ROWS * here
    per_step = 2
    own = pltpu.make_async_copy(table_ref.at[:, me], given_ref.at[:, me], local_sem)
    own.start()
    pl.semaphore_wait(pltpu.get_barrier_semaphore(), devices - 1)

    def copy(device):
        return ring.copy(table_ref.at[:, device], given_ref.at[:, me], send_sem, recv_sem, device)

    each(1, devices, 16, lambda step: copy(ring.after(step)).start())
    own.wait()
    steps = devices // ROWS

    def block(n):
        turn = ((me >> 3) - n) & (steps - 1)
        row = pl.multiple_of(turn * ROWS, ROWS)
        group = turn // (steps // groups)
        for s in range(ROWS):

            @pl.when(row + s != me)
            def _(s=s):
                target = given_ref.at[:, row + s]
                pltpu.make_async_copy(target, target, recv_sem.at[row + s]).wait()

        ids = got_ref[pl.ds(row, ROWS), 0, 0:LANES]
        values = [given_ref[k, pl.ds(row, ROWS), 0, :] for k in range(FIELDS)]
        total = None
        for first in range(0, ROWS, per_step):
            lefts, onehots = [], []
            for src in range(first, first + per_step):
                low, high = ids[src : src + 1] & (LANES - 1), ids[src : src + 1] >> LANE_BITS
                at_wide = iota((wide, LANES), 0) == high
                at_row = iota((ROWS, LANES), 0) == (high & (ROWS - 1))
                rows = [
                    jnp.where(at_wide if k < MOVING else at_row, values[k][src : src + 1], 0.0)
                    for k in range(FIELDS)
                ]
                lefts.append(jnp.concatenate(rows, axis=0))
                onehots.append((iota((LANES, LANES), 0) == low).astype(BF16))
            left_high, left_low = halves(jnp.concatenate(lefts, axis=1))
            right = jnp.concatenate(onehots, axis=1)
            found = dot_nt(left_high, right) + dot_nt(left_low, right)
            total = found if total is None else total + found
        moving_ref[group] += total[: MOVING * wide]
        fixed_ref[...] += total[MOVING * wide :]

    each(0, steps, 1, block)
    each(1, devices, 16, lambda step: copy(ring.after(step)).wait_send())

    centres = [field_of(centres_ref, n) for n in range(3)]
    shape_raw = [field_of(shape_ref, n) for n in range(6)]
    d_centres = [jnp.zeros((ROWS, LANES), F32)] * 3
    d_shape = [jnp.zeros((ROWS, LANES), F32)] * 6
    for view in range(views):
        camera = camera_view(camera_ref, view)
        _, pull = jax.vjp(lambda c, s: moving_fields(c, s, camera), centres, shape_raw)
        base = (view % here) * ROWS
        given = tuple(
            moving_ref[view // here, k * wide + base : k * wide + base + ROWS, :] for k in range(MOVING)
        )
        more_centres, more_shape = pull(given)
        d_centres = [a + b for a, b in zip(d_centres, more_centres)]
        d_shape = [a + b for a, b in zip(d_shape, more_shape)]

    def put(ref, row, value):
        for h in range(ROWS):
            ref[row : row + 1, h * LANES : (h + 1) * LANES] = value[h : h + 1, :]

    for n in range(3):
        put(d_centres_ref, n, d_centres[n])
        put(d_colours_ref, n, fixed_ref[(1 + n) * ROWS : (2 + n) * ROWS, :])
    for n in range(6):
        put(d_shape_ref, n, d_shape[n])
    _, pull = jax.vjp(opacity_of, logit_ref[...])
    d_logit_ref[...] = pull(fixed_ref[0:ROWS, :])[0]


def next_owner(ring, got_ref, live_ref, next_ref):
    here, tiles_here = live_ref.shape
    counts = got_ref[:, 0, LANES:].astype(F32)
    source = iota((ring.count, LANES), 0)
    mine = source >> ring.bits == lax.axis_index("view")
    lower = mine & ((source & (ring.tiles - 1)) < lax.axis_index("tile"))
    own_lane = iota((here, LANES), 0) == iota((here, LANES), 1)

    def column(mask):
        row = jnp.sum(jnp.where(mask, counts, 0.0), axis=0, keepdims=True)
        return jnp.sum(jnp.where(own_lane, spread(row, here), 0.0), axis=1, keepdims=True)

    whole, before = column(mine), column(lower)
    earlier = (iota((tiles_here, tiles_here), 0) < iota((tiles_here, tiles_here), 1)).astype(BF16)
    start = before + dot_nn(live_ref[...].astype(F32).astype(BF16), earlier)
    above, below = (start * ring.tiles).astype(I32), whole.astype(I32)
    quotient = (start * ring.tiles / whole).astype(I32)
    rest = above - quotient * below
    next_ref[...] = quotient + (rest >= below).astype(I32) - (rest < 0).astype(I32)


def render_kernel(
    sizes, recv_ref, owner_ref, rank_ref, target_ref, got_ref, live_ref, image_ref, back_ref, next_ref,
    cov_ref, odds_ref, high_ref, low_ref, dots_ref, acc_ref,
):
    tiles, _, slots = owner_ref.shape
    devices = recv_ref.shape[1]
    blocks = slots // LANES
    next_owner(Ring(*sizes), got_ref, live_ref, next_ref)
    half = (SIDE - 1) / 2.0
    log2e = 1.4426950408889634
    before = (iota((slots, slots), 0) < iota((slots, slots), 1)).astype(BF16)
    after = (iota((slots, slots), 0) > iota((slots, slots), 1)).astype(BF16)
    across = iota((SIDE, slots), 0).astype(F32) - half
    sublane = iota((ROWS, LANES), 0)
    split = devices // 2
    peers, places = iota((split, slots), 0), iota((2 * LANES, slots), 0)

    def fetch(t, block):
        here = slice(block * LANES, (block + 1) * LANES)
        owner = spread(owner_ref[t, :, here], ROWS) - sublane
        rank = spread(jnp.maximum(rank_ref[t, :, here], 0), ROWS)
        total = [jnp.zeros((ROWS, LANES), F32)] * FIELDS
        for group in range(devices // ROWS):
            mine = owner == group * ROWS
            for k in range(FIELDS):
                table = recv_ref[k, group * ROWS : (group + 1) * ROWS, :]
                total[k] = jnp.where(mine, lanes(table, rank), total[k])
        return [jnp.sum(one, axis=0, keepdims=True) for one in total]

    def tile(t, lane):
        cov, odds, high_part, low_part, dots = (
            ref.at[lane] for ref in (cov_ref, odds_ref, high_ref, low_ref, dots_ref)
        )
        found = [fetch(t, block) for block in range(blocks)]
        u, w, a, b, c, opacity, red, green, blue = (
            jnp.concatenate([found[block][k] for block in range(blocks)], axis=1) for k in range(FIELDS)
        )
        yield
        dx = across - u
        scale = -0.5 * log2e
        first = (scale * a) * dx * dx
        second = (2.0 * scale * b) * dx
        third = scale * c
        for y in range(SIDE):
            rows = slice(y * SIDE, (y + 1) * SIDE)
            dy = (y - half) - w
            cover = opacity * jnp.exp2((second + third * dy) * dy + first)
            cov[rows, :] = cover
            keep = jnp.log(1.0 - cover)
            odds[rows, :] = cover * jnp.exp(-keep)
            high, low = halves(keep)
            high_part[rows, :] = high
            low_part[rows, :] = low
        yield
        through = jnp.exp(dot_nn(high_part[...], before) + dot_nn(low_part[...], before))
        weights = through * cov[...]
        w_high, w_low = halves(weights)
        yield
        colour = jnp.concatenate([red, green, blue], axis=0)
        c_high = colour.astype(BF16).astype(F32)
        c_low = colour - c_high
        pair = jnp.concatenate([c_high, c_low], axis=0).astype(BF16)
        drawn = dot_nt(pair, w_high) + dot_nt(pair, w_low)
        image = drawn[0:3] + drawn[3:6]
        image_ref[t] = image
        error = image - target_ref[t]
        e_high = error.astype(BF16).astype(F32)
        e_low = error - e_high
        d_colour = jnp.concatenate([e_high, e_low], axis=0).astype(BF16)
        d_colour = dot_nn(d_colour, w_high) + dot_nn(d_colour, w_low)
        d_colour = d_colour[0:3] + d_colour[3:6]
        yield
        column = jnp.concatenate([error, jnp.zeros((ROWS - 3, PIX), F32)], axis=0).T
        shade = column[:, 0:1] * red + column[:, 1:2] * green + column[:, 2:3] * blue
        shaded = weights * shade
        s_high, s_low = halves(shaded)
        yield
        behind = dot_nn(s_high, after) + dot_nn(s_low, after)
        dots[...] = shaded - behind * odds[...]
        yield
        sum0 = jnp.zeros((SIDE, slots), F32)
        sum1, sum2 = sum0, sum0
        for y in range(SIDE):
            given = dots[y * SIDE : (y + 1) * SIDE, :]
            dy = (y - half) - w
            once = given * dy
            sum0, sum1, sum2 = sum0 + given, sum1 + once, sum2 + once * dy

        def down(x):
            return jnp.sum(x, axis=0, keepdims=True)

        once = sum0 * dx
        s0, sx, sxx = down(sum0), down(once), down(once * dx)
        sy, sxy, syy = down(sum1), down(sum1 * dx), down(sum2)
        grads = [
            a * sx + b * sy,
            b * sx + c * sy,
            -0.5 * sxx,
            -sxy,
            -0.5 * syy,
            jnp.where(opacity > 0.0, s0 / opacity, 0.0),
            d_colour[0:1],
            d_colour[1:2],
            d_colour[2:3],
        ]
        owner, rank = owner_ref[t], rank_ref[t]
        yield
        named = ((owner & (split - 1)) == peers).astype(BF16)
        place = (owner >> (split.bit_length() - 1)) * LANES + rank == places
        parts = [halves(grad) for grad in grads]
        left = [jnp.concatenate([named * part[n] for part in parts], axis=0) for n in range(2)]
        right = place.astype(BF16)
        acc_ref[...] += dot_nt(jnp.concatenate(left, axis=1), jnp.concatenate([right, right], axis=1))

    def together(n, carry):
        running = [tile(n * TOGETHER + lane, lane) for lane in range(TOGETHER)]
        while running:
            running = [one for one in running if next(one, one) is None]
        return carry

    acc_ref[...] = jnp.zeros_like(acc_ref)
    lax.fori_loop(0, tiles // TOGETHER, together, 0)
    for k in range(FIELDS):
        for n in range(2):
            back_ref[k, n * split : (n + 1) * split, :] = acc_ref[
                k * split : (k + 1) * split, n * LANES : (n + 1) * LANES
            ]


VMEM = pl.BlockSpec(memory_space=pltpu.VMEM)
SMEM = pl.BlockSpec(memory_space=pltpu.SMEM)


def params(number=None):
    limit = 40 * 2**20
    if number is None:
        return pltpu.CompilerParams(vmem_limit_bytes=limit)
    return pltpu.CompilerParams(vmem_limit_bytes=limit, collective_id=number, has_side_effects=True)


def shape(dims, kind=F32):
    return jax.ShapeDtypeStruct(dims, kind)


def dma(*dims):
    return pltpu.SemaphoreType.DMA(dims)


def ask(sizes, ids, order, live, centres, shape_raw, logit, colours, camera):
    tiles, slots = ids.shape
    devices, views, here = sizes[0] * sizes[1], camera.shape[0], live.shape[0]
    table = (FIELDS, devices, 1, LANES)
    return pl.pallas_call(
        partial(ask_kernel, sizes, views),
        out_shape=(
            shape(table),
            shape((devices, 1, 2 * LANES), I32),
            shape((tiles, 1, slots), I32),
            shape((tiles, 1, slots), I32),
        ),
        in_specs=[VMEM] * 7 + [SMEM],
        out_specs=(VMEM,) * 4,
        scratch_shapes=[
            pltpu.VMEM((tiles, 1, slots), I32),
            pltpu.VMEM((2 * devices, LANES), F32),
            pltpu.VMEM((devices, 1, 2 * LANES), I32),
            pltpu.VMEM(table, F32),
            pltpu.VMEM((views // here, MOVING, here * ROWS, LANES), F32),
            pltpu.VMEM((FIELDS - MOVING, ROWS, LANES), F32),
            dma(devices),
            dma(devices),
            dma(devices),
            dma(devices),
            dma(2),
        ],
        compiler_params=params(0),
        name="ask",
    )(ids, order, live, centres, shape_raw, logit, colours, camera)


def render(sizes, recv, owner, rank, target, got, live):
    tiles, _, slots = owner.shape
    return pl.pallas_call(
        partial(render_kernel, sizes),
        out_shape=(shape(target.shape), shape(recv.shape), shape(live.shape, I32)),
        in_specs=[VMEM] * 6,
        out_specs=(VMEM,) * 3,
        scratch_shapes=[
            pltpu.VMEM((TOGETHER, PIX, slots), F32),
            pltpu.VMEM((TOGETHER, PIX, slots), F32),
            pltpu.VMEM((TOGETHER, PIX, slots), BF16),
            pltpu.VMEM((TOGETHER, PIX, slots), BF16),
            pltpu.VMEM((TOGETHER, PIX, slots), F32),
            pltpu.VMEM((FIELDS * recv.shape[1] // 2, 2 * LANES), F32),
        ],
        compiler_params=params(),
        name="render",
    )(recv, owner, rank, target, got, live)


def give(sizes, here, centres, shape_raw, logit, colours, camera, got, table):
    views = camera.shape[0]
    devices = got.shape[0]
    return pl.pallas_call(
        partial(give_kernel, sizes, views, here),
        out_shape=(shape(centres.shape), shape(shape_raw.shape), shape(logit.shape), shape(colours.shape)),
        in_specs=[VMEM] * 4 + [SMEM, VMEM, VMEM],
        out_specs=(VMEM,) * 4,
        scratch_shapes=[
            pltpu.VMEM(table.shape, F32),
            pltpu.VMEM((views // here, MOVING * here * ROWS, LANES), F32),
            pltpu.VMEM(((FIELDS - MOVING) * ROWS, LANES), F32),
            dma(devices),
            dma(devices),
            pltpu.SemaphoreType.DMA,
        ],
        compiler_params=params(1),
        name="give",
    )(centres, shape_raw, logit, colours, camera, got, table)


def shards(centres, shape_raw, opacity_logit, colours, camera, target, intersection_ids, depth_order, live_count):
    sizes = (lax.axis_size("view"), lax.axis_size("tile"))
    devices = sizes[0] * sizes[1]
    here, tiles_here, slots = intersection_ids.shape
    tiles = here * tiles_here
    logit = opacity_logit.reshape(ROWS, LANES)
    recv, got, owner, rank = ask(
        sizes,
        intersection_ids.reshape(tiles, slots),
        depth_order.reshape(tiles, slots),
        live_count,
        centres,
        shape_raw,
        logit,
        colours,
        camera,
    )
    image, table, owners = render(
        sizes,
        recv.reshape(FIELDS, devices, LANES),
        owner,
        rank,
        target.reshape(tiles, 3, PIX),
        got,
        live_count,
    )
    d_centres, d_shape, d_logit, d_colours = give(
        sizes, here, centres, shape_raw, logit, colours, camera, got, table.reshape(FIELDS, devices, 1, LANES)
    )
    return (
        image.reshape(target.shape),
        d_centres,
        d_shape,
        d_logit.reshape(opacity_logit.shape),
        d_colours,
        owners,
    )


def solution(mesh):
    in_specs = (
        P(None, ("view", "tile")),
        P(None, ("view", "tile")),
        P(("view", "tile")),
        P(None, ("view", "tile")),
        P(),
        P("view", "tile", None, None),
        P("view", "tile", None),
        P("view", "tile", None),
        P("view", "tile"),
    )
    out_specs = (
        P("view", "tile", None, None),
        P(None, ("view", "tile")),
        P(None, ("view", "tile")),
        P(("view", "tile")),
        P(None, ("view", "tile")),
        P("view", "tile"),
    )
    return jax.shard_map(shards, mesh=mesh, in_specs=in_specs, out_specs=out_specs, check_vma=False)
```

```python
from functools import partial

import jax
import jax.numpy as jnp
from jax import lax
from jax.experimental import pallas as pl
from jax.experimental.pallas import tpu as pltpu
from jax.sharding import PartitionSpec as P

SIDE = 16
PIX = SIDE * SIDE
LANES = 128
LANE_BITS = 7
ROWS = 8
FIELDS = 9
MOVING = 5
TOGETHER = 4
F32 = jnp.float32
BF16 = jnp.bfloat16
I32 = jnp.int32


def lanes(table, index):
    return jnp.take_along_axis(table, index, axis=1, mode="promise_in_bounds")


def iota(shape, axis):
    return lax.broadcasted_iota(I32, shape, axis)


def spread(row, count):
    return jnp.broadcast_to(row, (count, row.shape[1]))


def halves(array):
    high = array.astype(BF16)
    return high, (array - high.astype(F32)).astype(BF16)


def dot_nn(a, b):
    return lax.dot_general(a, b, (((1,), (0,)), ((), ())), preferred_element_type=F32)


def dot_nt(a, b):
    return lax.dot_general(a, b, (((1,), (1,)), ((), ())), preferred_element_type=F32)


def dot_tn(a, b):
    return lax.dot_general(a, b, (((0,), (0,)), ((), ())), preferred_element_type=F32)


MESH = pl.DeviceIdType.MESH


class Ring:
    def __init__(self, view_group, tile_group):
        self.bits = tile_group.bit_length() - 1
        self.tiles = tile_group
        self.count = view_group * tile_group
        self.me = lax.axis_index("view") * tile_group + lax.axis_index("tile")

    def place(self, device):
        return (device >> self.bits, device & (self.tiles - 1))

    def after(self, step):
        return (self.me + step) & (self.count - 1)

    def greet(self, step):
        pl.semaphore_signal(
            pltpu.get_barrier_semaphore(), inc=1, device_id=self.place(self.after(step)), device_id_type=MESH
        )

    def copy(self, source, target, send_sem, recv_sem, device):
        return pltpu.make_async_remote_copy(
            src_ref=source,
            dst_ref=target,
            send_sem=send_sem.at[device],
            recv_sem=recv_sem.at[self.me],
            device_id=self.place(device),
            device_id_type=MESH,
        )


def each(first, last, unroll, body):
    def step(n, carry):
        body(n)
        return carry

    lax.fori_loop(first, last, step, 0, unroll=unroll)


def ask(
    ring, views, ids_ref, order_ref, live_ref, centres_ref, shape_ref, logit_ref, colours_ref, camera_ref,
    records_ref, got_ref, owner_ref, rank_ref,
    value_ref, acc_ref, send_ref, answer_ref, recv_ref, moving_ref, fixed_ref,
    request_send, request_recv, answer_send, answer_recv, local_sem,
):
    me, devices = ring.me, ring.count
    tiles, slots = ids_ref.shape
    here, tiles_here = live_ref.shape
    own_count = centres_ref.shape[1]
    own_bits = own_count.bit_length() - 1
    blocks = slots // LANES
    per_tile = devices // tiles
    turned = live_ref[...].astype(F32).T
    live = jnp.concatenate([turned[:, n : n + 1] for n in range(here)], axis=0).astype(I32)
    local_view = (iota((tiles, LANES), 0) >= tiles_here).astype(I32)
    for block in range(blocks):
        cut = slice(block * LANES, (block + 1) * LANES)
        order = order_ref[:, cut]
        low, high = order & (LANES - 1), order >> LANE_BITS
        picked = jnp.zeros((tiles, LANES), I32)
        for source in range(blocks):
            found = lanes(ids_ref[:, source * LANES : (source + 1) * LANES], low)
            picked = jnp.where(high == source, found, picked)
        owner = jnp.where(order < live, picked >> own_bits, -1)
        value = (picked & (own_count - 1)) + local_view * own_count
        for t in range(tiles):
            owner_ref[t, :, cut] = owner[t : t + 1, :]
            value_ref[t, :, cut] = value[t : t + 1, :]
    upto = (iota((slots, slots), 0) <= iota((slots, slots), 1)).astype(BF16)
    acc_ref[...] = jnp.zeros_like(acc_ref)
    peers = iota((devices, slots), 0)
    ranks = iota((LANES, slots), 0)

    def tile(t, before):
        for n in range(per_tile - 1):
            ring.greet(t * per_tile + n + 1)

        @pl.when(t < tiles - 1)
        def _():
            ring.greet(t * per_tile + per_tile)

        owner, value = owner_ref[t], value_ref[t]
        named = peers == owner
        count = dot_nn(named.astype(BF16), upto)
        rank = jnp.sum(jnp.where(named, count + before, 0.0), axis=0, keepdims=True) - 1.0
        rank = rank.astype(I32)
        rank_ref[t] = rank
        at_rank = (ranks == rank).astype(BF16)
        parts = [(value & 255).astype(F32), (value >> 8).astype(F32)]
        left = jnp.concatenate([jnp.where(named, part, 0.0).astype(BF16) for part in parts], axis=0)
        acc_ref[...] += dot_nt(left, at_rank)
        return before + count[:, slots - 1 :]

    lax.fori_loop(0, tiles, tile, jnp.zeros((devices, 1), F32), unroll=8)
    low, high = acc_ref[0:devices, :].astype(I32), acc_ref[devices:, :].astype(I32)
    lane = iota((1, LANES), 1)
    told = jnp.zeros((1, LANES), I32)
    for n in range(here):
        total = jnp.sum(live[n * tiles_here : (n + 1) * tiles_here].astype(F32), axis=0, keepdims=True)
        told = jnp.where(lane == n, total.astype(I32), told)
    send_ref[:, 0, 0:LANES] = low + 256 * high
    send_ref[:, 0, LANES:] = spread(told, devices)

    pl.semaphore_wait(pltpu.get_barrier_semaphore(), devices - 1)
    own_request = pltpu.make_async_copy(send_ref.at[me], got_ref.at[me], local_sem.at[0])
    own_request.start()

    def request(device):
        return ring.copy(send_ref.at[device], got_ref.at[me], request_send, request_recv, device)

    each(1, devices, 16, lambda step: request(ring.after(step)).start())

    centres = [field_of(centres_ref, n) for n in range(3)]
    shape_raw = [field_of(shape_ref, n) for n in range(6)]
    for view in range(views):
        found = moving_fields(centres, shape_raw, camera_view(camera_ref, view))
        for k in range(MOVING):
            moving_ref[view // here, k, (view % here) * ROWS : (view % here + 1) * ROWS, :] = found[k]
    fixed_ref[0] = opacity_of(logit_ref[...])
    for n in range(3):
        fixed_ref[1 + n] = field_of(colours_ref, n)
    own_request.wait()
    steps = devices // ROWS
    per_group = steps // (views // here)

    def arrived(semaphores, target, device):
        pltpu.make_async_copy(target, target, semaphores.at[device]).wait()

    def answer(device):
        return ring.copy(answer_ref.at[:, device], recv_ref.at[:, me], answer_send, answer_recv, device)

    def block(n):
        turn = ((me >> 3) - n) & (steps - 1)
        row = pl.multiple_of(turn * ROWS, ROWS)
        group = turn // per_group
        for s in range(ROWS):

            @pl.when(row + s != me)
            def _(s=s):
                arrived(request_recv, got_ref.at[row + s], row + s)

        ids = got_ref[pl.ds(row, ROWS), 0, 0:LANES]
        low, high = ids & (LANES - 1), ids >> LANE_BITS
        high_fixed = high & (ROWS - 1)
        for k in range(FIELDS):
            moves = k < MOVING
            total = jnp.zeros((ROWS, LANES), F32)
            for h in range(ROWS * here if moves else ROWS):
                line = moving_ref[group, k, h : h + 1, :] if moves else fixed_ref[k - MOVING, h : h + 1, :]
                total = jnp.where((high if moves else high_fixed) == h, lanes(spread(line, ROWS), low), total)
            answer_ref[k, pl.ds(row, ROWS), 0, :] = total
        for s in range(ROWS):
            device = row + ((me + s) & (ROWS - 1))

            @pl.when(device != me)
            def _(device=device):
                answer(device).start()

    each(0, steps, 1, block)
    own_answer = pltpu.make_async_copy(answer_ref.at[:, me], recv_ref.at[:, me], local_sem.at[1])
    own_answer.start()

    own_answer.wait()

    def land(n):
        turn = ((me >> 3) + n) & (steps - 1)
        row = pl.multiple_of(turn * ROWS, ROWS)
        for s in range(ROWS):

            @pl.when(row + s != me)
            def _(s=s):
                arrived(answer_recv, recv_ref.at[:, row + s], row + s)

        for k in range(FIELDS):
            records_ref[k, pl.ds(row, ROWS), :] = recv_ref[k, pl.ds(row, ROWS), 0, :]

    each(0, steps, 1, land)

    def sent(step):
        device = ring.after(step)
        request(device).wait_send()
        answer(device).wait_send()

    return lambda: each(1, devices, 16, sent)


def field_of(ref, row):
    return jnp.concatenate([ref[row : row + 1, h * LANES : (h + 1) * LANES] for h in range(ROWS)], axis=0)


def moving_fields(centres, shape_raw, view):
    rows = [view[0:4], view[4:8]]
    e0, e2, e5 = jnp.exp(shape_raw[0]), jnp.exp(shape_raw[2]), jnp.exp(shape_raw[5])
    screen, factor = [], []
    for m in rows:
        screen.append(m[0] * centres[0] + m[1] * centres[1] + m[2] * centres[2] + m[3])
        factor.append(
            (
                m[0] * e0 + m[1] * shape_raw[1] + m[2] * shape_raw[3],
                m[1] * e2 + m[2] * shape_raw[4],
                m[2] * e5,
            )
        )
    fx, fy = factor
    var_x = fx[0] * fx[0] + fx[1] * fx[1] + fx[2] * fx[2] + 0.3
    cov_xy = fx[0] * fy[0] + fx[1] * fy[1] + fx[2] * fy[2]
    var_y = fy[0] * fy[0] + fy[1] * fy[1] + fy[2] * fy[2] + 0.3
    inverse = 1.0 / (var_x * var_y - cov_xy * cov_xy)
    return screen[0], screen[1], var_y * inverse, -cov_xy * inverse, var_x * inverse


def opacity_of(logit):
    return 0.95 / (1.0 + jnp.exp(-logit))


def camera_view(camera_ref, view):
    return [camera_ref[view, n // 4, n % 4] for n in range(8)]


def give(ring, views, here, got_ref, table_ref, given_ref, moving_ref, fixed_ref, send_sem, recv_sem, local_sem):
    me, devices = ring.me, ring.count
    groups = views // here
    moving_ref[...] = jnp.zeros_like(moving_ref)
    fixed_ref[...] = jnp.zeros_like(fixed_ref)
    wide = ROWS * here
    per_step = 2
    own = pltpu.make_async_copy(table_ref.at[:, me], given_ref.at[:, me], local_sem)
    own.start()

    def copy(device):
        return ring.copy(table_ref.at[:, device], given_ref.at[:, me], send_sem, recv_sem, device)

    each(1, devices, 16, lambda step: copy(ring.after(step)).start())
    own.wait()
    steps = devices // ROWS

    def block(n):
        turn = ((me >> 3) - n) & (steps - 1)
        row = pl.multiple_of(turn * ROWS, ROWS)
        group = turn // (steps // groups)
        for s in range(ROWS):

            @pl.when(row + s != me)
            def _(s=s):
                target = given_ref.at[:, row + s]
                pltpu.make_async_copy(target, target, recv_sem.at[row + s]).wait()

        ids = got_ref[pl.ds(row, ROWS), 0, 0:LANES]
        values = [given_ref[k, pl.ds(row, ROWS), 0, :] for k in range(FIELDS)]
        total = None
        for first in range(0, ROWS, per_step):
            lefts, onehots = [], []
            for src in range(first, first + per_step):
                low, high = ids[src : src + 1] & (LANES - 1), ids[src : src + 1] >> LANE_BITS
                at_wide = iota((wide, LANES), 0) == high
                at_row = iota((ROWS, LANES), 0) == (high & (ROWS - 1))
                rows = [
                    jnp.where(at_wide if k < MOVING else at_row, values[k][src : src + 1], 0.0)
                    for k in range(FIELDS)
                ]
                lefts.append(jnp.concatenate(rows, axis=0))
                onehots.append((iota((LANES, LANES), 0) == low).astype(BF16))
            left_high, left_low = halves(jnp.concatenate(lefts, axis=1))
            right = jnp.concatenate(onehots, axis=1)
            found = dot_nt(left_high, right) + dot_nt(left_low, right)
            total = found if total is None else total + found
        moving_ref[group] += total[: MOVING * wide]
        fixed_ref[...] += total[MOVING * wide :]

    each(0, steps, 1, block)
    each(1, devices, 16, lambda step: copy(ring.after(step)).wait_send())


def pull_kernel(
    views, here, centres_ref, shape_ref, logit_ref, camera_ref, moving_ref, fixed_ref, owners_ref,
    d_centres_ref, d_shape_ref, d_logit_ref, d_colours_ref, next_ref,
):
    wide = ROWS * here
    next_ref[...] = owners_ref[...]
    centres = [field_of(centres_ref, n) for n in range(3)]
    shape_raw = [field_of(shape_ref, n) for n in range(6)]
    d_centres = [jnp.zeros((ROWS, LANES), F32)] * 3
    d_shape = [jnp.zeros((ROWS, LANES), F32)] * 6
    for view in range(views):
        camera = camera_view(camera_ref, view)
        _, pull = jax.vjp(lambda c, s: moving_fields(c, s, camera), centres, shape_raw)
        base = (view % here) * ROWS
        given = tuple(
            moving_ref[view // here, k * wide + base : k * wide + base + ROWS, :] for k in range(MOVING)
        )
        more_centres, more_shape = pull(given)
        d_centres = [a + b for a, b in zip(d_centres, more_centres)]
        d_shape = [a + b for a, b in zip(d_shape, more_shape)]

    def put(ref, row, value):
        for h in range(ROWS):
            ref[row : row + 1, h * LANES : (h + 1) * LANES] = value[h : h + 1, :]

    for n in range(3):
        put(d_centres_ref, n, d_centres[n])
        put(d_colours_ref, n, fixed_ref[(1 + n) * ROWS : (2 + n) * ROWS, :])
    for n in range(6):
        put(d_shape_ref, n, d_shape[n])
    _, pull = jax.vjp(opacity_of, logit_ref[...])
    d_logit_ref[...] = pull(fixed_ref[0:ROWS, :])[0]


def next_owner(ring, got_ref, live_ref, next_ref):
    here, tiles_here = live_ref.shape
    counts = got_ref[:, 0, LANES:].astype(F32)
    source = iota((ring.count, LANES), 0)
    mine = source >> ring.bits == lax.axis_index("view")
    lower = mine & ((source & (ring.tiles - 1)) < lax.axis_index("tile"))
    own_lane = iota((here, LANES), 0) == iota((here, LANES), 1)

    def column(mask):
        row = jnp.sum(jnp.where(mask, counts, 0.0), axis=0, keepdims=True)
        return jnp.sum(jnp.where(own_lane, spread(row, here), 0.0), axis=1, keepdims=True)

    whole, before = column(mine), column(lower)
    earlier = (iota((tiles_here, tiles_here), 0) < iota((tiles_here, tiles_here), 1)).astype(BF16)
    start = before + dot_nn(live_ref[...].astype(F32).astype(BF16), earlier)
    above, below = (start * ring.tiles).astype(I32), whole.astype(I32)
    quotient = (start * ring.tiles / whole).astype(I32)
    rest = above - quotient * below
    next_ref[...] = quotient + (rest >= below).astype(I32) - (rest < 0).astype(I32)


def render(
    ring, recv_ref, owner_ref, rank_ref, target_ref, image_ref, table_ref,
    cov_ref, odds_ref, high_ref, low_ref, dots_ref, acc_ref,
):
    tiles, _, slots = owner_ref.shape
    devices = ring.count
    blocks = slots // LANES
    half = (SIDE - 1) / 2.0
    log2e = 1.4426950408889634
    before = (iota((slots, slots), 0) < iota((slots, slots), 1)).astype(BF16)
    after = (iota((slots, slots), 0) > iota((slots, slots), 1)).astype(BF16)
    across = iota((SIDE, slots), 0).astype(F32) - half
    sublane = iota((ROWS, LANES), 0)
    split = devices // 2
    peers, places = iota((split, slots), 0), iota((2 * LANES, slots), 0)

    def fetch(t, block):
        here = slice(block * LANES, (block + 1) * LANES)
        owner = spread(owner_ref[t, :, here], ROWS) - sublane
        rank = spread(jnp.maximum(rank_ref[t, :, here], 0), ROWS)
        total = [jnp.zeros((ROWS, LANES), F32)] * FIELDS
        for group in range(devices // ROWS):
            mine = owner == group * ROWS
            for k in range(FIELDS):
                table = recv_ref[k, group * ROWS : (group + 1) * ROWS, :]
                total[k] = jnp.where(mine, lanes(table, rank), total[k])
        return [jnp.sum(one, axis=0, keepdims=True) for one in total]

    def tile(t, lane):
        cov, odds, high_part, low_part, dots = (
            ref.at[lane] for ref in (cov_ref, odds_ref, high_ref, low_ref, dots_ref)
        )
        found = [fetch(t, block) for block in range(blocks)]
        u, w, a, b, c, opacity, red, green, blue = (
            jnp.concatenate([found[block][k] for block in range(blocks)], axis=1) for k in range(FIELDS)
        )
        yield
        dx = across - u
        scale = -0.5 * log2e
        first = (scale * a) * dx * dx
        second = (2.0 * scale * b) * dx
        third = scale * c
        for y in range(SIDE):
            rows = slice(y * SIDE, (y + 1) * SIDE)
            dy = (y - half) - w
            cover = opacity * jnp.exp2((second + third * dy) * dy + first)
            cov[rows, :] = cover
            keep = jnp.log(1.0 - cover)
            odds[rows, :] = cover * jnp.exp(-keep)
            high, low = halves(keep)
            high_part[rows, :] = high
            low_part[rows, :] = low
        yield
        through = jnp.exp(dot_nn(high_part[...], before) + dot_nn(low_part[...], before))
        weights = through * cov[...]
        w_high, w_low = halves(weights)
        yield
        colour = jnp.concatenate([red, green, blue], axis=0)
        c_high = colour.astype(BF16).astype(F32)
        c_low = colour - c_high
        pair = jnp.concatenate([c_high, c_low], axis=0).astype(BF16)
        drawn = dot_nt(pair, w_high) + dot_nt(pair, w_low)
        image = drawn[0:3] + drawn[3:6]
        image_ref[t] = image
        error = image - target_ref[t]
        yield
        column = jnp.concatenate([error, jnp.zeros((ROWS - 3, PIX), F32)], axis=0).T
        d_colour = [jnp.sum(weights * column[:, n : n + 1], axis=0, keepdims=True) for n in range(3)]
        shade = column[:, 0:1] * red + column[:, 1:2] * green + column[:, 2:3] * blue
        shaded = weights * shade
        s_high, s_low = halves(shaded)
        yield
        behind = dot_nn(s_high, after) + dot_nn(s_low, after)
        dots[...] = shaded - behind * odds[...]
        yield
        sum0 = jnp.zeros((SIDE, slots), F32)
        sum1, sum2 = sum0, sum0
        for y in range(SIDE):
            given = dots[y * SIDE : (y + 1) * SIDE, :]
            dy = (y - half) - w
            once = given * dy
            sum0, sum1, sum2 = sum0 + given, sum1 + once, sum2 + once * dy

        def down(x):
            return jnp.sum(x, axis=0, keepdims=True)

        once = sum0 * dx
        s0, sx, sxx = down(sum0), down(once), down(once * dx)
        sy, sxy, syy = down(sum1), down(sum1 * dx), down(sum2)
        grads = [
            a * sx + b * sy,
            b * sx + c * sy,
            -0.5 * sxx,
            -sxy,
            -0.5 * syy,
            jnp.where(opacity > 0.0, s0 / opacity, 0.0),
            *d_colour,
        ]
        owner, rank = owner_ref[t], rank_ref[t]
        yield
        named = ((owner & (split - 1)) == peers).astype(BF16)
        place = (owner >> (split.bit_length() - 1)) * LANES + rank == places
        parts = [halves(grad) for grad in grads]
        left = [jnp.concatenate([named * part[n] for part in parts], axis=0) for n in range(2)]
        right = place.astype(BF16)
        acc_ref[...] += dot_nt(jnp.concatenate(left, axis=1), jnp.concatenate([right, right], axis=1))

    def together(n, carry):
        running = [tile(n * TOGETHER + lane, lane) for lane in range(TOGETHER)]
        while running:
            running = [one for one in running if next(one, one) is None]
        return carry

    acc_ref[...] = jnp.zeros_like(acc_ref)
    lax.fori_loop(0, tiles // TOGETHER, together, 0)
    for k in range(FIELDS):
        for n in range(2):
            table_ref[k, n * split : (n + 1) * split, 0, :] = acc_ref[
                k * split : (k + 1) * split, n * LANES : (n + 1) * LANES
            ]


def splat_kernel(
    sizes, views, ids_ref, order_ref, live_ref, centres_ref, shape_ref, logit_ref, colours_ref, camera_ref, target_ref,
    image_ref, moving_ref, fixed_ref, next_ref,
    records_ref, got_ref, owner_ref, rank_ref, value_ref, ask_acc_ref, send_ref, answer_ref, recv_ref,
    own_moving_ref, own_fixed_ref, cov_ref, odds_ref, high_ref, low_ref, dots_ref, acc_ref, table_ref, given_ref,
    request_send, request_recv, answer_send, answer_recv, give_send, give_recv, local_sem,
):
    ring = Ring(*sizes)
    sent = ask(
        ring, views, ids_ref, order_ref, live_ref, centres_ref, shape_ref, logit_ref, colours_ref, camera_ref,
        records_ref, got_ref, owner_ref, rank_ref,
        value_ref, ask_acc_ref, send_ref, answer_ref, recv_ref, own_moving_ref, own_fixed_ref,
        request_send, request_recv, answer_send, answer_recv, local_sem,
    )
    next_owner(ring, got_ref, live_ref, next_ref)
    render(
        ring, records_ref, owner_ref, rank_ref, target_ref, image_ref, table_ref,
        cov_ref, odds_ref, high_ref, low_ref, dots_ref, acc_ref,
    )
    give(
        ring, views, live_ref.shape[0], got_ref, table_ref, given_ref, moving_ref, fixed_ref,
        give_send, give_recv, local_sem.at[2],
    )
    sent()


VMEM = pl.BlockSpec(memory_space=pltpu.VMEM)
SMEM = pl.BlockSpec(memory_space=pltpu.SMEM)


def params(number=None):
    limit = 40 * 2**20
    if number is None:
        return pltpu.CompilerParams(vmem_limit_bytes=limit)
    return pltpu.CompilerParams(vmem_limit_bytes=limit, collective_id=number, has_side_effects=True)


def shape(dims, kind=F32):
    return jax.ShapeDtypeStruct(dims, kind)


def dma(*dims):
    return pltpu.SemaphoreType.DMA(dims)


def splat(sizes, ids, order, live, centres, shape_raw, logit, colours, camera, target):
    tiles, slots = ids.shape
    devices, views, here = sizes[0] * sizes[1], camera.shape[0], live.shape[0]
    table = (FIELDS, devices, 1, LANES)
    line = (tiles, 1, slots)
    return pl.pallas_call(
        partial(splat_kernel, sizes, views),
        out_shape=(
            shape(target.shape),
            shape((views // here, MOVING * here * ROWS, LANES)),
            shape(((FIELDS - MOVING) * ROWS, LANES)),
            shape(live.shape, I32),
        ),
        in_specs=[VMEM] * 7 + [SMEM, VMEM],
        out_specs=(VMEM,) * 4,
        scratch_shapes=[
            pltpu.VMEM((FIELDS, devices, LANES), F32),
            pltpu.VMEM((devices, 1, 2 * LANES), I32),
            pltpu.VMEM(line, I32),
            pltpu.VMEM(line, I32),
            pltpu.VMEM(line, I32),
            pltpu.VMEM((2 * devices, LANES), F32),
            pltpu.VMEM((devices, 1, 2 * LANES), I32),
            pltpu.VMEM(table, F32),
            pltpu.VMEM(table, F32),
            pltpu.VMEM((views // here, MOVING, here * ROWS, LANES), F32),
            pltpu.VMEM((FIELDS - MOVING, ROWS, LANES), F32),
            pltpu.VMEM((TOGETHER, PIX, slots), F32),
            pltpu.VMEM((TOGETHER, PIX, slots), F32),
            pltpu.VMEM((TOGETHER, PIX, slots), BF16),
            pltpu.VMEM((TOGETHER, PIX, slots), BF16),
            pltpu.VMEM((TOGETHER, PIX, slots), F32),
            pltpu.VMEM((FIELDS * devices // 2, 2 * LANES), F32),
            pltpu.VMEM(table, F32),
            pltpu.VMEM(table, F32),
        ]
        + [dma(devices)] * 6
        + [dma(3)],
        compiler_params=params(0),
        name="splat",
    )(ids, order, live, centres, shape_raw, logit, colours, camera, target)


def pull(here, centres, shape_raw, logit, camera, moving, fixed, owners):
    return pl.pallas_call(
        partial(pull_kernel, camera.shape[0], here),
        out_shape=(
            shape(centres.shape),
            shape(shape_raw.shape),
            shape(logit.shape),
            shape(centres.shape),
            shape(owners.shape, I32),
        ),
        in_specs=[VMEM] * 3 + [SMEM] + [VMEM] * 3,
        out_specs=(VMEM,) * 5,
        compiler_params=params(),
        name="pull",
    )(centres, shape_raw, logit, camera, moving, fixed, owners)


def shards(centres, shape_raw, opacity_logit, colours, camera, target, intersection_ids, depth_order, live_count):
    sizes = (lax.axis_size("view"), lax.axis_size("tile"))
    here, tiles_here, slots = intersection_ids.shape
    tiles = here * tiles_here
    logit = opacity_logit.reshape(ROWS, LANES)
    image, moving, fixed, owners = splat(
        sizes,
        intersection_ids.reshape(tiles, slots),
        depth_order.reshape(tiles, slots),
        live_count,
        centres,
        shape_raw,
        logit,
        colours,
        camera,
        target.reshape(tiles, 3, PIX),
    )
    d_centres, d_shape, d_logit, d_colours, owners = pull(
        here, centres, shape_raw, logit, camera, moving, fixed, owners
    )
    return (
        image.reshape(target.shape),
        d_centres,
        d_shape,
        d_logit.reshape(opacity_logit.shape),
        d_colours,
        owners,
    )


def solution(mesh):
    in_specs = (
        P(None, ("view", "tile")),
        P(None, ("view", "tile")),
        P(("view", "tile")),
        P(None, ("view", "tile")),
        P(),
        P("view", "tile", None, None),
        P("view", "tile", None),
        P("view", "tile", None),
        P("view", "tile"),
    )
    out_specs = (
        P("view", "tile", None, None),
        P(None, ("view", "tile")),
        P(None, ("view", "tile")),
        P(("view", "tile")),
        P(None, ("view", "tile")),
        P("view", "tile"),
    )
    return jax.shard_map(shards, mesh=mesh, in_specs=in_specs, out_specs=out_specs, check_vma=False)
```

```python
from functools import partial

import jax
import jax.numpy as jnp
from jax import lax
from jax.experimental import pallas as pl
from jax.experimental.pallas import tpu as pltpu
from jax.sharding import PartitionSpec as P

SIDE = 16
PIX = SIDE * SIDE
LANES = 128
LANE_BITS = 7
ROWS = 8
FIELDS = 9
MOVING = 5
TOGETHER = 4
F32 = jnp.float32
BF16 = jnp.bfloat16
I32 = jnp.int32


def lanes(table, index):
    return jnp.take_along_axis(table, index, axis=1, mode="promise_in_bounds")


def iota(shape, axis):
    return lax.broadcasted_iota(I32, shape, axis)


def spread(row, count):
    return jnp.broadcast_to(row, (count, row.shape[1]))


def halves(array):
    high = array.astype(BF16)
    return high, (array - high.astype(F32)).astype(BF16)


def dot_nn(a, b):
    return lax.dot_general(a, b, (((1,), (0,)), ((), ())), preferred_element_type=F32)


def dot_nt(a, b):
    return lax.dot_general(a, b, (((1,), (1,)), ((), ())), preferred_element_type=F32)


def dot_tn(a, b):
    return lax.dot_general(a, b, (((0,), (0,)), ((), ())), preferred_element_type=F32)


MESH = pl.DeviceIdType.MESH


class Ring:
    def __init__(self, view_group, tile_group):
        self.bits = tile_group.bit_length() - 1
        self.tiles = tile_group
        self.count = view_group * tile_group
        self.me = lax.axis_index("view") * tile_group + lax.axis_index("tile")

    def place(self, device):
        return (device >> self.bits, device & (self.tiles - 1))

    def after(self, step):
        return (self.me + step) & (self.count - 1)

    def greet(self, step):
        pl.semaphore_signal(
            pltpu.get_barrier_semaphore(), inc=1, device_id=self.place(self.after(step)), device_id_type=MESH
        )

    def copy(self, source, target, send_sem, recv_sem, device):
        return pltpu.make_async_remote_copy(
            src_ref=source,
            dst_ref=target,
            send_sem=send_sem.at[device],
            recv_sem=recv_sem.at[self.me],
            device_id=self.place(device),
            device_id_type=MESH,
        )


def each(first, last, unroll, body):
    def step(n, carry):
        body(n)
        return carry

    lax.fori_loop(first, last, step, 0, unroll=unroll)


def ask(
    ring, views, ids_ref, order_ref, live_ref, centres_ref, shape_ref, logit_ref, colours_ref, camera_ref,
    records_ref, got_ref, owner_ref, rank_ref,
    value_ref, acc_ref, send_ref, answer_ref, recv_ref, moving_ref, fixed_ref,
    request_send, request_recv, answer_send, answer_recv, local_sem,
):
    me, devices = ring.me, ring.count
    tiles, slots = ids_ref.shape
    here, tiles_here = live_ref.shape
    own_count = centres_ref.shape[1]
    own_bits = own_count.bit_length() - 1
    blocks = slots // LANES
    turned = live_ref[...].astype(F32).T
    live = jnp.concatenate([turned[:, n : n + 1] for n in range(here)], axis=0).astype(I32)
    local_view = (iota((tiles, LANES), 0) >= tiles_here).astype(I32)
    for block in range(blocks):
        cut = slice(block * LANES, (block + 1) * LANES)
        order = order_ref[:, cut]
        low, high = order & (LANES - 1), order >> LANE_BITS
        picked = jnp.zeros((tiles, LANES), I32)
        for source in range(blocks):
            found = lanes(ids_ref[:, source * LANES : (source + 1) * LANES], low)
            picked = jnp.where(high == source, found, picked)
        owner = jnp.where(order < live, picked >> own_bits, -1)
        value = (picked & (own_count - 1)) + local_view * own_count
        for t in range(tiles):
            owner_ref[t, :, cut] = owner[t : t + 1, :]
            value_ref[t, :, cut] = value[t : t + 1, :]
    upto = (iota((slots, slots), 0) <= iota((slots, slots), 1)).astype(BF16)
    acc_ref[...] = jnp.zeros_like(acc_ref)
    peers = iota((devices, slots), 0)
    ranks = iota((LANES, slots), 0)

    def tile(t, before):
        owner, value = owner_ref[t], value_ref[t]
        named = peers == owner
        count = dot_nn(named.astype(BF16), upto)
        rank = jnp.sum(jnp.where(named, count + before, 0.0), axis=0, keepdims=True) - 1.0
        rank = rank.astype(I32)
        rank_ref[t] = rank
        at_rank = (ranks == rank).astype(BF16)
        parts = [(value & 255).astype(F32), (value >> 8).astype(F32)]
        left = jnp.concatenate([jnp.where(named, part, 0.0).astype(BF16) for part in parts], axis=0)
        acc_ref[...] += dot_nt(left, at_rank)
        return before + count[:, slots - 1 :]

    def some(n, before):
        for step in range(greets):
            ring.greet(n * greets + step + 1)
        for t in range(ROWS):
            before = tile(n * ROWS + t, before)
        return before

    rounds = tiles // ROWS
    greets = (devices - 1) // rounds
    for step in range(rounds * greets + 1, devices):
        ring.greet(step)
    lax.fori_loop(0, rounds, some, jnp.zeros((devices, 1), F32))
    low, high = acc_ref[0:devices, :].astype(I32), acc_ref[devices:, :].astype(I32)
    lane = iota((1, LANES), 1)
    told = jnp.zeros((1, LANES), I32)
    for n in range(here):
        total = jnp.sum(live[n * tiles_here : (n + 1) * tiles_here].astype(F32), axis=0, keepdims=True)
        told = jnp.where(lane == n, total.astype(I32), told)
    send_ref[:, 0, 0:LANES] = low + 256 * high
    send_ref[:, 0, LANES:] = spread(told, devices)

    pl.semaphore_wait(pltpu.get_barrier_semaphore(), devices - 1)
    own_request = pltpu.make_async_copy(send_ref.at[me], got_ref.at[me], local_sem.at[0])
    own_request.start()

    def request(device):
        return ring.copy(send_ref.at[device], got_ref.at[me], request_send, request_recv, device)

    each(1, devices, 16, lambda step: request(ring.after(step)).start())

    centres = [field_of(centres_ref, n) for n in range(3)]
    shape_raw = [field_of(shape_ref, n) for n in range(6)]
    for view in range(views):
        found = moving_fields(centres, shape_raw, camera_view(camera_ref, view))
        for k in range(MOVING):
            moving_ref[view // here, k, (view % here) * ROWS : (view % here + 1) * ROWS, :] = found[k]
    fixed_ref[0] = opacity_of(logit_ref[...])
    for n in range(3):
        fixed_ref[1 + n] = field_of(colours_ref, n)
    own_request.wait()
    steps = devices // ROWS
    per_group = steps // (views // here)

    def arrived(semaphores, target, device):
        pltpu.make_async_copy(target, target, semaphores.at[device]).wait()

    def answer(device):
        return ring.copy(answer_ref.at[:, device], recv_ref.at[:, me], answer_send, answer_recv, device)

    def block(n):
        turn = ((me >> 3) - n) & (steps - 1)
        row = pl.multiple_of(turn * ROWS, ROWS)
        group = turn // per_group
        for s in range(ROWS):

            @pl.when(row + s != me)
            def _(s=s):
                arrived(request_recv, got_ref.at[row + s], row + s)

        ids = got_ref[pl.ds(row, ROWS), 0, 0:LANES]
        low, high = ids & (LANES - 1), ids >> LANE_BITS
        high_fixed = high & (ROWS - 1)
        for k in range(FIELDS):
            moves = k < MOVING
            total = jnp.zeros((ROWS, LANES), F32)
            for h in range(ROWS * here if moves else ROWS):
                line = moving_ref[group, k, h : h + 1, :] if moves else fixed_ref[k - MOVING, h : h + 1, :]
                total = jnp.where((high if moves else high_fixed) == h, lanes(spread(line, ROWS), low), total)
            answer_ref[k, pl.ds(row, ROWS), 0, :] = total
        for s in range(ROWS):
            device = row + ((me + s) & (ROWS - 1))

            @pl.when(device != me)
            def _(device=device):
                answer(device).start()

    each(0, steps, 1, block)
    own_answer = pltpu.make_async_copy(answer_ref.at[:, me], recv_ref.at[:, me], local_sem.at[1])
    own_answer.start()

    own_answer.wait()

    def land(n):
        turn = ((me >> 3) + n) & (steps - 1)
        row = pl.multiple_of(turn * ROWS, ROWS)
        for s in range(ROWS):

            @pl.when(row + s != me)
            def _(s=s):
                arrived(answer_recv, recv_ref.at[:, row + s], row + s)

        for k in range(FIELDS):
            records_ref[k, pl.ds(row, ROWS), :] = recv_ref[k, pl.ds(row, ROWS), 0, :]

    each(0, steps, 1, land)

    def sent(step):
        device = ring.after(step)
        request(device).wait_send()
        answer(device).wait_send()

    return lambda: each(1, devices, 16, sent)


def field_of(ref, row):
    return jnp.concatenate([ref[row : row + 1, h * LANES : (h + 1) * LANES] for h in range(ROWS)], axis=0)


def moving_fields(centres, shape_raw, view):
    rows = [view[0:4], view[4:8]]
    e0, e2, e5 = jnp.exp(shape_raw[0]), jnp.exp(shape_raw[2]), jnp.exp(shape_raw[5])
    screen, factor = [], []
    for m in rows:
        screen.append(m[0] * centres[0] + m[1] * centres[1] + m[2] * centres[2] + m[3])
        factor.append(
            (
                m[0] * e0 + m[1] * shape_raw[1] + m[2] * shape_raw[3],
                m[1] * e2 + m[2] * shape_raw[4],
                m[2] * e5,
            )
        )
    fx, fy = factor
    var_x = fx[0] * fx[0] + fx[1] * fx[1] + fx[2] * fx[2] + 0.3
    cov_xy = fx[0] * fy[0] + fx[1] * fy[1] + fx[2] * fy[2]
    var_y = fy[0] * fy[0] + fy[1] * fy[1] + fy[2] * fy[2] + 0.3
    inverse = 1.0 / (var_x * var_y - cov_xy * cov_xy)
    return screen[0], screen[1], var_y * inverse, -cov_xy * inverse, var_x * inverse


def opacity_of(logit):
    return 0.95 / (1.0 + jnp.exp(-logit))


def camera_view(camera_ref, view):
    return [camera_ref[n // 4, n % 4, view] for n in range(8)]


def give(ring, views, here, got_ref, table_ref, given_ref, moving_ref, fixed_ref, send_sem, recv_sem, local_sem):
    me, devices = ring.me, ring.count
    groups = views // here
    moving_ref[...] = jnp.zeros_like(moving_ref)
    fixed_ref[...] = jnp.zeros_like(fixed_ref)
    wide = ROWS * here
    per_step = 2
    own = pltpu.make_async_copy(table_ref.at[:, me], given_ref.at[:, me], local_sem)
    own.start()

    def copy(device):
        return ring.copy(table_ref.at[:, device], given_ref.at[:, me], send_sem, recv_sem, device)

    each(1, devices, 16, lambda step: copy(ring.after(step)).start())
    own.wait()
    steps = devices // ROWS

    def block(n):
        turn = ((me >> 3) - n) & (steps - 1)
        row = pl.multiple_of(turn * ROWS, ROWS)
        group = turn // (steps // groups)
        for s in range(ROWS):

            @pl.when(row + s != me)
            def _(s=s):
                target = given_ref.at[:, row + s]
                pltpu.make_async_copy(target, target, recv_sem.at[row + s]).wait()

        ids = got_ref[pl.ds(row, ROWS), 0, 0:LANES]
        values = [given_ref[k, pl.ds(row, ROWS), 0, :] for k in range(FIELDS)]
        total = None
        for first in range(0, ROWS, per_step):
            lefts, onehots = [], []
            for src in range(first, first + per_step):
                low, high = ids[src : src + 1] & (LANES - 1), ids[src : src + 1] >> LANE_BITS
                at_wide = iota((wide, LANES), 0) == high
                at_row = iota((ROWS, LANES), 0) == (high & (ROWS - 1))
                rows = [
                    jnp.where(at_wide if k < MOVING else at_row, values[k][src : src + 1], 0.0)
                    for k in range(FIELDS)
                ]
                lefts.append(jnp.concatenate(rows, axis=0))
                onehots.append((iota((LANES, LANES), 0) == low).astype(BF16))
            left_high, left_low = halves(jnp.concatenate(lefts, axis=1))
            right = jnp.concatenate(onehots, axis=1)
            found = dot_nt(left_high, right) + dot_nt(left_low, right)
            total = found if total is None else total + found
        moving_ref[group] += total[: MOVING * wide]
        fixed_ref[...] += total[MOVING * wide :]

    each(0, steps, 1, block)
    each(1, devices, 16, lambda step: copy(ring.after(step)).wait_send())


def pull_kernel(
    views, here, centres_ref, shape_ref, logit_ref, camera_ref, moving_ref, fixed_ref, owners_ref,
    d_centres_ref, d_shape_ref, d_logit_ref, d_colours_ref, next_ref,
):
    wide = ROWS * here
    next_ref[...] = owners_ref[...]
    centres = [field_of(centres_ref, n) for n in range(3)]
    shape_raw = [field_of(shape_ref, n) for n in range(6)]
    d_centres = [jnp.zeros((ROWS, LANES), F32)] * 3
    d_shape = [jnp.zeros((ROWS, LANES), F32)] * 6
    for view in range(views):
        camera = camera_view(camera_ref, view)
        _, pull = jax.vjp(lambda c, s: moving_fields(c, s, camera), centres, shape_raw)
        base = (view % here) * ROWS
        given = tuple(
            moving_ref[view // here, k * wide + base : k * wide + base + ROWS, :] for k in range(MOVING)
        )
        more_centres, more_shape = pull(given)
        d_centres = [a + b for a, b in zip(d_centres, more_centres)]
        d_shape = [a + b for a, b in zip(d_shape, more_shape)]

    def put(ref, row, value):
        for h in range(ROWS):
            ref[row : row + 1, h * LANES : (h + 1) * LANES] = value[h : h + 1, :]

    for n in range(3):
        put(d_centres_ref, n, d_centres[n])
        put(d_colours_ref, n, fixed_ref[(1 + n) * ROWS : (2 + n) * ROWS, :])
    for n in range(6):
        put(d_shape_ref, n, d_shape[n])
    _, pull = jax.vjp(opacity_of, logit_ref[...])
    d_logit_ref[...] = pull(fixed_ref[0:ROWS, :])[0]


def next_owner(ring, got_ref, live_ref, next_ref):
    here, tiles_here = live_ref.shape
    counts = got_ref[:, 0, LANES:].astype(F32)
    source = iota((ring.count, LANES), 0)
    mine = source >> ring.bits == lax.axis_index("view")
    lower = mine & ((source & (ring.tiles - 1)) < lax.axis_index("tile"))
    own_lane = iota((here, LANES), 0) == iota((here, LANES), 1)

    def column(mask):
        row = jnp.sum(jnp.where(mask, counts, 0.0), axis=0, keepdims=True)
        return jnp.sum(jnp.where(own_lane, spread(row, here), 0.0), axis=1, keepdims=True)

    whole, before = column(mine), column(lower)
    earlier = (iota((tiles_here, tiles_here), 0) < iota((tiles_here, tiles_here), 1)).astype(BF16)
    start = before + dot_nn(live_ref[...].astype(F32).astype(BF16), earlier)
    above, below = (start * ring.tiles).astype(I32), whole.astype(I32)
    quotient = (start * ring.tiles / whole).astype(I32)
    rest = above - quotient * below
    next_ref[...] = quotient + (rest >= below).astype(I32) - (rest < 0).astype(I32)


def render(
    ring, recv_ref, owner_ref, rank_ref, target_ref, image_ref, table_ref,
    cov_ref, odds_ref, high_ref, low_ref, dots_ref, acc_ref,
):
    tiles, _, slots = owner_ref.shape
    devices = ring.count
    blocks = slots // LANES
    half = (SIDE - 1) / 2.0
    log2e = 1.4426950408889634
    before = (iota((slots, slots), 0) < iota((slots, slots), 1)).astype(BF16)
    after = (iota((slots, slots), 0) > iota((slots, slots), 1)).astype(BF16)
    across = iota((SIDE, slots), 0).astype(F32) - half
    sublane = iota((ROWS, LANES), 0)
    split = devices // 2
    peers, places = iota((split, slots), 0), iota((2 * LANES, slots), 0)

    def fetch(t, block):
        here = slice(block * LANES, (block + 1) * LANES)
        owner = spread(owner_ref[t, :, here], ROWS) - sublane
        rank = spread(jnp.maximum(rank_ref[t, :, here], 0), ROWS)
        total = [jnp.zeros((ROWS, LANES), F32)] * FIELDS
        for group in range(devices // ROWS):
            mine = owner == group * ROWS
            for k in range(FIELDS):
                table = recv_ref[k, group * ROWS : (group + 1) * ROWS, :]
                total[k] = jnp.where(mine, lanes(table, rank), total[k])
        return [jnp.sum(one, axis=0, keepdims=True) for one in total]

    def tile(t, lane):
        cov, odds, high_part, low_part, dots = (
            ref.at[lane] for ref in (cov_ref, odds_ref, high_ref, low_ref, dots_ref)
        )
        found = [fetch(t, block) for block in range(blocks)]
        u, w, a, b, c, opacity, red, green, blue = (
            jnp.concatenate([found[block][k] for block in range(blocks)], axis=1) for k in range(FIELDS)
        )
        yield
        aim = jnp.concatenate([target_ref[t], jnp.zeros((ROWS - 3, PIX), F32)], axis=0).T
        dx = across - u
        scale = -0.5 * log2e
        first = (scale * a) * dx * dx
        second = (2.0 * scale * b) * dx
        third = scale * c
        for y in range(SIDE):
            rows = slice(y * SIDE, (y + 1) * SIDE)
            dy = (y - half) - w
            cover = opacity * jnp.exp2((second + third * dy) * dy + first)
            cov[rows, :] = cover
            keep = jnp.log(1.0 - cover)
            odds[rows, :] = cover * jnp.exp(-keep)
            high, low = halves(keep)
            high_part[rows, :] = high
            low_part[rows, :] = low
        yield
        through = jnp.exp(dot_nn(high_part[...], before) + dot_nn(low_part[...], before))
        weights = through * cov[...]
        w_high, w_low = halves(weights)
        yield
        colour = jnp.concatenate([red, green, blue], axis=0)
        colour = jnp.concatenate([colour, jnp.zeros((ROWS - 3, slots), F32)], axis=0)
        c_high, c_low = halves(colour)
        drawn = (dot_nt(w_high, c_high) + dot_nt(w_low, c_high)) + (dot_nt(w_high, c_low) + dot_nt(w_low, c_low))
        column = drawn - aim
        image_ref[t] = drawn.T[0:3]
        yield
        d_colour = [jnp.sum(weights * column[:, n : n + 1], axis=0, keepdims=True) for n in range(3)]
        shade = column[:, 0:1] * red + column[:, 1:2] * green + column[:, 2:3] * blue
        shaded = weights * shade
        s_high, s_low = halves(shaded)
        yield
        behind = dot_nn(s_high, after) + dot_nn(s_low, after)
        dots[...] = shaded - behind * odds[...]
        yield
        sum0 = jnp.zeros((SIDE, slots), F32)
        sum1, sum2 = sum0, sum0
        for y in range(SIDE):
            given = dots[y * SIDE : (y + 1) * SIDE, :]
            dy = (y - half) - w
            once = given * dy
            sum0, sum1, sum2 = sum0 + given, sum1 + once, sum2 + once * dy

        def down(x):
            return jnp.sum(x, axis=0, keepdims=True)

        once = sum0 * dx
        s0, sx, sxx = down(sum0), down(once), down(once * dx)
        sy, sxy, syy = down(sum1), down(sum1 * dx), down(sum2)
        grads = [
            a * sx + b * sy,
            b * sx + c * sy,
            -0.5 * sxx,
            -sxy,
            -0.5 * syy,
            jnp.where(opacity > 0.0, s0 / opacity, 0.0),
            *d_colour,
        ]
        owner, rank = owner_ref[t], rank_ref[t]
        yield
        named = ((owner & (split - 1)) == peers).astype(BF16)
        place = (owner >> (split.bit_length() - 1)) * LANES + rank == places
        parts = [halves(grad) for grad in grads]
        left = [jnp.concatenate([named * part[n] for part in parts], axis=0) for n in range(2)]
        right = place.astype(BF16)
        acc_ref[...] += dot_nt(jnp.concatenate(left, axis=1), jnp.concatenate([right, right], axis=1))

    def together(n, carry):
        running = [tile(n * TOGETHER + lane, lane) for lane in range(TOGETHER)]
        while running:
            running = [one for one in running if next(one, one) is None]
        return carry

    acc_ref[...] = jnp.zeros_like(acc_ref)
    lax.fori_loop(0, tiles // TOGETHER, together, 0)
    for k in range(FIELDS):
        for n in range(2):
            table_ref[k, n * split : (n + 1) * split, 0, :] = acc_ref[
                k * split : (k + 1) * split, n * LANES : (n + 1) * LANES
            ]


def splat_kernel(
    sizes, views, ids_ref, order_ref, live_ref, centres_ref, shape_ref, logit_ref, colours_ref, camera_ref, target_ref,
    image_ref, moving_ref, fixed_ref, next_ref,
    records_ref, got_ref, owner_ref, rank_ref, value_ref, ask_acc_ref, send_ref, answer_ref, recv_ref,
    own_moving_ref, own_fixed_ref, cov_ref, odds_ref, high_ref, low_ref, dots_ref, acc_ref, table_ref, given_ref, aims_ref, drawn_ref,
    request_send, request_recv, answer_send, answer_recv, give_send, give_recv, local_sem,
):
    ring = Ring(*sizes)
    here, channels, tiles_here, _ = target_ref.shape
    places = [(v, c, t) for v in range(here) for c in range(channels) for t in range(tiles_here)]
    for v, c, t in places:
        aims_ref[v * tiles_here + t, c : c + 1, :] = target_ref[v, c, t : t + 1, :]
    sent = ask(
        ring, views, ids_ref, order_ref, live_ref, centres_ref, shape_ref, logit_ref, colours_ref, camera_ref,
        records_ref, got_ref, owner_ref, rank_ref,
        value_ref, ask_acc_ref, send_ref, answer_ref, recv_ref, own_moving_ref, own_fixed_ref,
        request_send, request_recv, answer_send, answer_recv, local_sem,
    )
    next_owner(ring, got_ref, live_ref, next_ref)
    render(
        ring, records_ref, owner_ref, rank_ref, aims_ref, drawn_ref, table_ref,
        cov_ref, odds_ref, high_ref, low_ref, dots_ref, acc_ref,
    )
    give(
        ring, views, live_ref.shape[0], got_ref, table_ref, given_ref, moving_ref, fixed_ref,
        give_send, give_recv, local_sem.at[2],
    )
    for v, c, t in places:
        image_ref[v, c, t : t + 1, :] = drawn_ref[v * tiles_here + t, c : c + 1, :]
    sent()


VMEM = pl.BlockSpec(memory_space=pltpu.VMEM)
SMEM = pl.BlockSpec(memory_space=pltpu.SMEM)


def params(number=None):
    limit = 40 * 2**20
    if number is None:
        return pltpu.CompilerParams(vmem_limit_bytes=limit)
    return pltpu.CompilerParams(vmem_limit_bytes=limit, collective_id=number, has_side_effects=True)


def shape(dims, kind=F32):
    return jax.ShapeDtypeStruct(dims, kind)


def dma(*dims):
    return pltpu.SemaphoreType.DMA(dims)


def splat(sizes, ids, order, live, centres, shape_raw, logit, colours, camera, target):
    tiles, slots = ids.shape
    devices, views, here = sizes[0] * sizes[1], camera.shape[2], live.shape[0]
    table = (FIELDS, devices, 1, LANES)
    line = (tiles, 1, slots)
    return pl.pallas_call(
        partial(splat_kernel, sizes, views),
        out_shape=(
            shape(target.shape),
            shape((views // here, MOVING * here * ROWS, LANES)),
            shape(((FIELDS - MOVING) * ROWS, LANES)),
            shape(live.shape, I32),
        ),
        in_specs=[VMEM] * 7 + [SMEM, VMEM],
        out_specs=(VMEM,) * 4,
        scratch_shapes=[
            pltpu.VMEM((FIELDS, devices, LANES), F32),
            pltpu.VMEM((devices, 1, 2 * LANES), I32),
            pltpu.VMEM(line, I32),
            pltpu.VMEM(line, I32),
            pltpu.VMEM(line, I32),
            pltpu.VMEM((2 * devices, LANES), F32),
            pltpu.VMEM((devices, 1, 2 * LANES), I32),
            pltpu.VMEM(table, F32),
            pltpu.VMEM(table, F32),
            pltpu.VMEM((views // here, MOVING, here * ROWS, LANES), F32),
            pltpu.VMEM((FIELDS - MOVING, ROWS, LANES), F32),
            pltpu.VMEM((TOGETHER, PIX, slots), F32),
            pltpu.VMEM((TOGETHER, PIX, slots), F32),
            pltpu.VMEM((TOGETHER, PIX, slots), BF16),
            pltpu.VMEM((TOGETHER, PIX, slots), BF16),
            pltpu.VMEM((TOGETHER, PIX, slots), F32),
            pltpu.VMEM((FIELDS * devices // 2, 2 * LANES), F32),
            pltpu.VMEM(table, F32),
            pltpu.VMEM(table, F32),
            pltpu.VMEM((tiles, 3, PIX), F32),
            pltpu.VMEM((tiles, 3, PIX), F32),
        ]
        + [dma(devices)] * 6
        + [dma(3)],
        compiler_params=params(0),
        name="splat",
    )(ids, order, live, centres, shape_raw, logit, colours, camera, target)


def pull(here, centres, shape_raw, logit, camera, moving, fixed, owners):
    return pl.pallas_call(
        partial(pull_kernel, camera.shape[2], here),
        out_shape=(
            shape(centres.shape),
            shape(shape_raw.shape),
            shape(logit.shape),
            shape(centres.shape),
            shape(owners.shape, I32),
        ),
        in_specs=[VMEM] * 3 + [SMEM] + [VMEM] * 3,
        out_specs=(VMEM,) * 5,
        compiler_params=params(),
        name="pull",
    )(centres, shape_raw, logit, camera, moving, fixed, owners)


def shards(centres, shape_raw, opacity_logit, colours, camera, target, intersection_ids, depth_order, live_count):
    sizes = (lax.axis_size("view"), lax.axis_size("tile"))
    here, tiles_here, slots = intersection_ids.shape
    tiles = here * tiles_here
    logit = opacity_logit.reshape(ROWS, LANES)
    image, moving, fixed, owners = splat(
        sizes,
        intersection_ids.reshape(tiles, slots),
        depth_order.reshape(tiles, slots),
        live_count,
        centres,
        shape_raw,
        logit,
        colours,
        camera.transpose(1, 2, 0),
        target.transpose(0, 2, 1, 3),
    )
    d_centres, d_shape, d_logit, d_colours, owners = pull(
        here, centres, shape_raw, logit, camera.transpose(1, 2, 0), moving, fixed, owners
    )
    return (
        image.transpose(0, 2, 1, 3),
        d_centres,
        d_shape,
        d_logit.reshape(opacity_logit.shape),
        d_colours,
        owners,
    )


def solution(mesh):
    in_specs = (
        P(None, ("view", "tile")),
        P(None, ("view", "tile")),
        P(("view", "tile")),
        P(None, ("view", "tile")),
        P(),
        P("view", "tile", None, None),
        P("view", "tile", None),
        P("view", "tile", None),
        P("view", "tile"),
    )
    out_specs = (
        P("view", "tile", None, None),
        P(None, ("view", "tile")),
        P(None, ("view", "tile")),
        P(("view", "tile")),
        P(None, ("view", "tile")),
        P("view", "tile"),
    )
    return jax.shard_map(shards, mesh=mesh, in_specs=in_specs, out_specs=out_specs, check_vma=False)
```

```python
from functools import partial

import jax
import jax.numpy as jnp
from jax import lax
from jax.experimental import pallas as pl
from jax.experimental.pallas import tpu as pltpu
from jax.sharding import PartitionSpec as P

SIDE = 16
PIX = SIDE * SIDE
LANES = 128
LANE_BITS = 7
ROWS = 8
FIELDS = 9
MOVING = 5
TOGETHER = 4
F32 = jnp.float32
BF16 = jnp.bfloat16
I32 = jnp.int32


def lanes(table, index):
    return jnp.take_along_axis(table, index, axis=1, mode="promise_in_bounds")


def iota(shape, axis):
    return lax.broadcasted_iota(I32, shape, axis)


def spread(row, count):
    return jnp.broadcast_to(row, (count, row.shape[1]))


def halves(array):
    high = array.astype(BF16)
    return high, (array - high.astype(F32)).astype(BF16)


def dot_nn(a, b):
    return lax.dot_general(a, b, (((1,), (0,)), ((), ())), preferred_element_type=F32)


def dot_nt(a, b):
    return lax.dot_general(a, b, (((1,), (1,)), ((), ())), preferred_element_type=F32)


def dot_tn(a, b):
    return lax.dot_general(a, b, (((0,), (0,)), ((), ())), preferred_element_type=F32)


MESH = pl.DeviceIdType.MESH


class Ring:
    def __init__(self, view_group, tile_group):
        self.bits = tile_group.bit_length() - 1
        self.tiles = tile_group
        self.count = view_group * tile_group
        self.me = lax.axis_index("view") * tile_group + lax.axis_index("tile")

    def place(self, device):
        return (device >> self.bits, device & (self.tiles - 1))

    def after(self, step):
        return (self.me + step) & (self.count - 1)

    def greet(self, step):
        pl.semaphore_signal(
            pltpu.get_barrier_semaphore(), inc=1, device_id=self.place(self.after(step)), device_id_type=MESH
        )

    def copy(self, source, target, send_sem, recv_sem, device):
        return pltpu.make_async_remote_copy(
            src_ref=source,
            dst_ref=target,
            send_sem=send_sem.at[device],
            recv_sem=recv_sem.at[self.me],
            device_id=self.place(device),
            device_id_type=MESH,
        )


def each(first, last, unroll, body):
    def step(n, carry):
        body(n)
        return carry

    lax.fori_loop(first, last, step, 0, unroll=unroll)


def ask(
    ring, views, ids_ref, order_ref, live_ref, centres_ref, shape_ref, logit_ref, colours_ref, camera_ref,
    records_ref, got_ref, owner_ref, rank_ref,
    value_ref, acc_ref, send_ref, answer_ref, recv_ref, moving_ref, fixed_ref,
    request_send, request_recv, answer_send, answer_recv, local_sem, loaded,
):
    me, devices = ring.me, ring.count
    tiles, slots = ids_ref.shape
    here, tiles_here = live_ref.shape
    own_count = centres_ref.shape[1]
    own_bits = own_count.bit_length() - 1
    blocks = slots // LANES
    turned = live_ref[...].astype(F32).T
    live = jnp.concatenate([turned[:, n : n + 1] for n in range(here)], axis=0).astype(I32)
    local_view = (iota((tiles, LANES), 0) >= tiles_here).astype(I32)
    for block in range(blocks):
        cut = slice(block * LANES, (block + 1) * LANES)
        order = order_ref[:, cut]
        low, high = order & (LANES - 1), order >> LANE_BITS
        picked = jnp.zeros((tiles, LANES), I32)
        for source in range(blocks):
            found = lanes(ids_ref[:, source * LANES : (source + 1) * LANES], low)
            picked = jnp.where(high == source, found, picked)
        owner = jnp.where(order < live, picked >> own_bits, -1)
        value = (picked & (own_count - 1)) + local_view * own_count
        for t in range(tiles):
            owner_ref[t, :, cut] = owner[t : t + 1, :]
            value_ref[t, :, cut] = value[t : t + 1, :]
    upto = (iota((slots, slots), 0) <= iota((slots, slots), 1)).astype(BF16)
    acc_ref[...] = jnp.zeros_like(acc_ref)
    peers = iota((devices, slots), 0)
    ranks = iota((LANES, slots), 0)

    def tile(t, before):
        owner, value = owner_ref[t], value_ref[t]
        named = peers == owner
        count = dot_nn(named.astype(BF16), upto)
        rank = jnp.sum(jnp.where(named, count + before, 0.0), axis=0, keepdims=True) - 1.0
        rank = rank.astype(I32)
        rank_ref[t] = rank
        at_rank = (ranks == rank).astype(BF16)
        parts = [(value & 255).astype(F32), (value >> 8).astype(F32)]
        left = jnp.concatenate([jnp.where(named, part, 0.0).astype(BF16) for part in parts], axis=0)
        acc_ref[...] += dot_nt(left, at_rank)
        return before + count[:, slots - 1 :]

    def some(n, before):
        for step in range(greets):
            ring.greet(n * greets + step + 1)
        for t in range(ROWS):
            before = tile(n * ROWS + t, before)
        return before

    rounds = tiles // ROWS
    greets = (devices - 1) // rounds
    for step in range(rounds * greets + 1, devices):
        ring.greet(step)
    lax.fori_loop(0, rounds, some, jnp.zeros((devices, 1), F32))
    low, high = acc_ref[0:devices, :].astype(I32), acc_ref[devices:, :].astype(I32)
    lane = iota((1, LANES), 1)
    told = jnp.zeros((1, LANES), I32)
    for n in range(here):
        total = jnp.sum(live[n * tiles_here : (n + 1) * tiles_here].astype(F32), axis=0, keepdims=True)
        told = jnp.where(lane == n, total.astype(I32), told)
    send_ref[:, 0, 0:LANES] = low + 256 * high
    send_ref[:, 0, LANES:] = spread(told, devices)

    pl.semaphore_wait(pltpu.get_barrier_semaphore(), devices - 1)
    own_request = pltpu.make_async_copy(send_ref.at[me], got_ref.at[me], local_sem.at[0])
    own_request.start()

    def request(device):
        return ring.copy(send_ref.at[device], got_ref.at[me], request_send, request_recv, device)

    each(1, devices, 16, lambda step: request(ring.after(step)).start())

    loaded()
    centres = [field_of(centres_ref, n) for n in range(3)]
    shape_raw = [field_of(shape_ref, n) for n in range(6)]
    for view in range(views):
        found = moving_fields(centres, shape_raw, camera_view(camera_ref, view))
        for k in range(MOVING):
            moving_ref[view // here, k, (view % here) * ROWS : (view % here + 1) * ROWS, :] = found[k]
    fixed_ref[0] = opacity_of(logit_ref[...])
    for n in range(3):
        fixed_ref[1 + n] = field_of(colours_ref, n)
    own_request.wait()
    steps = devices // ROWS
    per_group = steps // (views // here)

    def arrived(semaphores, target, device):
        pltpu.make_async_copy(target, target, semaphores.at[device]).wait()

    def answer(device):
        return ring.copy(answer_ref.at[:, device], recv_ref.at[:, me], answer_send, answer_recv, device)

    def block(n):
        turn = ((me >> 3) - n) & (steps - 1)
        row = pl.multiple_of(turn * ROWS, ROWS)
        group = turn // per_group
        for s in range(ROWS):

            @pl.when(row + s != me)
            def _(s=s):
                arrived(request_recv, got_ref.at[row + s], row + s)

        ids = got_ref[pl.ds(row, ROWS), 0, 0:LANES]
        low, high = ids & (LANES - 1), ids >> LANE_BITS
        high_fixed = high & (ROWS - 1)
        for k in range(FIELDS):
            moves = k < MOVING
            total = jnp.zeros((ROWS, LANES), F32)
            for h in range(ROWS * here if moves else ROWS):
                line = moving_ref[group, k, h : h + 1, :] if moves else fixed_ref[k - MOVING, h : h + 1, :]
                total = jnp.where((high if moves else high_fixed) == h, lanes(spread(line, ROWS), low), total)
            answer_ref[k, pl.ds(row, ROWS), 0, :] = total
        for s in range(ROWS):
            device = row + ((me + s) & (ROWS - 1))

            @pl.when(device != me)
            def _(device=device):
                answer(device).start()

    each(0, steps, 1, block)
    own_answer = pltpu.make_async_copy(answer_ref.at[:, me], recv_ref.at[:, me], local_sem.at[1])
    own_answer.start()

    own_answer.wait()

    def land(n):
        turn = ((me >> 3) + n) & (steps - 1)
        row = pl.multiple_of(turn * ROWS, ROWS)
        for s in range(ROWS):

            @pl.when(row + s != me)
            def _(s=s):
                arrived(answer_recv, recv_ref.at[:, row + s], row + s)

        for k in range(FIELDS):
            records_ref[k, pl.ds(row, ROWS), :] = recv_ref[k, pl.ds(row, ROWS), 0, :]

    each(0, steps, 1, land)

    def sent(step):
        device = ring.after(step)
        request(device).wait_send()
        answer(device).wait_send()

    return lambda: each(1, devices, 16, sent)


def field_of(ref, row):
    return jnp.concatenate([ref[row : row + 1, h * LANES : (h + 1) * LANES] for h in range(ROWS)], axis=0)


def moving_fields(centres, shape_raw, view):
    rows = [view[0:4], view[4:8]]
    e0, e2, e5 = jnp.exp(shape_raw[0]), jnp.exp(shape_raw[2]), jnp.exp(shape_raw[5])
    screen, factor = [], []
    for m in rows:
        screen.append(m[0] * centres[0] + m[1] * centres[1] + m[2] * centres[2] + m[3])
        factor.append(
            (
                m[0] * e0 + m[1] * shape_raw[1] + m[2] * shape_raw[3],
                m[1] * e2 + m[2] * shape_raw[4],
                m[2] * e5,
            )
        )
    fx, fy = factor
    var_x = fx[0] * fx[0] + fx[1] * fx[1] + fx[2] * fx[2] + 0.3
    cov_xy = fx[0] * fy[0] + fx[1] * fy[1] + fx[2] * fy[2]
    var_y = fy[0] * fy[0] + fy[1] * fy[1] + fy[2] * fy[2] + 0.3
    inverse = 1.0 / (var_x * var_y - cov_xy * cov_xy)
    return screen[0], screen[1], var_y * inverse, -cov_xy * inverse, var_x * inverse


def opacity_of(logit):
    return 0.95 / (1.0 + jnp.exp(-logit))


def camera_view(camera_ref, view):
    return [camera_ref[n // 4, n % 4, view] for n in range(8)]


def give(ring, views, here, got_ref, table_ref, given_ref, moving_ref, fixed_ref, send_sem, recv_sem, local_sem):
    me, devices = ring.me, ring.count
    groups = views // here
    moving_ref[...] = jnp.zeros_like(moving_ref)
    fixed_ref[...] = jnp.zeros_like(fixed_ref)
    wide = ROWS * here
    per_step = 2
    own = pltpu.make_async_copy(table_ref.at[:, me], given_ref.at[:, me], local_sem)
    own.start()

    def copy(device):
        return ring.copy(table_ref.at[:, device], given_ref.at[:, me], send_sem, recv_sem, device)

    each(1, devices, 16, lambda step: copy(ring.after(step)).start())
    own.wait()
    steps = devices // ROWS

    def block(n):
        turn = ((me >> 3) - n) & (steps - 1)
        row = pl.multiple_of(turn * ROWS, ROWS)
        group = turn // (steps // groups)
        for s in range(ROWS):

            @pl.when(row + s != me)
            def _(s=s):
                target = given_ref.at[:, row + s]
                pltpu.make_async_copy(target, target, recv_sem.at[row + s]).wait()

        ids = got_ref[pl.ds(row, ROWS), 0, 0:LANES]
        values = [given_ref[k, pl.ds(row, ROWS), 0, :] for k in range(FIELDS)]
        total = None
        for first in range(0, ROWS, per_step):
            lefts, onehots = [], []
            for src in range(first, first + per_step):
                low, high = ids[src : src + 1] & (LANES - 1), ids[src : src + 1] >> LANE_BITS
                at_wide = iota((wide, LANES), 0) == high
                at_row = iota((ROWS, LANES), 0) == (high & (ROWS - 1))
                rows = [
                    jnp.where(at_wide if k < MOVING else at_row, values[k][src : src + 1], 0.0)
                    for k in range(FIELDS)
                ]
                lefts.append(jnp.concatenate(rows, axis=0))
                onehots.append((iota((LANES, LANES), 0) == low).astype(BF16))
            left_high, left_low = halves(jnp.concatenate(lefts, axis=1))
            right = jnp.concatenate(onehots, axis=1)
            found = dot_nt(left_high, right) + dot_nt(left_low, right)
            total = found if total is None else total + found
        moving_ref[group] += total[: MOVING * wide]
        fixed_ref[...] += total[MOVING * wide :]

    each(0, steps, 1, block)
    each(1, devices, 16, lambda step: copy(ring.after(step)).wait_send())


def pull_kernel(
    views, here, centres_ref, shape_ref, logit_ref, camera_ref, moving_ref, fixed_ref, owners_ref, drawn_ref,
    d_centres_ref, d_shape_ref, d_logit_ref, d_colours_ref, next_ref, image_ref,
):
    wide = ROWS * here
    next_ref[...] = owners_ref[...]
    image_ref[...] = drawn_ref[...]
    centres = [field_of(centres_ref, n) for n in range(3)]
    shape_raw = [field_of(shape_ref, n) for n in range(6)]
    d_centres = [jnp.zeros((ROWS, LANES), F32)] * 3
    d_shape = [jnp.zeros((ROWS, LANES), F32)] * 6
    for view in range(views):
        camera = camera_view(camera_ref, view)
        _, pull = jax.vjp(lambda c, s: moving_fields(c, s, camera), centres, shape_raw)
        base = (view % here) * ROWS
        given = tuple(
            moving_ref[view // here, k * wide + base : k * wide + base + ROWS, :] for k in range(MOVING)
        )
        more_centres, more_shape = pull(given)
        d_centres = [a + b for a, b in zip(d_centres, more_centres)]
        d_shape = [a + b for a, b in zip(d_shape, more_shape)]

    def put(ref, row, value):
        for h in range(ROWS):
            ref[row : row + 1, h * LANES : (h + 1) * LANES] = value[h : h + 1, :]

    for n in range(3):
        put(d_centres_ref, n, d_centres[n])
        put(d_colours_ref, n, fixed_ref[(1 + n) * ROWS : (2 + n) * ROWS, :])
    for n in range(6):
        put(d_shape_ref, n, d_shape[n])
    _, pull = jax.vjp(opacity_of, logit_ref[...])
    d_logit_ref[...] = pull(fixed_ref[0:ROWS, :])[0]


def next_owner(ring, got_ref, live_ref, next_ref):
    here, tiles_here = live_ref.shape
    counts = got_ref[:, 0, LANES:].astype(F32)
    source = iota((ring.count, LANES), 0)
    mine = source >> ring.bits == lax.axis_index("view")
    lower = mine & ((source & (ring.tiles - 1)) < lax.axis_index("tile"))
    own_lane = iota((here, LANES), 0) == iota((here, LANES), 1)

    def column(mask):
        row = jnp.sum(jnp.where(mask, counts, 0.0), axis=0, keepdims=True)
        return jnp.sum(jnp.where(own_lane, spread(row, here), 0.0), axis=1, keepdims=True)

    whole, before = column(mine), column(lower)
    earlier = (iota((tiles_here, tiles_here), 0) < iota((tiles_here, tiles_here), 1)).astype(BF16)
    start = before + dot_nn(live_ref[...].astype(F32).astype(BF16), earlier)
    above, below = (start * ring.tiles).astype(I32), whole.astype(I32)
    quotient = (start * ring.tiles / whole).astype(I32)
    rest = above - quotient * below
    next_ref[...] = quotient + (rest >= below).astype(I32) - (rest < 0).astype(I32)


def render(
    ring, recv_ref, owner_ref, rank_ref, target_ref, image_ref, table_ref,
    cov_ref, odds_ref, high_ref, low_ref, dots_ref, acc_ref,
):
    tiles, _, slots = owner_ref.shape
    devices = ring.count
    blocks = slots // LANES
    half = (SIDE - 1) / 2.0
    log2e = 1.4426950408889634
    before = (iota((slots, slots), 0) < iota((slots, slots), 1)).astype(BF16)
    after = (iota((slots, slots), 0) > iota((slots, slots), 1)).astype(BF16)
    across = iota((SIDE, slots), 0).astype(F32) - half
    sublane = iota((ROWS, LANES), 0)
    split = devices // 2
    peers, places = iota((split, slots), 0), iota((2 * LANES, slots), 0)

    def fetch(t, block):
        here = slice(block * LANES, (block + 1) * LANES)
        owner = spread(owner_ref[t, :, here], ROWS) - sublane
        rank = spread(jnp.maximum(rank_ref[t, :, here], 0), ROWS)
        total = [jnp.zeros((ROWS, LANES), F32)] * FIELDS
        for group in range(devices // ROWS):
            mine = owner == group * ROWS
            for k in range(FIELDS):
                table = recv_ref[k, group * ROWS : (group + 1) * ROWS, :]
                total[k] = jnp.where(mine, lanes(table, rank), total[k])
        return [jnp.sum(one, axis=0, keepdims=True) for one in total]

    def tile(t, lane):
        cov, odds, high_part, low_part, dots = (
            ref.at[lane] for ref in (cov_ref, odds_ref, high_ref, low_ref, dots_ref)
        )
        found = [fetch(t, block) for block in range(blocks)]
        u, w, a, b, c, opacity, red, green, blue = (
            jnp.concatenate([found[block][k] for block in range(blocks)], axis=1) for k in range(FIELDS)
        )
        yield
        aim = jnp.concatenate([target_ref[t], jnp.zeros((ROWS - 3, PIX), F32)], axis=0).T
        dx = across - u
        scale = -0.5 * log2e
        first = (scale * a) * dx * dx
        second = (2.0 * scale * b) * dx
        third = scale * c
        for y in range(SIDE):
            rows = slice(y * SIDE, (y + 1) * SIDE)
            dy = (y - half) - w
            cover = opacity * jnp.exp2((second + third * dy) * dy + first)
            cov[rows, :] = cover
            keep = jnp.log(1.0 - cover)
            odds[rows, :] = cover * jnp.exp(-keep)
            high, low = halves(keep)
            high_part[rows, :] = high
            low_part[rows, :] = low
        yield
        through = jnp.exp(dot_nn(high_part[...], before) + dot_nn(low_part[...], before))
        weights = through * cov[...]
        w_high, w_low = halves(weights)
        yield
        colour = jnp.concatenate([red, green, blue], axis=0)
        colour = jnp.concatenate([colour, jnp.zeros((ROWS - 3, slots), F32)], axis=0)
        c_high, c_low = halves(colour)
        drawn = (dot_nt(w_high, c_high) + dot_nt(w_low, c_high)) + (dot_nt(w_high, c_low) + dot_nt(w_low, c_low))
        column = drawn - aim
        image_ref[t] = drawn.T[0:3]
        yield
        d_colour = [jnp.sum(weights * column[:, n : n + 1], axis=0, keepdims=True) for n in range(3)]
        shade = column[:, 0:1] * red + column[:, 1:2] * green + column[:, 2:3] * blue
        shaded = weights * shade
        s_high, s_low = halves(shaded)
        yield
        behind = dot_nn(s_high, after) + dot_nn(s_low, after)
        dots[...] = shaded - behind * odds[...]
        yield
        sum0 = jnp.zeros((SIDE, slots), F32)
        sum1, sum2 = sum0, sum0
        for y in range(SIDE):
            given = dots[y * SIDE : (y + 1) * SIDE, :]
            dy = (y - half) - w
            once = given * dy
            sum0, sum1, sum2 = sum0 + given, sum1 + once, sum2 + once * dy

        def down(x):
            return jnp.sum(x, axis=0, keepdims=True)

        once = sum0 * dx
        s0, sx, sxx = down(sum0), down(once), down(once * dx)
        sy, sxy, syy = down(sum1), down(sum1 * dx), down(sum2)
        grads = [
            a * sx + b * sy,
            b * sx + c * sy,
            -0.5 * sxx,
            -sxy,
            -0.5 * syy,
            jnp.where(opacity > 0.0, s0 / opacity, 0.0),
            *d_colour,
        ]
        owner, rank = owner_ref[t], rank_ref[t]
        yield
        named = ((owner & (split - 1)) == peers).astype(BF16)
        place = (owner >> (split.bit_length() - 1)) * LANES + rank == places
        parts = [halves(grad) for grad in grads]
        left = [jnp.concatenate([named * part[n] for part in parts], axis=0) for n in range(2)]
        right = place.astype(BF16)
        acc_ref[...] += dot_nt(jnp.concatenate(left, axis=1), jnp.concatenate([right, right], axis=1))

    def together(n, carry):
        running = [tile(n * TOGETHER + lane, lane) for lane in range(TOGETHER)]
        while running:
            running = [one for one in running if next(one, one) is None]
        return carry

    acc_ref[...] = jnp.zeros_like(acc_ref)
    lax.fori_loop(0, tiles // TOGETHER, together, 0)
    for k in range(FIELDS):
        for n in range(2):
            table_ref[k, n * split : (n + 1) * split, 0, :] = acc_ref[
                k * split : (k + 1) * split, n * LANES : (n + 1) * LANES
            ]


def splat_kernel(
    sizes, views, *refs
):
    given, rest = refs[:8], refs[8:]
    held, rest, load_sem = rest[-9:-1], rest[:-9], rest[-1]
    loads = [pltpu.make_async_copy(a, b, load_sem.at[n]) for n, (a, b) in enumerate(zip(given, held))]
    for load in loads:
        load.start()
    splat(sizes, views, loads, *held, *rest)


def splat(
    sizes, views, loads, ids_ref, order_ref, live_ref, centres_ref, shape_ref, logit_ref, colours_ref, target_ref, camera_ref,
    image_ref, moving_ref, fixed_ref, next_ref,
    records_ref, got_ref, owner_ref, rank_ref, value_ref, ask_acc_ref, send_ref, answer_ref, recv_ref,
    own_moving_ref, own_fixed_ref, cov_ref, odds_ref, high_ref, low_ref, dots_ref, acc_ref, table_ref, given_ref, aims_ref, drawn_ref,
    request_send, request_recv, answer_send, answer_recv, give_send, give_recv, local_sem,
):
    ring = Ring(*sizes)
    here, channels, tiles_here, _ = target_ref.shape
    places = [(v, c, t) for v in range(here) for c in range(channels) for t in range(tiles_here)]

    def loaded():
        for load in loads[3:]:
            load.wait()
        for v, c, t in places:
            aims_ref[v * tiles_here + t, c : c + 1, :] = target_ref[v, c, t : t + 1, :]

    for load in loads[:3]:
        load.wait()
    sent = ask(
        ring, views, ids_ref, order_ref, live_ref, centres_ref, shape_ref, logit_ref, colours_ref, camera_ref,
        records_ref, got_ref, owner_ref, rank_ref,
        value_ref, ask_acc_ref, send_ref, answer_ref, recv_ref, own_moving_ref, own_fixed_ref,
        request_send, request_recv, answer_send, answer_recv, local_sem, loaded,
    )
    next_owner(ring, got_ref, live_ref, next_ref)
    render(
        ring, records_ref, owner_ref, rank_ref, aims_ref, drawn_ref, table_ref,
        cov_ref, odds_ref, high_ref, low_ref, dots_ref, acc_ref,
    )
    give(
        ring, views, live_ref.shape[0], got_ref, table_ref, given_ref, moving_ref, fixed_ref,
        give_send, give_recv, local_sem.at[2],
    )
    for v, c, t in places:
        image_ref[v, c, t : t + 1, :] = drawn_ref[v * tiles_here + t, c : c + 1, :]
    sent()


VMEM = pl.BlockSpec(memory_space=pltpu.VMEM)
HBM = pl.BlockSpec(memory_space=pltpu.HBM)
SMEM = pl.BlockSpec(memory_space=pltpu.SMEM)


def params(number=None):
    limit = 60 * 2**20
    if number is None:
        return pltpu.CompilerParams(vmem_limit_bytes=limit)
    return pltpu.CompilerParams(vmem_limit_bytes=limit, collective_id=number, has_side_effects=True)


def shape(dims, kind=F32):
    return jax.ShapeDtypeStruct(dims, kind)


def dma(*dims):
    return pltpu.SemaphoreType.DMA(dims)


def splats(sizes, ids, order, live, centres, shape_raw, logit, colours, camera, target):
    tiles, slots = ids.shape
    devices, views, here = sizes[0] * sizes[1], camera.shape[2], live.shape[0]
    inputs = (ids, order, live, centres, shape_raw, logit, colours, target)
    table = (FIELDS, devices, 1, LANES)
    line = (tiles, 1, slots)
    return pl.pallas_call(
        partial(splat_kernel, sizes, views),
        out_shape=(
            shape(target.shape),
            shape((views // here, MOVING * here * ROWS, LANES)),
            shape(((FIELDS - MOVING) * ROWS, LANES)),
            shape(live.shape, I32),
        ),
        in_specs=[HBM] * 8 + [SMEM],
        out_specs=(VMEM,) * 4,
        scratch_shapes=[
            pltpu.VMEM((FIELDS, devices, LANES), F32),
            pltpu.VMEM((devices, 1, 2 * LANES), I32),
            pltpu.VMEM(line, I32),
            pltpu.VMEM(line, I32),
            pltpu.VMEM(line, I32),
            pltpu.VMEM((2 * devices, LANES), F32),
            pltpu.VMEM((devices, 1, 2 * LANES), I32),
            pltpu.VMEM(table, F32),
            pltpu.VMEM(table, F32),
            pltpu.VMEM((views // here, MOVING, here * ROWS, LANES), F32),
            pltpu.VMEM((FIELDS - MOVING, ROWS, LANES), F32),
            pltpu.VMEM((TOGETHER, PIX, slots), F32),
            pltpu.VMEM((TOGETHER, PIX, slots), F32),
            pltpu.VMEM((TOGETHER, PIX, slots), BF16),
            pltpu.VMEM((TOGETHER, PIX, slots), BF16),
            pltpu.VMEM((TOGETHER, PIX, slots), F32),
            pltpu.VMEM((FIELDS * devices // 2, 2 * LANES), F32),
            pltpu.VMEM(table, F32),
            pltpu.VMEM(table, F32),
            pltpu.VMEM((tiles, 3, PIX), F32),
            pltpu.VMEM((tiles, 3, PIX), F32),
        ]
        + [dma(devices)] * 6
        + [dma(3)]
        + [pltpu.VMEM(one.shape, one.dtype) for one in inputs]
        + [dma(len(inputs))],
        compiler_params=params(0),
        name="splat",
    )(*inputs, camera)


def pull(here, centres, shape_raw, logit, camera, moving, fixed, owners, image):
    return pl.pallas_call(
        partial(pull_kernel, camera.shape[2], here),
        out_shape=(
            shape(centres.shape),
            shape(shape_raw.shape),
            shape(logit.shape),
            shape(centres.shape),
            shape(owners.shape, I32),
            shape(image.shape),
        ),
        in_specs=[VMEM] * 3 + [SMEM] + [VMEM] * 4,
        out_specs=(VMEM,) * 6,
        compiler_params=params(),
        name="pull",
    )(centres, shape_raw, logit, camera, moving, fixed, owners, image)


def shards(centres, shape_raw, opacity_logit, colours, camera, target, intersection_ids, depth_order, live_count):
    sizes = (lax.axis_size("view"), lax.axis_size("tile"))
    here, tiles_here, slots = intersection_ids.shape
    tiles = here * tiles_here
    logit = opacity_logit.reshape(ROWS, LANES)
    image, moving, fixed, owners = splats(
        sizes,
        intersection_ids.reshape(tiles, slots),
        depth_order.reshape(tiles, slots),
        live_count,
        centres,
        shape_raw,
        logit,
        colours,
        camera.transpose(1, 2, 0),
        target.transpose(0, 2, 1, 3),
    )
    d_centres, d_shape, d_logit, d_colours, owners, image = pull(
        here, centres, shape_raw, logit, camera.transpose(1, 2, 0), moving, fixed, owners, image
    )
    return (
        image.transpose(0, 2, 1, 3),
        d_centres,
        d_shape,
        d_logit.reshape(opacity_logit.shape),
        d_colours,
        owners,
    )


def solution(mesh):
    in_specs = (
        P(None, ("view", "tile")),
        P(None, ("view", "tile")),
        P(("view", "tile")),
        P(None, ("view", "tile")),
        P(),
        P("view", "tile", None, None),
        P("view", "tile", None),
        P("view", "tile", None),
        P("view", "tile"),
    )
    out_specs = (
        P("view", "tile", None, None),
        P(None, ("view", "tile")),
        P(None, ("view", "tile")),
        P(("view", "tile")),
        P(None, ("view", "tile")),
        P("view", "tile"),
    )
    return jax.shard_map(shards, mesh=mesh, in_specs=in_specs, out_specs=out_specs, check_vma=False)
```

```python
from functools import partial

import jax
import jax.numpy as jnp
from jax import lax
from jax.experimental import pallas as pl
from jax.experimental.pallas import tpu as pltpu
from jax.sharding import PartitionSpec as P

SIDE = 16
PIX = SIDE * SIDE
LANES = 128
LANE_BITS = 7
ROWS = 8
FIELDS = 9
MOVING = 5
TOGETHER = 8
F32 = jnp.float32
BF16 = jnp.bfloat16
I32 = jnp.int32


def lanes(table, index):
    return jnp.take_along_axis(table, index, axis=1, mode="promise_in_bounds")


def iota(shape, axis):
    return lax.broadcasted_iota(I32, shape, axis)


def spread(row, count):
    return jnp.broadcast_to(row, (count, row.shape[1]))


def halves(array):
    high = array.astype(BF16)
    return high, (array - high.astype(F32)).astype(BF16)


def dot_nn(a, b):
    return lax.dot_general(a, b, (((1,), (0,)), ((), ())), preferred_element_type=F32)


def dot_nt(a, b):
    return lax.dot_general(a, b, (((1,), (1,)), ((), ())), preferred_element_type=F32)


def dot_tn(a, b):
    return lax.dot_general(a, b, (((0,), (0,)), ((), ())), preferred_element_type=F32)


MESH = pl.DeviceIdType.MESH


class Ring:
    def __init__(self, view_group, tile_group):
        self.bits = tile_group.bit_length() - 1
        self.tiles = tile_group
        self.count = view_group * tile_group
        self.me = lax.axis_index("view") * tile_group + lax.axis_index("tile")

    def place(self, device):
        return (device >> self.bits, device & (self.tiles - 1))

    def after(self, step):
        return (self.me + step) & (self.count - 1)

    def greet(self, step):
        pl.semaphore_signal(
            pltpu.get_barrier_semaphore(), inc=1, device_id=self.place(self.after(step)), device_id_type=MESH
        )

    def copy(self, source, target, send_sem, recv_sem, device):
        return pltpu.make_async_remote_copy(
            src_ref=source,
            dst_ref=target,
            send_sem=send_sem.at[device],
            recv_sem=recv_sem.at[self.me],
            device_id=self.place(device),
            device_id_type=MESH,
        )


def each(first, last, unroll, body):
    def step(n, carry):
        body(n)
        return carry

    lax.fori_loop(first, last, step, 0, unroll=unroll)


def ask(
    ring, views, ids_ref, order_ref, live_ref, centres_ref, shape_ref, logit_ref, colours_ref, camera_ref,
    records_ref, got_ref, owner_ref, rank_ref,
    value_ref, acc_ref, send_ref, answer_ref, recv_ref, moving_ref, fixed_ref,
    request_send, request_recv, answer_send, answer_recv, local_sem, loaded,
):
    me, devices = ring.me, ring.count
    tiles, slots = ids_ref.shape
    here, tiles_here = live_ref.shape
    own_count = centres_ref.shape[1]
    own_bits = own_count.bit_length() - 1
    blocks = slots // LANES
    turned = live_ref[...].astype(F32).T
    live = jnp.concatenate([turned[:, n : n + 1] for n in range(here)], axis=0).astype(I32)
    local_view = (iota((tiles, LANES), 0) >= tiles_here).astype(I32)
    for block in range(blocks):
        cut = slice(block * LANES, (block + 1) * LANES)
        order = order_ref[:, cut]
        low, high = order & (LANES - 1), order >> LANE_BITS
        picked = jnp.zeros((tiles, LANES), I32)
        for source in range(blocks):
            found = lanes(ids_ref[:, source * LANES : (source + 1) * LANES], low)
            picked = jnp.where(high == source, found, picked)
        owner = jnp.where(order < live, picked >> own_bits, -1)
        value = (picked & (own_count - 1)) + local_view * own_count
        for t in range(tiles):
            owner_ref[t, :, cut] = owner[t : t + 1, :]
            value_ref[t, :, cut] = value[t : t + 1, :]
    upto = (iota((slots, slots), 0) <= iota((slots, slots), 1)).astype(BF16)
    acc_ref[...] = jnp.zeros_like(acc_ref)
    peers = iota((devices, slots), 0)
    ranks = iota((LANES, slots), 0)

    def tile(t, before):
        owner, value = owner_ref[t], value_ref[t]
        named = peers == owner
        count = dot_nn(named.astype(BF16), upto)
        rank = jnp.sum(jnp.where(named, count + before, 0.0), axis=0, keepdims=True) - 1.0
        rank = rank.astype(I32)
        rank_ref[t] = rank
        at_rank = (ranks == rank).astype(BF16)
        parts = [(value & 255).astype(F32), (value >> 8).astype(F32)]
        left = jnp.concatenate([jnp.where(named, part, 0.0).astype(BF16) for part in parts], axis=0)
        acc_ref[...] += dot_nt(left, at_rank)
        return before + count[:, slots - 1 :]

    def some(n, before):
        for step in range(greets):
            ring.greet(n * greets + step + 1)
        for t in range(ROWS):
            before = tile(n * ROWS + t, before)
        return before

    rounds = tiles // ROWS
    greets = (devices - 1) // rounds
    for step in range(rounds * greets + 1, devices):
        ring.greet(step)
    lax.fori_loop(0, rounds, some, jnp.zeros((devices, 1), F32))
    low, high = acc_ref[0:devices, :].astype(I32), acc_ref[devices:, :].astype(I32)
    lane = iota((1, LANES), 1)
    told = jnp.zeros((1, LANES), I32)
    for n in range(here):
        total = jnp.sum(live[n * tiles_here : (n + 1) * tiles_here].astype(F32), axis=0, keepdims=True)
        told = jnp.where(lane == n, total.astype(I32), told)
    send_ref[:, 0, 0:LANES] = low + 256 * high
    send_ref[:, 0, LANES:] = spread(told, devices)

    pl.semaphore_wait(pltpu.get_barrier_semaphore(), devices - 1)
    own_request = pltpu.make_async_copy(send_ref.at[me], got_ref.at[me], local_sem.at[0])
    own_request.start()

    def request(device):
        return ring.copy(send_ref.at[device], got_ref.at[me], request_send, request_recv, device)

    each(1, devices, 16, lambda step: request(ring.after(step)).start())

    loaded()
    centres = [field_of(centres_ref, n) for n in range(3)]
    shape_raw = [field_of(shape_ref, n) for n in range(6)]
    for view in range(views):
        found = moving_fields(centres, shape_raw, camera_view(camera_ref, view))
        for k in range(MOVING):
            moving_ref[view // here, k, (view % here) * ROWS : (view % here + 1) * ROWS, :] = found[k]
    fixed_ref[0] = opacity_of(logit_ref[...])
    for n in range(3):
        fixed_ref[1 + n] = field_of(colours_ref, n)
    own_request.wait()
    steps = devices // ROWS
    per_group = steps // (views // here)

    def arrived(semaphores, target, device):
        pltpu.make_async_copy(target, target, semaphores.at[device]).wait()

    def answer(device):
        return ring.copy(answer_ref.at[:, device], recv_ref.at[:, me], answer_send, answer_recv, device)

    def block(n):
        turn = ((me >> 3) - n) & (steps - 1)
        row = pl.multiple_of(turn * ROWS, ROWS)
        group = turn // per_group
        for s in range(ROWS):

            @pl.when(row + s != me)
            def _(s=s):
                arrived(request_recv, got_ref.at[row + s], row + s)

        ids = got_ref[pl.ds(row, ROWS), 0, 0:LANES]
        low, high = ids & (LANES - 1), ids >> LANE_BITS
        high_fixed = high & (ROWS - 1)
        for k in range(FIELDS):
            moves = k < MOVING
            total = jnp.zeros((ROWS, LANES), F32)
            for h in range(ROWS * here if moves else ROWS):
                line = moving_ref[group, k, h : h + 1, :] if moves else fixed_ref[k - MOVING, h : h + 1, :]
                total = jnp.where((high if moves else high_fixed) == h, lanes(spread(line, ROWS), low), total)
            answer_ref[k, pl.ds(row, ROWS), 0, :] = total
        for s in range(ROWS):
            device = row + ((me + s) & (ROWS - 1))

            @pl.when(device != me)
            def _(device=device):
                answer(device).start()

    each(0, steps, 1, block)
    own_answer = pltpu.make_async_copy(answer_ref.at[:, me], recv_ref.at[:, me], local_sem.at[1])
    own_answer.start()

    own_answer.wait()

    def land(n):
        turn = ((me >> 3) + n) & (steps - 1)
        row = pl.multiple_of(turn * ROWS, ROWS)
        for s in range(ROWS):

            @pl.when(row + s != me)
            def _(s=s):
                arrived(answer_recv, recv_ref.at[:, row + s], row + s)

        for k in range(FIELDS):
            records_ref[k, pl.ds(row, ROWS), :] = recv_ref[k, pl.ds(row, ROWS), 0, :]

    each(0, steps, 1, land)

    def sent(step):
        device = ring.after(step)
        request(device).wait_send()
        answer(device).wait_send()

    return lambda: each(1, devices, 16, sent)


def field_of(ref, row):
    return jnp.concatenate([ref[row : row + 1, h * LANES : (h + 1) * LANES] for h in range(ROWS)], axis=0)


def moving_fields(centres, shape_raw, view):
    rows = [view[0:4], view[4:8]]
    e0, e2, e5 = jnp.exp(shape_raw[0]), jnp.exp(shape_raw[2]), jnp.exp(shape_raw[5])
    screen, factor = [], []
    for m in rows:
        screen.append(m[0] * centres[0] + m[1] * centres[1] + m[2] * centres[2] + m[3])
        factor.append(
            (
                m[0] * e0 + m[1] * shape_raw[1] + m[2] * shape_raw[3],
                m[1] * e2 + m[2] * shape_raw[4],
                m[2] * e5,
            )
        )
    fx, fy = factor
    var_x = fx[0] * fx[0] + fx[1] * fx[1] + fx[2] * fx[2] + 0.3
    cov_xy = fx[0] * fy[0] + fx[1] * fy[1] + fx[2] * fy[2]
    var_y = fy[0] * fy[0] + fy[1] * fy[1] + fy[2] * fy[2] + 0.3
    inverse = 1.0 / (var_x * var_y - cov_xy * cov_xy)
    return screen[0], screen[1], var_y * inverse, -cov_xy * inverse, var_x * inverse


def opacity_of(logit):
    return 0.95 / (1.0 + jnp.exp(-logit))


def camera_view(camera_ref, view):
    return [camera_ref[n // 4, n % 4, view] for n in range(8)]


def give(ring, views, here, got_ref, table_ref, given_ref, moving_ref, fixed_ref, send_sem, recv_sem, local_sem):
    me, devices = ring.me, ring.count
    groups = views // here
    moving_ref[...] = jnp.zeros_like(moving_ref)
    fixed_ref[...] = jnp.zeros_like(fixed_ref)
    wide = ROWS * here
    per_step = 2
    own = pltpu.make_async_copy(table_ref.at[:, me], given_ref.at[:, me], local_sem)
    own.start()

    def copy(device):
        return ring.copy(table_ref.at[:, device], given_ref.at[:, me], send_sem, recv_sem, device)

    each(1, devices, 16, lambda step: copy(ring.after(step)).start())
    own.wait()
    steps = devices // ROWS

    def block(n):
        turn = ((me >> 3) - n) & (steps - 1)
        row = pl.multiple_of(turn * ROWS, ROWS)
        group = turn // (steps // groups)
        for s in range(ROWS):

            @pl.when(row + s != me)
            def _(s=s):
                target = given_ref.at[:, row + s]
                pltpu.make_async_copy(target, target, recv_sem.at[row + s]).wait()

        ids = got_ref[pl.ds(row, ROWS), 0, 0:LANES]
        values = [given_ref[k, pl.ds(row, ROWS), 0, :] for k in range(FIELDS)]
        total = None
        for first in range(0, ROWS, per_step):
            lefts, onehots = [], []
            for src in range(first, first + per_step):
                low, high = ids[src : src + 1] & (LANES - 1), ids[src : src + 1] >> LANE_BITS
                at_wide = iota((wide, LANES), 0) == high
                at_row = iota((ROWS, LANES), 0) == (high & (ROWS - 1))
                rows = [
                    jnp.where(at_wide if k < MOVING else at_row, values[k][src : src + 1], 0.0)
                    for k in range(FIELDS)
                ]
                lefts.append(jnp.concatenate(rows, axis=0))
                onehots.append((iota((LANES, LANES), 0) == low).astype(BF16))
            left_high, left_low = halves(jnp.concatenate(lefts, axis=1))
            right = jnp.concatenate(onehots, axis=1)
            found = dot_nt(left_high, right) + dot_nt(left_low, right)
            total = found if total is None else total + found
        moving_ref[group] += total[: MOVING * wide]
        fixed_ref[...] += total[MOVING * wide :]

    each(0, steps, 1, block)
    each(1, devices, 16, lambda step: copy(ring.after(step)).wait_send())


def pull_kernel(
    views, here, centres_ref, shape_ref, logit_ref, camera_ref, moving_ref, fixed_ref, owners_ref, drawn_ref,
    d_centres_ref, d_shape_ref, d_logit_ref, d_colours_ref, next_ref, image_ref,
):
    wide = ROWS * here
    next_ref[...] = owners_ref[...]
    image_ref[...] = drawn_ref[...]
    centres = [field_of(centres_ref, n) for n in range(3)]
    shape_raw = [field_of(shape_ref, n) for n in range(6)]
    d_centres = [jnp.zeros((ROWS, LANES), F32)] * 3
    d_shape = [jnp.zeros((ROWS, LANES), F32)] * 6
    for view in range(views):
        camera = camera_view(camera_ref, view)
        _, pull = jax.vjp(lambda c, s: moving_fields(c, s, camera), centres, shape_raw)
        base = (view % here) * ROWS
        given = tuple(
            moving_ref[view // here, k * wide + base : k * wide + base + ROWS, :] for k in range(MOVING)
        )
        more_centres, more_shape = pull(given)
        d_centres = [a + b for a, b in zip(d_centres, more_centres)]
        d_shape = [a + b for a, b in zip(d_shape, more_shape)]

    def put(ref, row, value):
        for h in range(ROWS):
            ref[row : row + 1, h * LANES : (h + 1) * LANES] = value[h : h + 1, :]

    for n in range(3):
        put(d_centres_ref, n, d_centres[n])
        put(d_colours_ref, n, fixed_ref[(1 + n) * ROWS : (2 + n) * ROWS, :])
    for n in range(6):
        put(d_shape_ref, n, d_shape[n])
    _, pull = jax.vjp(opacity_of, logit_ref[...])
    d_logit_ref[...] = pull(fixed_ref[0:ROWS, :])[0]


def next_owner(ring, got_ref, live_ref, next_ref):
    here, tiles_here = live_ref.shape
    counts = got_ref[:, 0, LANES:].astype(F32)
    source = iota((ring.count, LANES), 0)
    mine = source >> ring.bits == lax.axis_index("view")
    lower = mine & ((source & (ring.tiles - 1)) < lax.axis_index("tile"))
    own_lane = iota((here, LANES), 0) == iota((here, LANES), 1)

    def column(mask):
        row = jnp.sum(jnp.where(mask, counts, 0.0), axis=0, keepdims=True)
        return jnp.sum(jnp.where(own_lane, spread(row, here), 0.0), axis=1, keepdims=True)

    whole, before = column(mine), column(lower)
    earlier = (iota((tiles_here, tiles_here), 0) < iota((tiles_here, tiles_here), 1)).astype(BF16)
    start = before + dot_nn(live_ref[...].astype(F32).astype(BF16), earlier)
    above, below = (start * ring.tiles).astype(I32), whole.astype(I32)
    quotient = (start * ring.tiles / whole).astype(I32)
    rest = above - quotient * below
    next_ref[...] = quotient + (rest >= below).astype(I32) - (rest < 0).astype(I32)


def render(
    ring, recv_ref, owner_ref, rank_ref, target_ref, image_ref, table_ref,
    cov_ref, odds_ref, high_ref, low_ref, dots_ref, acc_ref,
):
    tiles, _, slots = owner_ref.shape
    devices = ring.count
    blocks = slots // LANES
    half = (SIDE - 1) / 2.0
    log2e = 1.4426950408889634
    before = (iota((slots, slots), 0) < iota((slots, slots), 1)).astype(BF16)
    after = (iota((slots, slots), 0) > iota((slots, slots), 1)).astype(BF16)
    across = iota((SIDE, slots), 0).astype(F32) - half
    sublane = iota((ROWS, LANES), 0)
    split = devices // 2
    peers, places = iota((split, slots), 0), iota((2 * LANES, slots), 0)

    def fetch(t, block):
        here = slice(block * LANES, (block + 1) * LANES)
        owner = spread(owner_ref[t, :, here], ROWS) - sublane
        rank = spread(jnp.maximum(rank_ref[t, :, here], 0), ROWS)
        total = [jnp.zeros((ROWS, LANES), F32)] * FIELDS
        for group in range(devices // ROWS):
            mine = owner == group * ROWS
            for k in range(FIELDS):
                table = recv_ref[k, group * ROWS : (group + 1) * ROWS, :]
                total[k] = jnp.where(mine, lanes(table, rank), total[k])
        return [jnp.sum(one, axis=0, keepdims=True) for one in total]

    def tile(t, lane):
        cov, odds, high_part, low_part, dots = (
            ref.at[lane] for ref in (cov_ref, odds_ref, high_ref, low_ref, dots_ref)
        )
        found = [fetch(t, block) for block in range(blocks)]
        u, w, a, b, c, opacity, red, green, blue = (
            jnp.concatenate([found[block][k] for block in range(blocks)], axis=1) for k in range(FIELDS)
        )
        yield
        aim = jnp.concatenate([target_ref[t], jnp.zeros((ROWS - 3, PIX), F32)], axis=0).T
        dx = across - u
        scale = -0.5 * log2e
        first = (scale * a) * dx * dx
        second = (2.0 * scale * b) * dx
        third = scale * c
        for y in range(SIDE):
            rows = slice(y * SIDE, (y + 1) * SIDE)
            dy = (y - half) - w
            cover = opacity * jnp.exp2((second + third * dy) * dy + first)
            cov[rows, :] = cover
            keep = jnp.log(1.0 - cover)
            odds[rows, :] = cover * jnp.exp(-keep)
            high, low = halves(keep)
            high_part[rows, :] = high
            low_part[rows, :] = low
        yield
        through = jnp.exp(dot_nn(high_part[...], before) + dot_nn(low_part[...], before))
        weights = through * cov[...]
        w_high, w_low = halves(weights)
        yield
        colour = jnp.concatenate([red, green, blue], axis=0)
        colour = jnp.concatenate([colour, jnp.zeros((ROWS - 3, slots), F32)], axis=0)
        c_high, c_low = halves(colour)
        drawn = (dot_nt(w_high, c_high) + dot_nt(w_low, c_high)) + (dot_nt(w_high, c_low) + dot_nt(w_low, c_low))
        column = drawn - aim
        image_ref[t] = drawn.T[0:3]
        yield
        d_colour = [jnp.sum(weights * column[:, n : n + 1], axis=0, keepdims=True) for n in range(3)]
        shade = column[:, 0:1] * red + column[:, 1:2] * green + column[:, 2:3] * blue
        shaded = weights * shade
        s_high, s_low = halves(shaded)
        yield
        behind = dot_nn(s_high, after) + dot_nn(s_low, after)
        dots[...] = shaded - behind * odds[...]
        yield
        sum0 = jnp.zeros((SIDE, slots), F32)
        sum1, sum2 = sum0, sum0
        for y in range(SIDE):
            given = dots[y * SIDE : (y + 1) * SIDE, :]
            dy = (y - half) - w
            once = given * dy
            sum0, sum1, sum2 = sum0 + given, sum1 + once, sum2 + once * dy

        def down(x):
            return jnp.sum(x, axis=0, keepdims=True)

        once = sum0 * dx
        s0, sx, sxx = down(sum0), down(once), down(once * dx)
        sy, sxy, syy = down(sum1), down(sum1 * dx), down(sum2)
        grads = [
            a * sx + b * sy,
            b * sx + c * sy,
            -0.5 * sxx,
            -sxy,
            -0.5 * syy,
            jnp.where(opacity > 0.0, s0 / opacity, 0.0),
            *d_colour,
        ]
        owner, rank = owner_ref[t], rank_ref[t]
        yield
        named = ((owner & (split - 1)) == peers).astype(BF16)
        place = (owner >> (split.bit_length() - 1)) * LANES + rank == places
        parts = [halves(grad) for grad in grads]
        left = [jnp.concatenate([named * part[n] for part in parts], axis=0) for n in range(2)]
        right = place.astype(BF16)
        acc_ref[...] += dot_nt(jnp.concatenate(left, axis=1), jnp.concatenate([right, right], axis=1))

    def together(n, carry):
        running = [tile(n * TOGETHER + lane, lane) for lane in range(TOGETHER)]
        while running:
            running = [one for one in running if next(one, one) is None]
        return carry

    acc_ref[...] = jnp.zeros_like(acc_ref)
    lax.fori_loop(0, tiles // TOGETHER, together, 0)
    for k in range(FIELDS):
        for n in range(2):
            table_ref[k, n * split : (n + 1) * split, 0, :] = acc_ref[
                k * split : (k + 1) * split, n * LANES : (n + 1) * LANES
            ]


def splat_kernel(
    sizes, views, *refs
):
    given, rest = refs[:8], refs[8:]
    held, rest, load_sem = rest[-9:-1], rest[:-9], rest[-1]
    loads = [pltpu.make_async_copy(a, b, load_sem.at[n]) for n, (a, b) in enumerate(zip(given, held))]
    for load in loads:
        load.start()
    splat(sizes, views, loads, *held, *rest)


def splat(
    sizes, views, loads, ids_ref, order_ref, live_ref, centres_ref, shape_ref, logit_ref, colours_ref, target_ref, camera_ref,
    image_ref, moving_ref, fixed_ref, next_ref,
    records_ref, got_ref, owner_ref, rank_ref, value_ref, ask_acc_ref, send_ref, answer_ref, recv_ref,
    own_moving_ref, own_fixed_ref, cov_ref, odds_ref, high_ref, low_ref, dots_ref, acc_ref, table_ref, given_ref, aims_ref, drawn_ref,
    request_send, request_recv, answer_send, answer_recv, give_send, give_recv, local_sem,
):
    ring = Ring(*sizes)
    here, channels, tiles_here, _ = target_ref.shape
    places = [(v, c, t) for v in range(here) for c in range(channels) for t in range(tiles_here)]

    def loaded():
        for load in loads[3:]:
            load.wait()
        for v, c, t in places:
            aims_ref[v * tiles_here + t, c : c + 1, :] = target_ref[v, c, t : t + 1, :]

    for load in loads[:3]:
        load.wait()
    sent = ask(
        ring, views, ids_ref, order_ref, live_ref, centres_ref, shape_ref, logit_ref, colours_ref, camera_ref,
        records_ref, got_ref, owner_ref, rank_ref,
        value_ref, ask_acc_ref, send_ref, answer_ref, recv_ref, own_moving_ref, own_fixed_ref,
        request_send, request_recv, answer_send, answer_recv, local_sem, loaded,
    )
    next_owner(ring, got_ref, live_ref, next_ref)
    render(
        ring, records_ref, owner_ref, rank_ref, aims_ref, drawn_ref, table_ref,
        cov_ref, odds_ref, high_ref, low_ref, dots_ref, acc_ref,
    )
    give(
        ring, views, live_ref.shape[0], got_ref, table_ref, given_ref, moving_ref, fixed_ref,
        give_send, give_recv, local_sem.at[2],
    )
    for v, c, t in places:
        image_ref[v, c, t : t + 1, :] = drawn_ref[v * tiles_here + t, c : c + 1, :]
    sent()


VMEM = pl.BlockSpec(memory_space=pltpu.VMEM)
HBM = pl.BlockSpec(memory_space=pltpu.HBM)
SMEM = pl.BlockSpec(memory_space=pltpu.SMEM)


def params(number=None):
    limit = 60 * 2**20
    if number is None:
        return pltpu.CompilerParams(vmem_limit_bytes=limit)
    return pltpu.CompilerParams(vmem_limit_bytes=limit, collective_id=number, has_side_effects=True)


def shape(dims, kind=F32):
    return jax.ShapeDtypeStruct(dims, kind)


def dma(*dims):
    return pltpu.SemaphoreType.DMA(dims)


def splats(sizes, ids, order, live, centres, shape_raw, logit, colours, camera, target):
    tiles, slots = ids.shape
    devices, views, here = sizes[0] * sizes[1], camera.shape[2], live.shape[0]
    inputs = (ids, order, live, centres, shape_raw, logit, colours, target)
    table = (FIELDS, devices, 1, LANES)
    line = (tiles, 1, slots)
    return pl.pallas_call(
        partial(splat_kernel, sizes, views),
        out_shape=(
            shape(target.shape),
            shape((views // here, MOVING * here * ROWS, LANES)),
            shape(((FIELDS - MOVING) * ROWS, LANES)),
            shape(live.shape, I32),
        ),
        in_specs=[HBM] * 8 + [SMEM],
        out_specs=(VMEM,) * 4,
        scratch_shapes=[
            pltpu.VMEM((FIELDS, devices, LANES), F32),
            pltpu.VMEM((devices, 1, 2 * LANES), I32),
            pltpu.VMEM(line, I32),
            pltpu.VMEM(line, I32),
            pltpu.VMEM(line, I32),
            pltpu.VMEM((2 * devices, LANES), F32),
            pltpu.VMEM((devices, 1, 2 * LANES), I32),
            pltpu.VMEM(table, F32),
            pltpu.VMEM(table, F32),
            pltpu.VMEM((views // here, MOVING, here * ROWS, LANES), F32),
            pltpu.VMEM((FIELDS - MOVING, ROWS, LANES), F32),
            pltpu.VMEM((TOGETHER, PIX, slots), F32),
            pltpu.VMEM((TOGETHER, PIX, slots), F32),
            pltpu.VMEM((TOGETHER, PIX, slots), BF16),
            pltpu.VMEM((TOGETHER, PIX, slots), BF16),
            pltpu.VMEM((TOGETHER, PIX, slots), F32),
            pltpu.VMEM((FIELDS * devices // 2, 2 * LANES), F32),
            pltpu.VMEM(table, F32),
            pltpu.VMEM(table, F32),
            pltpu.VMEM((tiles, 3, PIX), F32),
            pltpu.VMEM((tiles, 3, PIX), F32),
        ]
        + [dma(devices)] * 6
        + [dma(3)]
        + [pltpu.VMEM(one.shape, one.dtype) for one in inputs]
        + [dma(len(inputs))],
        compiler_params=params(0),
        name="splat",
    )(*inputs, camera)


def pull(here, centres, shape_raw, logit, camera, moving, fixed, owners, image):
    return pl.pallas_call(
        partial(pull_kernel, camera.shape[2], here),
        out_shape=(
            shape(centres.shape),
            shape(shape_raw.shape),
            shape(logit.shape),
            shape(centres.shape),
            shape(owners.shape, I32),
            shape(image.shape),
        ),
        in_specs=[VMEM] * 3 + [SMEM] + [VMEM] * 4,
        out_specs=(VMEM,) * 6,
        compiler_params=params(),
        name="pull",
    )(centres, shape_raw, logit, camera, moving, fixed, owners, image)


def shards(centres, shape_raw, opacity_logit, colours, camera, target, intersection_ids, depth_order, live_count):
    sizes = (lax.axis_size("view"), lax.axis_size("tile"))
    here, tiles_here, slots = intersection_ids.shape
    tiles = here * tiles_here
    logit = opacity_logit.reshape(ROWS, LANES)
    image, moving, fixed, owners = splats(
        sizes,
        intersection_ids.reshape(tiles, slots),
        depth_order.reshape(tiles, slots),
        live_count,
        centres,
        shape_raw,
        logit,
        colours,
        camera.transpose(1, 2, 0),
        target.transpose(0, 2, 1, 3),
    )
    d_centres, d_shape, d_logit, d_colours, owners, image = pull(
        here, centres, shape_raw, logit, camera.transpose(1, 2, 0), moving, fixed, owners, image
    )
    return (
        image.transpose(0, 2, 1, 3),
        d_centres,
        d_shape,
        d_logit.reshape(opacity_logit.shape),
        d_colours,
        owners,
    )


def solution(mesh):
    in_specs = (
        P(None, ("view", "tile")),
        P(None, ("view", "tile")),
        P(("view", "tile")),
        P(None, ("view", "tile")),
        P(),
        P("view", "tile", None, None),
        P("view", "tile", None),
        P("view", "tile", None),
        P("view", "tile"),
    )
    out_specs = (
        P("view", "tile", None, None),
        P(None, ("view", "tile")),
        P(None, ("view", "tile")),
        P(("view", "tile")),
        P(None, ("view", "tile")),
        P("view", "tile"),
    )
    return jax.shard_map(shards, mesh=mesh, in_specs=in_specs, out_specs=out_specs, check_vma=False)
```

```python
from functools import partial

import jax
import jax.numpy as jnp
from jax import lax
from jax.experimental import pallas as pl
from jax.experimental.pallas import tpu as pltpu
from jax.sharding import PartitionSpec as P

SIDE = 16
PIX = SIDE * SIDE
LANES = 128
LANE_BITS = 7
ROWS = 8
FIELDS = 9
MOVING = 5
TOGETHER = 8
F32 = jnp.float32
BF16 = jnp.bfloat16
I32 = jnp.int32


def lanes(table, index):
    return jnp.take_along_axis(table, index, axis=1, mode="promise_in_bounds")


def iota(shape, axis):
    return lax.broadcasted_iota(I32, shape, axis)


def spread(row, count):
    return jnp.broadcast_to(row, (count, row.shape[1]))


def halves(array):
    high = array.astype(BF16)
    return high, (array - high.astype(F32)).astype(BF16)


def dot_nn(a, b):
    return lax.dot_general(a, b, (((1,), (0,)), ((), ())), preferred_element_type=F32)


def dot_nt(a, b):
    return lax.dot_general(a, b, (((1,), (1,)), ((), ())), preferred_element_type=F32)


def dot_tn(a, b):
    return lax.dot_general(a, b, (((0,), (0,)), ((), ())), preferred_element_type=F32)


MESH = pl.DeviceIdType.MESH


class Ring:
    def __init__(self, view_group, tile_group):
        self.bits = tile_group.bit_length() - 1
        self.tiles = tile_group
        self.count = view_group * tile_group
        self.me = lax.axis_index("view") * tile_group + lax.axis_index("tile")

    def place(self, device):
        return (device >> self.bits, device & (self.tiles - 1))

    def after(self, step):
        return (self.me + step) & (self.count - 1)

    def greet(self, step):
        pl.semaphore_signal(
            pltpu.get_barrier_semaphore(), inc=1, device_id=self.place(self.after(step)), device_id_type=MESH
        )

    def copy(self, source, target, send_sem, recv_sem, device):
        return pltpu.make_async_remote_copy(
            src_ref=source,
            dst_ref=target,
            send_sem=send_sem.at[device],
            recv_sem=recv_sem.at[self.me],
            device_id=self.place(device),
            device_id_type=MESH,
        )


def each(first, last, unroll, body):
    def step(n, carry):
        body(n)
        return carry

    lax.fori_loop(first, last, step, 0, unroll=unroll)


def ask(
    ring, views, ids_ref, order_ref, live_ref, centres_ref, shape_ref, logit_ref, colours_ref, camera_ref,
    records_ref, got_ref, owner_ref, rank_ref,
    value_ref, acc_ref, send_ref, answer_ref, recv_ref, moving_ref, fixed_ref,
    request_send, request_recv, answer_send, answer_recv, local_sem, loaded,
):
    me, devices = ring.me, ring.count
    tiles, slots = ids_ref.shape
    here, tiles_here = live_ref.shape
    own_count = centres_ref.shape[1]
    own_bits = own_count.bit_length() - 1
    blocks = slots // LANES
    turned = live_ref[...].astype(F32).T
    live = jnp.concatenate([turned[:, n : n + 1] for n in range(here)], axis=0).astype(I32)
    local_view = (iota((tiles, LANES), 0) >= tiles_here).astype(I32)
    for block in range(blocks):
        cut = slice(block * LANES, (block + 1) * LANES)
        order = order_ref[:, cut]
        low, high = order & (LANES - 1), order >> LANE_BITS
        picked = jnp.zeros((tiles, LANES), I32)
        for source in range(blocks):
            found = lanes(ids_ref[:, source * LANES : (source + 1) * LANES], low)
            picked = jnp.where(high == source, found, picked)
        owner = jnp.where(order < live, picked >> own_bits, -1)
        value = (picked & (own_count - 1)) + local_view * own_count
        for t in range(tiles):
            owner_ref[t, :, cut] = owner[t : t + 1, :]
            value_ref[t, :, cut] = value[t : t + 1, :]
    upto = (iota((slots, slots), 0) <= iota((slots, slots), 1)).astype(BF16)
    acc_ref[...] = jnp.zeros_like(acc_ref)
    peers = iota((devices, slots), 0)
    ranks = iota((LANES, slots), 0)

    def tile(t, before):
        owner, value = owner_ref[t], value_ref[t]
        named = peers == owner
        flags = named.astype(BF16)
        count = dot_nn(flags, upto)
        rank = jnp.sum(jnp.where(named, count + before, 0.0), axis=0, keepdims=True) - 1.0
        rank = rank.astype(I32)
        rank_ref[t] = rank
        at_rank = (ranks == rank).astype(BF16)
        parts = [(value & 255).astype(F32), (value >> 8).astype(F32)]
        left = jnp.concatenate([flags * part.astype(BF16) for part in parts], axis=0)
        acc_ref[...] += dot_nt(left, at_rank)
        return before + count[:, slots - 1 :]

    def some(n, before):
        for step in range(greets):
            ring.greet(n * greets + step + 1)
        for t in range(ROWS):
            before = tile(n * ROWS + t, before)
        return before

    rounds = tiles // ROWS
    greets = (devices - 1) // rounds
    for step in range(rounds * greets + 1, devices):
        ring.greet(step)
    lax.fori_loop(0, rounds, some, jnp.zeros((devices, 1), F32))
    low, high = acc_ref[0:devices, :].astype(I32), acc_ref[devices:, :].astype(I32)
    lane = iota((1, LANES), 1)
    told = jnp.zeros((1, LANES), I32)
    for n in range(here):
        total = jnp.sum(live[n * tiles_here : (n + 1) * tiles_here].astype(F32), axis=0, keepdims=True)
        told = jnp.where(lane == n, total.astype(I32), told)
    send_ref[:, 0, 0:LANES] = low + 256 * high
    send_ref[:, 0, LANES:] = spread(told, devices)

    pl.semaphore_wait(pltpu.get_barrier_semaphore(), devices - 1)
    own_request = pltpu.make_async_copy(send_ref.at[me], got_ref.at[me], local_sem.at[0])
    own_request.start()

    def request(device):
        return ring.copy(send_ref.at[device], got_ref.at[me], request_send, request_recv, device)

    each(1, devices, 16, lambda step: request(ring.after(step)).start())

    loaded()
    centres = [field_of(centres_ref, n) for n in range(3)]
    shape_raw = [field_of(shape_ref, n) for n in range(6)]
    for view in range(views):
        found = moving_fields(centres, shape_raw, camera_view(camera_ref, view))
        for k in range(MOVING):
            moving_ref[view // here, k, (view % here) * ROWS : (view % here + 1) * ROWS, :] = found[k]
    fixed_ref[0] = opacity_of(logit_ref[...])
    for n in range(3):
        fixed_ref[1 + n] = field_of(colours_ref, n)
    own_request.wait()
    steps = devices // ROWS
    per_group = steps // (views // here)

    def arrived(semaphores, target, device):
        pltpu.make_async_copy(target, target, semaphores.at[device]).wait()

    def answer(device):
        return ring.copy(answer_ref.at[:, device], recv_ref.at[:, me], answer_send, answer_recv, device)

    def block(n):
        turn = ((me >> 3) - n) & (steps - 1)
        row = pl.multiple_of(turn * ROWS, ROWS)
        group = turn // per_group
        for s in range(ROWS):

            @pl.when(row + s != me)
            def _(s=s):
                arrived(request_recv, got_ref.at[row + s], row + s)

        ids = got_ref[pl.ds(row, ROWS), 0, 0:LANES]
        low, high = ids & (LANES - 1), ids >> LANE_BITS
        high_fixed = high & (ROWS - 1)
        for k in range(FIELDS):
            moves = k < MOVING
            total = jnp.zeros((ROWS, LANES), F32)
            for h in range(ROWS * here if moves else ROWS):
                line = moving_ref[group, k, h : h + 1, :] if moves else fixed_ref[k - MOVING, h : h + 1, :]
                total = jnp.where((high if moves else high_fixed) == h, lanes(spread(line, ROWS), low), total)
            answer_ref[k, pl.ds(row, ROWS), 0, :] = total
        for s in range(ROWS):
            device = row + ((me + s) & (ROWS - 1))

            @pl.when(device != me)
            def _(device=device):
                answer(device).start()

    each(0, steps, 1, block)
    own_answer = pltpu.make_async_copy(answer_ref.at[:, me], recv_ref.at[:, me], local_sem.at[1])
    own_answer.start()

    own_answer.wait()

    def land(n):
        turn = ((me >> 3) + n) & (steps - 1)
        row = pl.multiple_of(turn * ROWS, ROWS)
        for s in range(ROWS):

            @pl.when(row + s != me)
            def _(s=s):
                arrived(answer_recv, recv_ref.at[:, row + s], row + s)

        for k in range(FIELDS):
            records_ref[k, pl.ds(row, ROWS), :] = recv_ref[k, pl.ds(row, ROWS), 0, :]

    each(0, steps, 1, land)

    def sent(step):
        device = ring.after(step)
        request(device).wait_send()
        answer(device).wait_send()

    return lambda: each(1, devices, 16, sent)


def field_of(ref, row):
    return jnp.concatenate([ref[row : row + 1, h * LANES : (h + 1) * LANES] for h in range(ROWS)], axis=0)


def moving_fields(centres, shape_raw, view):
    rows = [view[0:4], view[4:8]]
    e0, e2, e5 = jnp.exp(shape_raw[0]), jnp.exp(shape_raw[2]), jnp.exp(shape_raw[5])
    screen, factor = [], []
    for m in rows:
        screen.append(m[0] * centres[0] + m[1] * centres[1] + m[2] * centres[2] + m[3])
        factor.append(
            (
                m[0] * e0 + m[1] * shape_raw[1] + m[2] * shape_raw[3],
                m[1] * e2 + m[2] * shape_raw[4],
                m[2] * e5,
            )
        )
    fx, fy = factor
    var_x = fx[0] * fx[0] + fx[1] * fx[1] + fx[2] * fx[2] + 0.3
    cov_xy = fx[0] * fy[0] + fx[1] * fy[1] + fx[2] * fy[2]
    var_y = fy[0] * fy[0] + fy[1] * fy[1] + fy[2] * fy[2] + 0.3
    inverse = 1.0 / (var_x * var_y - cov_xy * cov_xy)
    return screen[0], screen[1], var_y * inverse, -cov_xy * inverse, var_x * inverse


def opacity_of(logit):
    return 0.95 / (1.0 + jnp.exp(-logit))


def camera_view(camera_ref, view):
    return [camera_ref[n // 4, n % 4, view] for n in range(8)]


def give(ring, views, here, got_ref, table_ref, given_ref, moving_ref, fixed_ref, send_sem, recv_sem, local_sem):
    me, devices = ring.me, ring.count
    groups = views // here
    moving_ref[...] = jnp.zeros_like(moving_ref)
    fixed_ref[...] = jnp.zeros_like(fixed_ref)
    wide = ROWS * here
    per_step = 2
    own = pltpu.make_async_copy(table_ref.at[:, me], given_ref.at[:, me], local_sem)
    own.start()

    def copy(device):
        return ring.copy(table_ref.at[:, device], given_ref.at[:, me], send_sem, recv_sem, device)

    each(1, devices, 16, lambda step: copy(ring.after(step)).start())
    own.wait()
    steps = devices // ROWS

    def block(n):
        turn = ((me >> 3) - n) & (steps - 1)
        row = pl.multiple_of(turn * ROWS, ROWS)
        group = turn // (steps // groups)
        for s in range(ROWS):

            @pl.when(row + s != me)
            def _(s=s):
                target = given_ref.at[:, row + s]
                pltpu.make_async_copy(target, target, recv_sem.at[row + s]).wait()

        ids = got_ref[pl.ds(row, ROWS), 0, 0:LANES]
        values = [given_ref[k, pl.ds(row, ROWS), 0, :] for k in range(FIELDS)]
        total = None
        for first in range(0, ROWS, per_step):
            lefts, onehots = [], []
            for src in range(first, first + per_step):
                low, high = ids[src : src + 1] & (LANES - 1), ids[src : src + 1] >> LANE_BITS
                at_wide = iota((wide, LANES), 0) == high
                at_row = iota((ROWS, LANES), 0) == (high & (ROWS - 1))
                rows = [
                    jnp.where(at_wide if k < MOVING else at_row, values[k][src : src + 1], 0.0)
                    for k in range(FIELDS)
                ]
                lefts.append(jnp.concatenate(rows, axis=0))
                onehots.append((iota((LANES, LANES), 0) == low).astype(BF16))
            left_high, left_low = halves(jnp.concatenate(lefts, axis=1))
            right = jnp.concatenate(onehots, axis=1)
            found = dot_nt(left_high, right) + dot_nt(left_low, right)
            total = found if total is None else total + found
        moving_ref[group] += total[: MOVING * wide]
        fixed_ref[...] += total[MOVING * wide :]

    each(0, steps, 1, block)
    each(1, devices, 16, lambda step: copy(ring.after(step)).wait_send())


def pull_kernel(
    views, here, centres_ref, shape_ref, logit_ref, camera_ref, moving_ref, fixed_ref, owners_ref, drawn_ref,
    d_centres_ref, d_shape_ref, d_logit_ref, d_colours_ref, next_ref, image_ref,
):
    wide = ROWS * here
    next_ref[...] = owners_ref[...]
    image_ref[...] = drawn_ref[...]
    centres = [field_of(centres_ref, n) for n in range(3)]
    shape_raw = [field_of(shape_ref, n) for n in range(6)]
    d_centres = [jnp.zeros((ROWS, LANES), F32)] * 3
    d_shape = [jnp.zeros((ROWS, LANES), F32)] * 6
    for view in range(views):
        camera = camera_view(camera_ref, view)
        _, pull = jax.vjp(lambda c, s: moving_fields(c, s, camera), centres, shape_raw)
        base = (view % here) * ROWS
        given = tuple(
            moving_ref[view // here, k * wide + base : k * wide + base + ROWS, :] for k in range(MOVING)
        )
        more_centres, more_shape = pull(given)
        d_centres = [a + b for a, b in zip(d_centres, more_centres)]
        d_shape = [a + b for a, b in zip(d_shape, more_shape)]

    def put(ref, row, value):
        for h in range(ROWS):
            ref[row : row + 1, h * LANES : (h + 1) * LANES] = value[h : h + 1, :]

    for n in range(3):
        put(d_centres_ref, n, d_centres[n])
        put(d_colours_ref, n, fixed_ref[(1 + n) * ROWS : (2 + n) * ROWS, :])
    for n in range(6):
        put(d_shape_ref, n, d_shape[n])
    _, pull = jax.vjp(opacity_of, logit_ref[...])
    d_logit_ref[...] = pull(fixed_ref[0:ROWS, :])[0]


def next_owner(ring, got_ref, live_ref, next_ref):
    here, tiles_here = live_ref.shape
    counts = got_ref[:, 0, LANES:].astype(F32)
    source = iota((ring.count, LANES), 0)
    mine = source >> ring.bits == lax.axis_index("view")
    lower = mine & ((source & (ring.tiles - 1)) < lax.axis_index("tile"))
    own_lane = iota((here, LANES), 0) == iota((here, LANES), 1)

    def column(mask):
        row = jnp.sum(jnp.where(mask, counts, 0.0), axis=0, keepdims=True)
        return jnp.sum(jnp.where(own_lane, spread(row, here), 0.0), axis=1, keepdims=True)

    whole, before = column(mine), column(lower)
    earlier = (iota((tiles_here, tiles_here), 0) < iota((tiles_here, tiles_here), 1)).astype(BF16)
    start = before + dot_nn(live_ref[...].astype(F32).astype(BF16), earlier)
    above, below = (start * ring.tiles).astype(I32), whole.astype(I32)
    quotient = (start * ring.tiles / whole).astype(I32)
    rest = above - quotient * below
    next_ref[...] = quotient + (rest >= below).astype(I32) - (rest < 0).astype(I32)


def render(
    ring, recv_ref, owner_ref, rank_ref, target_ref, image_ref, table_ref,
    cov_ref, odds_ref, high_ref, low_ref, dots_ref, acc_ref,
):
    tiles, _, slots = owner_ref.shape
    devices = ring.count
    blocks = slots // LANES
    half = (SIDE - 1) / 2.0
    log2e = 1.4426950408889634
    before = (iota((slots, slots), 0) < iota((slots, slots), 1)).astype(BF16)
    after = (iota((slots, slots), 0) > iota((slots, slots), 1)).astype(BF16)
    across = iota((SIDE, slots), 0).astype(F32) - half
    sublane = iota((ROWS, LANES), 0)
    split = devices // 2
    peers, places = iota((split, slots), 0), iota((2 * LANES, slots), 0)

    def fetch(t, block):
        here = slice(block * LANES, (block + 1) * LANES)
        owner = spread(owner_ref[t, :, here], ROWS) - sublane
        rank = spread(jnp.maximum(rank_ref[t, :, here], 0), ROWS)
        total = [jnp.zeros((ROWS, LANES), F32)] * FIELDS
        for group in range(devices // ROWS):
            mine = owner == group * ROWS
            for k in range(FIELDS):
                table = recv_ref[k, group * ROWS : (group + 1) * ROWS, :]
                total[k] = jnp.where(mine, lanes(table, rank), total[k])
        return [jnp.sum(one, axis=0, keepdims=True) for one in total]

    def tile(t, lane):
        cov, odds, high_part, low_part, dots = (
            ref.at[lane] for ref in (cov_ref, odds_ref, high_ref, low_ref, dots_ref)
        )
        found = [fetch(t, block) for block in range(blocks)]
        u, w, a, b, c, opacity, red, green, blue = (
            jnp.concatenate([found[block][k] for block in range(blocks)], axis=1) for k in range(FIELDS)
        )
        yield
        aim = jnp.concatenate([target_ref[t], jnp.zeros((ROWS - 3, PIX), F32)], axis=0).T
        dx = across - u
        scale = -0.5 * log2e
        first = (scale * a) * dx * dx
        second = (2.0 * scale * b) * dx
        third = scale * c
        for y in range(SIDE):
            rows = slice(y * SIDE, (y + 1) * SIDE)
            dy = (y - half) - w
            cover = opacity * jnp.exp2((second + third * dy) * dy + first)
            cov[rows, :] = cover
            keep = jnp.log(1.0 - cover)
            odds[rows, :] = cover * jnp.exp(-keep)
            high, low = halves(keep)
            high_part[rows, :] = high
            low_part[rows, :] = low
        yield
        through = jnp.exp(dot_nn(high_part[...], before) + dot_nn(low_part[...], before))
        weights = through * cov[...]
        w_high, w_low = halves(weights)
        yield
        colour = jnp.concatenate([red, green, blue], axis=0)
        colour = jnp.concatenate([colour, jnp.zeros((ROWS - 3, slots), F32)], axis=0)
        c_high, c_low = halves(colour)
        drawn = (dot_nt(w_high, c_high) + dot_nt(w_low, c_high)) + (dot_nt(w_high, c_low) + dot_nt(w_low, c_low))
        column = drawn - aim
        image_ref[t] = drawn.T[0:3]
        yield
        d_colour = [jnp.sum(weights * column[:, n : n + 1], axis=0, keepdims=True) for n in range(3)]
        shade = column[:, 0:1] * red + column[:, 1:2] * green + column[:, 2:3] * blue
        shaded = weights * shade
        s_high, s_low = halves(shaded)
        yield
        behind = dot_nn(s_high, after) + dot_nn(s_low, after)
        dots[...] = shaded - behind * odds[...]
        yield
        sum0 = jnp.zeros((SIDE, slots), F32)
        sum1, sum2 = sum0, sum0
        for y in range(SIDE):
            given = dots[y * SIDE : (y + 1) * SIDE, :]
            dy = (y - half) - w
            once = given * dy
            sum0, sum1, sum2 = sum0 + given, sum1 + once, sum2 + once * dy

        def down(x):
            return jnp.sum(x, axis=0, keepdims=True)

        once = sum0 * dx
        s0, sx, sxx = down(sum0), down(once), down(once * dx)
        sy, sxy, syy = down(sum1), down(sum1 * dx), down(sum2)
        grads = [
            a * sx + b * sy,
            b * sx + c * sy,
            -0.5 * sxx,
            -sxy,
            -0.5 * syy,
            jnp.where(opacity > 0.0, s0 / opacity, 0.0),
            *d_colour,
        ]
        owner, rank = owner_ref[t], rank_ref[t]
        yield
        named = ((owner & (split - 1)) == peers).astype(BF16)
        place = (owner >> (split.bit_length() - 1)) * LANES + rank == places
        parts = [halves(grad) for grad in grads]
        left = [jnp.concatenate([named * part[n] for part in parts], axis=0) for n in range(2)]
        right = place.astype(BF16)
        acc_ref[...] += dot_nt(jnp.concatenate(left, axis=1), jnp.concatenate([right, right], axis=1))

    def together(n, carry):
        running = [tile(n * TOGETHER + lane, lane) for lane in range(TOGETHER)]
        while running:
            running = [one for one in running if next(one, one) is None]
        return carry

    acc_ref[...] = jnp.zeros_like(acc_ref)
    lax.fori_loop(0, tiles // TOGETHER, together, 0)
    for k in range(FIELDS):
        for n in range(2):
            table_ref[k, n * split : (n + 1) * split, 0, :] = acc_ref[
                k * split : (k + 1) * split, n * LANES : (n + 1) * LANES
            ]


def splat_kernel(
    sizes, views, *refs
):
    given, rest = refs[:8], refs[8:]
    held, rest, load_sem = rest[-9:-1], rest[:-9], rest[-1]
    loads = [pltpu.make_async_copy(a, b, load_sem.at[n]) for n, (a, b) in enumerate(zip(given, held))]
    for load in loads:
        load.start()
    splat(sizes, views, loads, *held, *rest)


def splat(
    sizes, views, loads, ids_ref, order_ref, live_ref, centres_ref, shape_ref, logit_ref, colours_ref, target_ref, camera_ref,
    image_ref, moving_ref, fixed_ref, next_ref,
    records_ref, got_ref, owner_ref, rank_ref, value_ref, ask_acc_ref, send_ref, answer_ref, recv_ref,
    own_moving_ref, own_fixed_ref, cov_ref, odds_ref, high_ref, low_ref, dots_ref, acc_ref, table_ref, given_ref, aims_ref, drawn_ref,
    request_send, request_recv, answer_send, answer_recv, give_send, give_recv, local_sem,
):
    ring = Ring(*sizes)
    here, channels, tiles_here, _ = target_ref.shape
    places = [(v, c, t) for v in range(here) for c in range(channels) for t in range(tiles_here)]

    def loaded():
        for load in loads[3:]:
            load.wait()
        for v, c, t in places:
            aims_ref[v * tiles_here + t, c : c + 1, :] = target_ref[v, c, t : t + 1, :]

    for load in loads[:3]:
        load.wait()
    sent = ask(
        ring, views, ids_ref, order_ref, live_ref, centres_ref, shape_ref, logit_ref, colours_ref, camera_ref,
        records_ref, got_ref, owner_ref, rank_ref,
        value_ref, ask_acc_ref, send_ref, answer_ref, recv_ref, own_moving_ref, own_fixed_ref,
        request_send, request_recv, answer_send, answer_recv, local_sem, loaded,
    )
    next_owner(ring, got_ref, live_ref, next_ref)
    render(
        ring, records_ref, owner_ref, rank_ref, aims_ref, drawn_ref, table_ref,
        cov_ref, odds_ref, high_ref, low_ref, dots_ref, acc_ref,
    )
    give(
        ring, views, live_ref.shape[0], got_ref, table_ref, given_ref, moving_ref, fixed_ref,
        give_send, give_recv, local_sem.at[2],
    )
    for v, c, t in places:
        image_ref[v, c, t : t + 1, :] = drawn_ref[v * tiles_here + t, c : c + 1, :]
    sent()


VMEM = pl.BlockSpec(memory_space=pltpu.VMEM)
HBM = pl.BlockSpec(memory_space=pltpu.HBM)
SMEM = pl.BlockSpec(memory_space=pltpu.SMEM)


def params(number=None):
    limit = 60 * 2**20
    if number is None:
        return pltpu.CompilerParams(vmem_limit_bytes=limit)
    return pltpu.CompilerParams(vmem_limit_bytes=limit, collective_id=number, has_side_effects=True)


def shape(dims, kind=F32):
    return jax.ShapeDtypeStruct(dims, kind)


def dma(*dims):
    return pltpu.SemaphoreType.DMA(dims)


def splats(sizes, ids, order, live, centres, shape_raw, logit, colours, camera, target):
    tiles, slots = ids.shape
    devices, views, here = sizes[0] * sizes[1], camera.shape[2], live.shape[0]
    inputs = (ids, order, live, centres, shape_raw, logit, colours, target)
    table = (FIELDS, devices, 1, LANES)
    line = (tiles, 1, slots)
    return pl.pallas_call(
        partial(splat_kernel, sizes, views),
        out_shape=(
            shape(target.shape),
            shape((views // here, MOVING * here * ROWS, LANES)),
            shape(((FIELDS - MOVING) * ROWS, LANES)),
            shape(live.shape, I32),
        ),
        in_specs=[HBM] * 8 + [SMEM],
        out_specs=(VMEM,) * 4,
        scratch_shapes=[
            pltpu.VMEM((FIELDS, devices, LANES), F32),
            pltpu.VMEM((devices, 1, 2 * LANES), I32),
            pltpu.VMEM(line, I32),
            pltpu.VMEM(line, I32),
            pltpu.VMEM(line, I32),
            pltpu.VMEM((2 * devices, LANES), F32),
            pltpu.VMEM((devices, 1, 2 * LANES), I32),
            pltpu.VMEM(table, F32),
            pltpu.VMEM(table, F32),
            pltpu.VMEM((views // here, MOVING, here * ROWS, LANES), F32),
            pltpu.VMEM((FIELDS - MOVING, ROWS, LANES), F32),
            pltpu.VMEM((TOGETHER, PIX, slots), F32),
            pltpu.VMEM((TOGETHER, PIX, slots), F32),
            pltpu.VMEM((TOGETHER, PIX, slots), BF16),
            pltpu.VMEM((TOGETHER, PIX, slots), BF16),
            pltpu.VMEM((TOGETHER, PIX, slots), F32),
            pltpu.VMEM((FIELDS * devices // 2, 2 * LANES), F32),
            pltpu.VMEM(table, F32),
            pltpu.VMEM(table, F32),
            pltpu.VMEM((tiles, 3, PIX), F32),
            pltpu.VMEM((tiles, 3, PIX), F32),
        ]
        + [dma(devices)] * 6
        + [dma(3)]
        + [pltpu.VMEM(one.shape, one.dtype) for one in inputs]
        + [dma(len(inputs))],
        compiler_params=params(0),
        name="splat",
    )(*inputs, camera)


def pull(here, centres, shape_raw, logit, camera, moving, fixed, owners, image):
    return pl.pallas_call(
        partial(pull_kernel, camera.shape[2], here),
        out_shape=(
            shape(centres.shape),
            shape(shape_raw.shape),
            shape(logit.shape),
            shape(centres.shape),
            shape(owners.shape, I32),
            shape(image.shape),
        ),
        in_specs=[VMEM] * 3 + [SMEM] + [VMEM] * 4,
        out_specs=(VMEM,) * 6,
        compiler_params=params(),
        name="pull",
    )(centres, shape_raw, logit, camera, moving, fixed, owners, image)


def shards(centres, shape_raw, opacity_logit, colours, camera, target, intersection_ids, depth_order, live_count):
    sizes = (lax.axis_size("view"), lax.axis_size("tile"))
    here, tiles_here, slots = intersection_ids.shape
    tiles = here * tiles_here
    logit = opacity_logit.reshape(ROWS, LANES)
    image, moving, fixed, owners = splats(
        sizes,
        intersection_ids.reshape(tiles, slots),
        depth_order.reshape(tiles, slots),
        live_count,
        centres,
        shape_raw,
        logit,
        colours,
        camera.transpose(1, 2, 0),
        target.transpose(0, 2, 1, 3),
    )
    d_centres, d_shape, d_logit, d_colours, owners, image = pull(
        here, centres, shape_raw, logit, camera.transpose(1, 2, 0), moving, fixed, owners, image
    )
    return (
        image.transpose(0, 2, 1, 3),
        d_centres,
        d_shape,
        d_logit.reshape(opacity_logit.shape),
        d_colours,
        owners,
    )


def solution(mesh):
    in_specs = (
        P(None, ("view", "tile")),
        P(None, ("view", "tile")),
        P(("view", "tile")),
        P(None, ("view", "tile")),
        P(),
        P("view", "tile", None, None),
        P("view", "tile", None),
        P("view", "tile", None),
        P("view", "tile"),
    )
    out_specs = (
        P("view", "tile", None, None),
        P(None, ("view", "tile")),
        P(None, ("view", "tile")),
        P(("view", "tile")),
        P(None, ("view", "tile")),
        P("view", "tile"),
    )
    return jax.shard_map(shards, mesh=mesh, in_specs=in_specs, out_specs=out_specs, check_vma=False)
```
